32 devices in a mesh: dp: 8 (over z, y), pass: 2 (over x), vocab: 2 (over core).
Axes of the slice: x: 2, y: 2, z: 4, core: 2. Of those that a mesh axis runs over, the one named last changes fastest.
Arguments:
- inputs: bfloat16 [4096, 512], P('dp'), may hold values from -6 to 6
- memory: bfloat16 [8192, 512], P('dp'), may hold values from -6 to 6
- expert_ids: int32 [2, 4096, 1], P('pass', 'dp'), may hold values from 0 to 3; in each aligned block of 512 rows (0 to 511, 512 to 1023, ..., all dimensions but the last counted through in order) at most 256 rows name the same one
- targets: int32 [4096], P('dp'), may hold values from 0 to 31999
- lengths: int32 [8], replicated, may hold values from 128 to 512, as said below
- memory_mask: int32 [8, 1024], P('dp'), may hold values from 0 to 1, as said below
- norm_gain: bfloat16 [4, 512], P(None, ('dp', 'pass')), may hold values from 0.5 to 1.5
- norm_bias: bfloat16 [4, 512], P(None, ('dp', 'pass')), may hold values from -3 to 3
- self_project: bfloat16 [512, 1536], P(None, ('dp', 'pass')), may hold values from -0.25 to 0.25
- self_output: bfloat16 [512, 512], P(None, ('dp', 'pass')), may hold values from -1 to 1
- cross_query: bfloat16 [512, 512], P(None, ('dp', 'pass')), may hold values from -0.25 to 0.25
- memory_project: bfloat16 [512, 1024], P(None, ('dp', 'pass')), may hold values from -0.25 to 0.25
- cross_output: bfloat16 [512, 512], P(None, ('dp', 'pass')), may hold values from -1 to 1
- expert_in: bfloat16 [4, 512, 2048], P(None, None, ('dp', 'pass')), may hold values from -0.25 to 0.25
- expert_out: bfloat16 [4, 512, 2048], P(None, None, ('dp', 'pass')), may hold values from -0.125 to 0.125
- embedding: bfloat16 [32000, 512], P(('dp', 'pass', 'vocab')), may hold values from -0.5 to 0.5
Outputs:
- block_out: float32 [2, 4096, 512], P('pass', 'dp')
- mean_loss: float32 [], replicated
- inputs_gradient: float32 [4096, 512], P('dp')
- memory_gradient: float32 [8192, 512], P('dp')
- norm_gain_gradient: float32 [4, 512], P(None, ('dp', 'pass'))
- norm_bias_gradient: float32 [4, 512], P(None, ('dp', 'pass'))
- self_project_gradient: float32 [512, 1536], P(None, ('dp', 'pass'))
- self_output_gradient: float32 [512, 512], P(None, ('dp', 'pass'))
- cross_query_gradient: float32 [512, 512], P(None, ('dp', 'pass'))
- memory_project_gradient: float32 [512, 1024], P(None, ('dp', 'pass'))
- cross_output_gradient: float32 [512, 512], P(None, ('dp', 'pass'))
- expert_in_gradient: float32 [4, 512, 2048], P(None, None, ('dp', 'pass'))
- expert_out_gradient: float32 [4, 512, 2048], P(None, None, ('dp', 'pass'))
- embedding_gradient: float32 [32000, 512], P(('dp', 'pass', 'vocab'))
The draws below stay inside these ranges and needn't reach their ends.
Inputs may be any that keep to these rules, and one draw needn't show every extreme that they name: `expert_ids`: in each pass no expert is named by more than 256 tokens of one row, and some row reaches 256. `lengths`: some row has all 512 slots valid. `memory_mask`: the first memory position of every row is 1.
All inputs are finite; a program needn't handle non-finite values.
Results may differ from the reference program's by a relative error of at most 0.017.
Values may be sent and summed in bfloat16 or wider, within the bound.
No kernel may reach another device: no remote copies, remote signals or barrier semaphores. Data moves between devices by JAX's collectives and lax.ppermute only.
A program may use at most 192 MiB of HBM per device.

```python
import math
import jax
import jax.numpy as jnp
import numpy as np
from jax import lax

D = 512
HEADS = 8
HEAD = 64
FF = 2048
VOCAB = 32000
EXPERTS = 4
SEQ = 512
MEM = 1024
CAP = 256
ROWS = 8
TOKENS = 4096
MEMTOK = 8192


def draw_lengths(key, part):
    key = jax.random.fold_in(key, 11)
    first_key, second_key = jax.random.split(key)
    drawn = jax.random.randint(first_key, (ROWS,), SEQ // 4, SEQ + 1)
    chosen = jax.random.randint(second_key, (), 0, ROWS)
    return jnp.where(jnp.arange(ROWS) == chosen, SEQ, drawn).astype(jnp.int32)


def draw_memory_mask(key, part):
    key = jax.random.fold_in(key, 23)
    levels = jax.random.randint(key, (ROWS, MEM), 0, 4)
    opened = jnp.where(levels > 0, 1, 0)
    return jnp.where(jnp.arange(MEM)[None, :] == 0, 1, opened).astype(jnp.int32)


def touch_ends(entries, rng, low, top_value):
    longest = entries.shape.index(max(entries.shape))
    spots = []
    for shift in (0, 1):
        where = [jax.random.randint(jax.random.fold_in(rng, axis), (), 0, length) for axis, length in enumerate(entries.shape)]
        where[longest] = (where[longest] + shift) % entries.shape[longest]
        spots.append(tuple(where))
    return entries.at[spots[0]].set(low).at[spots[1]].set(top_value)


def block_scale(rng, shape, pieces, low, high):
    level, own = 1.0, jax.random.fold_in(rng, 6)
    for position, blocks in pieces:
        draws = jnp.exp(jax.random.uniform(jax.random.fold_in(own, position), (blocks,), jnp.float32, low / len(pieces), high / len(pieces)))
        level = level * jnp.repeat(draws, shape[position] // blocks).reshape([-1 if axis == position else 1 for axis in range(len(shape))])
    return level


def rank_table(count, skew):
    portions = [(1 << 20) // math.isqrt(standing ** skew) + 1 for standing in range(1, count + 1)]
    scale = 1 + sum(portions) // (1 << 30)
    return np.cumsum(np.array([max(1, weight // scale) for weight in portions]))


def ranked(key, extent, count, skew):
    listing = rank_table(count, skew)
    lot = jax.random.randint(jax.random.fold_in(key, 1), extent, 0, int(listing[count - 1]))
    grade = jnp.searchsorted(jnp.asarray(listing, jnp.int32), lot, side="right")
    return jax.random.permutation(jax.random.fold_in(key, 2), count)[grade].astype(jnp.int32)


def shared_out(rng, own, number, rows, count, top, limit, slope):
    sequence = jax.random.permutation(rng, count)
    crowded, common = shares(count, rows * top, limit, slope, True), shares(count, rows * top, limit, slope, False)
    places = jnp.arange(count)

    def named(tallies, offset_by):
        used = int((tallies > 0).sum())
        fixed = max(1, used // 4)
        passed = fixed + (places - fixed + offset_by * (used - fixed)) % max(1, count - fixed)
        return jnp.zeros((count,), jnp.int32).at[sequence[jnp.where(places < fixed, places, passed)]].set(jnp.asarray(tallies, jnp.int32))

    tallies = jnp.where(number % 4 == 0, named(crowded, number // 4), named(common, number - number // 4 - 1))
    mixed = jax.random.permutation(jax.random.fold_in(own, 3), count)
    giver, receiver = mixed[0:count // 2 * 2:2], mixed[1:count // 2 * 2:2]
    room = jnp.minimum(tallies[giver] - 1, limit - tallies[receiver]) // 2
    room = jnp.where((giver == sequence[0]) | (receiver == sequence[0]) | (tallies[receiver] == 0), 0, jnp.maximum(room, 0))
    passed = jax.random.randint(jax.random.fold_in(own, 4), (count // 2,), 0, 1 << 20) % (room + 1)
    tallies = tallies.at[giver].add(-passed).at[receiver].add(passed)
    items = jnp.searchsorted(jnp.cumsum(tallies), jnp.arange(rows * top), side="right").astype(jnp.int32)
    table = items.reshape(top, rows).T
    table = table[jax.random.permutation(jax.random.fold_in(own, 1), rows)]
    offset_by = jax.random.randint(jax.random.fold_in(own, 2), (rows, 1), 0, top)
    return jnp.take_along_axis(table, (jnp.arange(top)[None, :] + offset_by) % top, axis=1)


def shares(number_of, total, limit, skew, full):
    weights = [(1 << 20) // math.isqrt(rank ** skew) + 1 for rank in range(1, number_of + 1)]
    largest = limit if full else min(limit, max(-(-total // number_of), total * weights[0] // sum(weights)))
    least = 1 if total - largest >= number_of - 1 else 0
    holding, spare = [largest] + [least] * (number_of - 1), total - largest - least * (number_of - 1)
    while spare > 0:
        movable = [i for i in range(1, number_of) if holding[i] < largest] or [i for i in range(1, number_of) if holding[i] < limit]
        whole, remaining = sum([weights[i] for i in movable]), spare
        for i in movable:
            addition = min(limit - holding[i], max(1, remaining * weights[i] // whole), spare)
            holding[i] = holding[i] + addition
            spare = spare - addition
    return np.array(holding)


def scatter_about(rng, dims, deviation, bound, cuts=(), kind=jnp.bfloat16):
    factor_of = block_scale(rng, dims, cuts, -0.22, 0.18) if cuts else 1.0
    values = jax.random.normal(rng, dims, jnp.float32) * deviation * factor_of
    return jnp.minimum(jnp.maximum(values, -bound), bound).astype(kind)


def setup_inputs(seed: int = 0) -> dict:
    seeds = jax.random.split(jax.random.key(seed), 17)
    inputs = scatter_about(seeds[0], (TOKENS, D), 1.0, 6.0, ((0, 8),))
    memory = scatter_about(seeds[1], (MEMTOK, D), 1.0, 6.0, ((0, 8),))
    expert_ids_keys = jax.random.split(jax.random.fold_in(seeds[2], 1), 2 * TOKENS // SEQ)
    expert_ids_turns = jax.random.permutation(jax.random.fold_in(seeds[2], 3), 2 * TOKENS // SEQ)
    expert_ids = jax.vmap(lambda own, number: shared_out(jax.random.fold_in(seeds[2], 2), own, number, SEQ, EXPERTS, 1, CAP, 2))(expert_ids_keys, expert_ids_turns).reshape((2, TOKENS, 1))
    targets = touch_ends(ranked(seeds[3], (TOKENS,), VOCAB, 2), jax.random.fold_in(seeds[3], 3), 0, VOCAB - 1).astype(jnp.int32)
    lengths = draw_lengths(jax.random.fold_in(seeds[16], 71), 0)
    memory_mask = draw_memory_mask(jax.random.fold_in(seeds[16], 71), 0)
    norm_gain = jnp.clip(1.0 + 0.1 * jax.random.normal(seeds[6], (4, D), jnp.float32), 0.5, 1.5).astype(jnp.bfloat16)
    norm_bias = scatter_about(seeds[7], (4, D), 0.2, 3.0, ((1, 16),))
    self_project = scatter_about(seeds[8], (D, 3 * D), D ** -0.5, 0.25, ((1, 16),))
    self_output = scatter_about(seeds[9], (D, D), (D // 16) ** -0.5, 1.0, ((1, 16),))
    cross_query = scatter_about(seeds[10], (D, D), D ** -0.5, 0.25, ((1, 16),))
    memory_project = scatter_about(seeds[11], (D, 2 * D), D ** -0.5, 0.25, ((1, 16),))
    cross_output = scatter_about(seeds[12], (D, D), (D // 16) ** -0.5, 1.0, ((1, 16),))
    expert_in = scatter_about(seeds[13], (EXPERTS, D, FF), D ** -0.5, 0.25, ((2, 16),))
    expert_out = scatter_about(seeds[14], (EXPERTS, D, FF), FF ** -0.5, 0.125, ((2, 16),))
    embedding = scatter_about(seeds[15], (VOCAB, D), (D // 4) ** -0.5, 0.5, ((0, 32),))
    return dict(inputs=inputs, memory=memory, expert_ids=expert_ids, targets=targets, lengths=lengths, memory_mask=memory_mask, norm_gain=norm_gain, norm_bias=norm_bias, self_project=self_project, self_output=self_output, cross_query=cross_query, memory_project=memory_project, cross_output=cross_output, expert_in=expert_in, expert_out=expert_out, embedding=embedding)


@jax.custom_vjp
def low(v):
    return lax.optimization_barrier(v.astype(jnp.bfloat16)).astype(jnp.float32)

@jax.custom_vjp
def low_back(v):
    return v

def low_keep(v):
    return (low(v), None)

def low_pass(kept, grad):
    return (grad,)

def back_keep(v):
    return (v, None)

def back_low(kept, grad):
    return (low(grad),)
low.defvjp(low_keep, low_pass)
low_back.defvjp(back_keep, back_low)
epsilon = 1e-05
smoothing = 0.1
consistency = 1.0
highest = lax.Precision.HIGHEST

def product(left, right):
    return jnp.dot(left, right, precision=highest, preferred_element_type=jnp.float32)

def normalize(values, norm_gain, norm_bias):
    average = lax.optimization_barrier(jnp.mean(values, axis=-1, keepdims=True))
    centered = values - average
    variance = lax.optimization_barrier(jnp.mean(centered * centered, axis=-1, keepdims=True))
    return centered * lax.rsqrt(variance + epsilon) * norm_gain + norm_bias

def attention(queries, keys, values, allowed):
    length = queries.shape[0]
    query_heads = queries.reshape(length, HEADS, HEAD)
    key_heads = keys.reshape(keys.shape[0], HEADS, HEAD)
    value_heads = values.reshape(values.shape[0], HEADS, HEAD)
    scores = jnp.einsum('qhd,khd->hqk', query_heads, key_heads, precision=highest) * HEAD ** (-0.5)
    scores = low_back(scores)
    scores = jnp.where(allowed[None], scores, -1e+30)
    weights = low(jax.nn.softmax(scores, axis=-1))
    mixed = jnp.einsum('hqk,khd->qhd', weights, value_heads, precision=highest)
    return low(low_back(mixed.reshape(length, HEADS * HEAD)))

def smoothed(log_prob, target_row):
    picked = jnp.take_along_axis(log_prob, target_row[:, None], axis=1)[:, 0]
    return -(1.0 - smoothing) * picked - smoothing / VOCAB * lax.optimization_barrier(jnp.sum(log_prob, axis=-1))

def layer_row(row, params):
    tokens, memory, routes, target_row, length_row, mask_row = row
    norm_gain, norm_bias, self_project, self_output, cross_query, memory_project, cross_output, expert_in, expert_out, embedding = params
    positions = jnp.arange(SEQ)
    causal = positions[None, :] <= positions[:, None]
    visible = jnp.broadcast_to(mask_row[None, :] == 1, (SEQ, MEM))
    normed = low(normalize(tokens, norm_gain[0], norm_bias[0]))
    projected = low(low_back(product(normed, self_project)))
    attended = attention(projected[:, :D], projected[:, D:2 * D], projected[:, 2 * D:], causal)
    hidden_one = tokens + low_back(product(attended, self_output))
    normed = low(normalize(hidden_one, norm_gain[1], norm_bias[1]))
    query_cross = low(low_back(product(normed, cross_query)))
    keyval = low(low_back(product(memory, memory_project)))
    attended = attention(query_cross, keyval[:, :D], keyval[:, D:], visible)
    hidden_two = hidden_one + low_back(product(attended, cross_output))
    normed = low(normalize(hidden_two, norm_gain[2], norm_bias[2]))
    valid_mask = (positions < length_row).astype(jnp.float32)
    outputs = []
    log_probs = []
    for pass_index in range(2):
        expert_sum = jnp.zeros((SEQ, D), jnp.float32)
        for expert in range(EXPERTS):
            pre_act = low_back(product(normed, expert_in[expert]))
            activation = low(jax.nn.gelu(pre_act))
            result = product(activation, expert_out[expert].T)
            expert_sum = expert_sum + jnp.where((routes[pass_index] == expert)[:, None], result, 0.0)
        block_out = hidden_two + low_back(expert_sum)
        final_normed = low(normalize(block_out, norm_gain[3], norm_bias[3]))
        logits = low_back(product(final_normed, embedding.T))
        outputs.append(block_out)
        log_probs.append(jax.nn.log_softmax(logits, axis=-1))
    first_pass, second_pass = log_probs
    symmetric = lax.optimization_barrier(jnp.sum((jnp.exp(first_pass) - jnp.exp(second_pass)) * (first_pass - second_pass), axis=-1))
    per_token = 0.5 * (smoothed(first_pass, target_row) + smoothed(second_pass, target_row) + consistency * symmetric)
    return (jnp.stack(outputs), jnp.sum(valid_mask * per_token))

def reference(inputs, memory, expert_ids, targets, lengths, memory_mask, norm_gain, norm_bias, self_project, self_output, cross_query, memory_project, cross_output, expert_in, expert_out, embedding):
    params = tuple((weight.astype(jnp.float32) for weight in (norm_gain, norm_bias, self_project, self_output, cross_query, memory_project, cross_output, expert_in, expert_out, embedding)))
    token_rows = inputs.astype(jnp.float32).reshape(ROWS, SEQ, D)
    memory_rows = memory.astype(jnp.float32).reshape(ROWS, MEM, D)
    route_rows = expert_ids[:, :, 0].reshape(2, ROWS, SEQ).transpose(1, 0, 2)
    target_rows = targets.reshape(ROWS, SEQ)

    def whole(token_part, memory_part, weights):

        def one_row(row):
            return jax.checkpoint(layer_row)(row, weights)
        blocks, sums = lax.map(one_row, (token_part, memory_part, route_rows, target_rows, lengths, memory_mask))
        return (blocks, jnp.sum(sums))
    (blocks, objective), pullback = jax.vjp(whole, token_rows, memory_rows, params)
    grads = pullback((jnp.zeros_like(blocks), jnp.ones_like(objective)))
    block_out = blocks.transpose(1, 0, 2, 3).reshape(2, ROWS * SEQ, D)
    mean_loss = objective / jnp.sum(lengths).astype(jnp.float32)
    weight_grads = grads[2]
    return (block_out, mean_loss, grads[0].reshape(ROWS * SEQ, D), grads[1].reshape(ROWS * MEM, D), weight_grads[0], weight_grads[1], weight_grads[2], weight_grads[3], weight_grads[4], weight_grads[5], weight_grads[6], weight_grads[7], weight_grads[8], weight_grads[9])
```

```python
import functools

import jax
import jax.numpy as jnp
from jax import lax
from jax.experimental import pallas as pl
from jax.experimental.pallas import tpu as pltpu
from jax.sharding import PartitionSpec as P

HEADS = 8
VOCAB = 32000
GROUPS = 4
EPSILON = 1e-05
SMOOTH = 0.1
F32 = jnp.float32
BF16 = jnp.bfloat16
PARAMS = pltpu.CompilerParams(vmem_limit_bytes=56 * 1024 * 1024)


def swap(block, axis, mask):
    count = lax.axis_size(axis)
    return lax.ppermute(block, axis, [(i, i ^ mask) for i in range(count)])


def after(value, *others):
    return lax.optimization_barrier((value,) + others)[0]


def gather_xor(block, axis):
    count = lax.axis_size(axis)
    if count == 8:
        far = {g: swap(block, axis, 2 * g) for g in (2, 3, 1)}
        near = {0: swap(block, axis, 1)}
        for g in (1, 3, 2):
            near[g] = swap(far[g], axis, 1)
        far[0] = block
        return [part for g in range(4) for part in (far[g], near[g])]
    blocks = [block]
    step = 1
    while step < count:
        blocks = blocks + [swap(part, axis, step) for part in blocks]
        step *= 2
    return blocks


def scatter_sum_xor(blocks, axis):
    count = lax.axis_size(axis)
    if count == 8:
        near = {g: swap(blocks[2 * g + 1].astype(BF16), axis, 1) for g in (2, 3, 1, 0)}
        total = None
        for g in (2, 3, 1, 0):
            part = blocks[2 * g].astype(F32) + near[g].astype(F32)
            if g:
                part = swap(part.astype(BF16), axis, 2 * g).astype(F32)
            total = part if total is None else total + part
        return total
    step = count // 2
    while step >= 1:
        blocks = [
            blocks[k].astype(F32) + swap(blocks[k + step].astype(BF16), axis, step).astype(F32)
            for k in range(step)
        ]
        step //= 2
    return blocks[0]


def dot(left, right):
    return jnp.dot(left, right, preferred_element_type=F32)


def ein(spec, left, right):
    return jnp.einsum(spec, left, right, preferred_element_type=F32)


def attend_forward_kernel(causal, kn_ref, qt_ref, vt_ref, bias_ref, ot_ref, lse_ref):
    keys, tokens = kn_ref.shape[0], qt_ref.shape[1]
    head = qt_ref.shape[0] // 2
    zeros = jnp.zeros((head, tokens), BF16)
    if causal:
        rows = lax.broadcasted_iota(jnp.int32, (keys, tokens), 0)
        cols = lax.broadcasted_iota(jnp.int32, (keys, tokens), 1)
        allowed = rows <= cols
    for h in range(2):
        q = qt_ref[h * head : (h + 1) * head, :]
        q = jnp.concatenate([zeros, q] if h else [q, zeros], axis=0)
        s = dot(kn_ref[...], q)
        s = jnp.where(allowed, s, -1e30) if causal else s + bias_ref[...]
        m = jnp.max(s, axis=0, keepdims=True)
        e = jnp.exp(s - m)
        total = jnp.sum(e, axis=0, keepdims=True)
        p = (e * (1.0 / total)).astype(BF16)
        ot_ref[h * head : (h + 1) * head, :] = dot(
            vt_ref[h * head : (h + 1) * head, :], p
        ).astype(BF16)
        lse_ref[0, h : h + 1, :] = m + jnp.log(total)


def attend_forward(kn, qt, vt, bias, causal):
    keys, width = kn.shape
    tokens = qt.shape[1]
    pair = 2 * width // HEADS
    wide = pl.BlockSpec((pair, tokens), lambda j: (j, 0))
    return pl.pallas_call(
        functools.partial(attend_forward_kernel, causal),
        grid=(HEADS // 2,),
        in_specs=[
            pl.BlockSpec((keys, pair), lambda j: (0, j)),
            wide,
            pl.BlockSpec((pair, keys), lambda j: (j, 0)),
            pl.BlockSpec((keys, 1), lambda j: (0, 0)),
        ],
        out_specs=[wide, pl.BlockSpec((1, 2, tokens), lambda j: (j, 0, 0))],
        out_shape=[
            jax.ShapeDtypeStruct((width, tokens), BF16),
            jax.ShapeDtypeStruct((HEADS // 2, 2, tokens), F32),
        ],
        compiler_params=PARAMS,
    )(kn, qt, vt, bias)


def attend_backward_kernel(
    causal, kn_ref, kt_ref, vn_ref, qt_ref, qn_ref, dot_ref, don_ref, lse_ref, bias_ref, dqt_ref, dk_ref, dv_ref
):
    keys, tokens = kn_ref.shape[0], qt_ref.shape[1]
    head = qt_ref.shape[0] // 2
    zeros = jnp.zeros((head, tokens), BF16)
    lanes = lax.broadcasted_iota(jnp.int32, (tokens, 2 * head), 1)
    if causal:
        rows = lax.broadcasted_iota(jnp.int32, (keys, tokens), 0)
        cols = lax.broadcasted_iota(jnp.int32, (keys, tokens), 1)
        allowed = rows <= cols
    dk = jnp.zeros((keys, 2 * head), F32)
    dv = jnp.zeros((keys, 2 * head), F32)
    for h in range(2):
        mine = (lanes >= head) if h else (lanes < head)
        span = slice(h * head, (h + 1) * head)
        q, do = qt_ref[span, :], dot_ref[span, :]
        q = jnp.concatenate([zeros, q] if h else [q, zeros], axis=0)
        do = jnp.concatenate([zeros, do] if h else [do, zeros], axis=0)
        s = dot(kn_ref[...], q)
        s = jnp.where(allowed, s, -1e30) if causal else s + bias_ref[...]
        p = jnp.exp(s - lse_ref[0, h : h + 1, :])
        dp = dot(vn_ref[...], do)
        pdp = p * dp
        total = jnp.sum(pdp, axis=0, keepdims=True)
        ds = (pdp - p * total).astype(BF16)
        dqt_ref[span, :] = (dot(kt_ref[span, :], ds) * head**-0.5).astype(BF16)
        dk = dk + dot(ds, jnp.where(mine, qn_ref[...], jnp.zeros_like(qn_ref[...])))
        dv = dv + dot(p.astype(BF16), jnp.where(mine, don_ref[...], jnp.zeros_like(don_ref[...])))
    dk_ref[...] = dk.astype(BF16)
    dv_ref[...] = dv.astype(BF16)


def attend_backward(kn, kt, vn, qt, qn, do_t, do_n, lse, bias, causal):
    keys, width = kn.shape
    tokens = qt.shape[1]
    pair = 2 * width // HEADS
    key_rows = pl.BlockSpec((keys, pair), lambda j: (0, j))
    wide = pl.BlockSpec((pair, tokens), lambda j: (j, 0))
    tall = pl.BlockSpec((tokens, pair), lambda j: (0, j))
    return pl.pallas_call(
        functools.partial(attend_backward_kernel, causal),
        grid=(HEADS // 2,),
        in_specs=[
            key_rows,
            pl.BlockSpec((pair, keys), lambda j: (j, 0)),
            key_rows,
            wide,
            tall,
            wide,
            tall,
            pl.BlockSpec((1, 2, tokens), lambda j: (j, 0, 0)),
            pl.BlockSpec((keys, 1), lambda j: (0, 0)),
        ],
        out_specs=[wide, key_rows, key_rows],
        out_shape=[
            jax.ShapeDtypeStruct((width, tokens), BF16),
            jax.ShapeDtypeStruct((keys, width), BF16),
            jax.ShapeDtypeStruct((keys, width), BF16),
        ],
        compiler_params=PARAMS,
    )(kn, kt, vn, qt, qn, do_t, do_n, lse, bias)


def first_sweep_kernel(e_ref, ht_ref, stat_in_ref, sum_in_ref, stat_ref, sum_ref):
    half = ht_ref.shape[1] // 2

    @pl.when(pl.program_id(0) == 0)
    def _():
        stat_ref[...] = stat_in_ref[...]
        sum_ref[...] = sum_in_ref[...]

    rows = e_ref[...]
    z = dot(rows, ht_ref[...])
    old = stat_ref[0:1, :]
    top = jnp.maximum(old, jnp.max(z, axis=0, keepdims=True))
    e = jnp.exp(z - top)
    gap = z[:, :half] - z[:, half:]
    drift = jnp.concatenate(
        [
            jnp.sum(e[:, :half] * gap, axis=0, keepdims=True),
            -jnp.sum(e[:, half:] * gap, axis=0, keepdims=True),
        ],
        axis=1,
    )
    factor = jnp.exp(old - top)
    stat_ref[0:1, :] = top
    stat_ref[1:2, :] = stat_ref[1:2, :] * factor + jnp.sum(e, axis=0, keepdims=True)
    stat_ref[2:3, :] = stat_ref[2:3, :] * factor + drift
    sum_ref[...] += dot(jnp.ones((8, rows.shape[0]), BF16), rows)


def block_of(rows):
    for size in (400, 200, 80, 40, 16):
        if rows % size == 0:
            return size
    return rows


def first_sweep(rows, ht, stats, sums):
    count, width = rows.shape
    block = block_of(count)
    whole = lambda a: pl.BlockSpec(a.shape, lambda i: (0, 0))
    return pl.pallas_call(
        first_sweep_kernel,
        grid=(count // block,),
        in_specs=[pl.BlockSpec((block, width), lambda i: (i, 0)), whole(ht), whole(stats), whole(sums)],
        out_specs=[whole(stats), whole(sums)],
        out_shape=[jax.ShapeDtypeStruct(stats.shape, F32), jax.ShapeDtypeStruct(sums.shape, F32)],
        compiler_params=PARAMS,
    )(rows, ht, stats, sums)


def second_sweep_kernel(
    base, e_ref, ht_ref, hn_ref, row_ref, target_ref, flat_ref, acc_in_ref, hit_in_ref, de_ref, acc_ref, hit_ref
):
    half = ht_ref.shape[1] // 2
    block = e_ref.shape[0]
    step = pl.program_id(0)

    @pl.when(step == 0)
    def _():
        acc_ref[...] = acc_in_ref[...]
        hit_ref[...] = hit_in_ref[...]

    rows = e_ref[...]
    z = dot(rows, ht_ref[...])
    z0, z1 = z[:, :half], z[:, half:]
    p0 = jnp.exp(z0 - row_ref[0:1, :half])
    p1 = jnp.exp(z1 - row_ref[0:1, half:])
    gap = z0 - z1
    spot = lax.broadcasted_iota(jnp.int32, (block, half), 0)
    hit = spot == target_ref[0:1, :] - (base + step * block)
    picked = jnp.where(hit, row_ref[2:3, :half], 0.0)
    hit_ref[0:1, :] += jnp.sum(jnp.where(hit, z0 + z1, 0.0), axis=0, keepdims=True)
    g0 = p0 * (row_ref[1:2, :half] + gap) - p1 - picked
    g1 = p1 * (row_ref[1:2, half:] - gap) - p0 - picked
    dz = jnp.concatenate([g0.astype(BF16), g1.astype(BF16)], axis=1)
    de_ref[...] = (dot(dz, hn_ref[...]) + flat_ref[0:1, :]).astype(BF16)
    acc_ref[...] += lax.dot_general(rows, dz, (((0,), (0,)), ((), ())), preferred_element_type=F32)


def second_sweep(base, rows, ht, hn, row_stats, target, flat, acc, hits):
    count, width = rows.shape
    block = block_of(count)
    whole = lambda a: pl.BlockSpec(a.shape, lambda i: (0, 0))
    tall = pl.BlockSpec((block, width), lambda i: (i, 0))
    return pl.pallas_call(
        functools.partial(second_sweep_kernel, base),
        grid=(count // block,),
        in_specs=[tall] + [whole(a) for a in (ht, hn, row_stats, target, flat, acc, hits)],
        out_specs=[tall, whole(acc), whole(hits)],
        out_shape=[
            jax.ShapeDtypeStruct((count, width), BF16),
            jax.ShapeDtypeStruct(acc.shape, F32),
            jax.ShapeDtypeStruct(hits.shape, F32),
        ],
        compiler_params=PARAMS,
    )(rows, ht, hn, row_stats, target, flat, acc, hits)


def pick_kernel(order_ref, block_ref, out_ref):
    out_ref[...] = block_ref[...].astype(out_ref.dtype)


def pick_blocks(stack, order, dtype):
    shape = stack.shape[1:]
    return pl.pallas_call(
        pick_kernel,
        grid_spec=pltpu.PrefetchScalarGridSpec(
            num_scalar_prefetch=1,
            grid=(order.shape[0],),
            in_specs=[pl.BlockSpec((1,) + shape, lambda j, order_ref: (order_ref[j], 0, 0))],
            out_specs=pl.BlockSpec((1,) + shape, lambda j, order_ref: (j, 0, 0)),
        ),
        out_shape=jax.ShapeDtypeStruct((order.shape[0],) + shape, dtype),
        compiler_params=PARAMS,
    )(order, stack)


def norm_forward(values, gain, bias):
    average = jnp.mean(values, axis=0, keepdims=True)
    centered = values - average
    scale = lax.rsqrt(jnp.mean(centered * centered, axis=0, keepdims=True) + EPSILON)
    return centered * scale * gain + bias


def norm_backward(values, gain, upstream):
    average = jnp.mean(values, axis=0, keepdims=True)
    centered = values - average
    scale = lax.rsqrt(jnp.mean(centered * centered, axis=0, keepdims=True) + EPSILON)
    unit = centered * scale
    grad = upstream * gain
    result = scale * (
        grad - jnp.mean(grad, axis=0, keepdims=True) - unit * jnp.mean(grad * unit, axis=0, keepdims=True)
    )
    return result, jnp.sum(upstream * unit, axis=1), jnp.sum(upstream, axis=1)


def group_sum(first, second):
    core = lax.axis_index("vocab")
    mine = jnp.where(core == 0, first, second)
    theirs = jnp.where(core == 0, second, first)
    part = mine + swap(theirs.astype(BF16), "vocab", 1).astype(F32)
    part = part.astype(BF16)
    part = part.astype(F32) + swap(part, "pass", 1).astype(F32)
    other = swap(part, "vocab", 1)
    return jnp.where(core == 0, part, other), jnp.where(core == 0, other, part)


def local(
    inputs,
    memory,
    expert_ids,
    targets,
    lengths,
    memory_mask,
    norm_gain,
    norm_bias,
    self_project,
    self_output,
    cross_query,
    memory_project,
    cross_output,
    expert_in,
    expert_out,
    embedding,
):
    seq_len, width = inputs.shape
    rows_axis = lax.axis_size("dp")
    here = lax.axis_index("dp")
    which = lax.axis_index("pass")
    core = lax.axis_index("vocab")
    shards = 2 * rows_axis

    matrices = (self_project, self_output, cross_query, memory_project, cross_output)
    sizes = [matrix.shape[1] for matrix in matrices]
    half_rows = sizes[0] + sizes[1]
    norm_width = norm_gain.shape[1]
    norm_pack = jnp.concatenate([norm_gain, norm_bias], axis=0).reshape(1, 8 * norm_width)
    norm_pack = jnp.pad(norm_pack, ((0, 15), (0, width - 8 * norm_width)))
    packed = jnp.concatenate(matrices, axis=1).T
    mine = jnp.concatenate(
        [jnp.where(core == 0, packed[:half_rows], packed[half_rows:]), norm_pack], axis=0
    )
    got = gather_xor(mine, "dp")
    got = jnp.stack(got)
    got = jnp.stack([got, swap(got, "pass", 1)], axis=1)
    twin = swap(got, "vocab", 1)
    order = jnp.arange(rows_axis)[:, None] ^ here
    order = (2 * order + (jnp.arange(2)[None, :] ^ which)).reshape(-1).astype(jnp.int32)
    flat = (shards,) + mine.shape
    got = pick_blocks(got.reshape(flat), order, BF16)
    twin = pick_blocks(twin.reshape(flat), order, BF16)
    self_pack = jnp.where(core == 0, got, twin)
    cross_pack = jnp.where(core == 0, twin, got)
    norms = self_pack[:, half_rows, : 8 * norm_width].reshape(shards, 8, norm_width)
    norms = norms.transpose(1, 0, 2).reshape(8, width).astype(F32)
    gains = [norms[j][:, None] for j in range(4)]
    biases = [norms[4 + j][:, None] for j in range(4)]
    project_t = self_pack[:, : sizes[0]].reshape(-1, width)
    self_output_t = self_pack[:, sizes[0] : half_rows].reshape(-1, width)
    cross_query_t = cross_pack[:, : sizes[2]].reshape(-1, width)
    memory_project_t = cross_pack[:, sizes[2] : sizes[2] + sizes[3]].reshape(-1, width)
    cross_output_t = cross_pack[:, sizes[2] + sizes[3] : half_rows].reshape(-1, width)

    experts = expert_in.shape[0] // 2
    hidden = expert_in.shape[2]

    def core_half(weights):
        halves = weights.reshape(2, experts, width, hidden)
        return jnp.where(core == 0, halves[0], halves[1]).transpose(0, 2, 1)

    expert_block = jnp.stack([core_half(expert_in), core_half(expert_out)])
    expert_got = gather_xor(after(expert_block, got), "dp")
    weight_in = jnp.concatenate([part[0].reshape(-1, width) for part in expert_got])
    weight_out = jnp.concatenate([part[1].reshape(-1, width) for part in expert_got])

    word_got = gather_xor(after(embedding, expert_got[-1]), "dp")
    per_group = rows_axis // GROUPS
    words = [
        jnp.concatenate(word_got[g * per_group : (g + 1) * per_group]) for g in range(GROUPS)
    ]
    group_rows = words[0].shape[0]

    scaling = (width // HEADS) ** -0.5
    tokens = inputs.T.astype(F32)
    a1 = norm_forward(tokens, gains[0], biases[0]).astype(BF16)
    qkv_t = dot(project_t, a1).astype(BF16)
    query_t = qkv_t[:width] * jnp.asarray(scaling, BF16)
    key_t, value_t = qkv_t[width : 2 * width], qkv_t[2 * width :]
    key_n, value_n = key_t.T, value_t.T
    no_bias = jnp.zeros((seq_len, 1), F32)
    attended_t, self_lse = attend_forward(key_n, query_t, value_t, no_bias, True)
    h1 = tokens + dot(self_output_t, attended_t)
    a2 = norm_forward(h1, gains[1], biases[1]).astype(BF16)
    cross_t = dot(cross_query_t, a2).astype(BF16) * jnp.asarray(scaling, BF16)
    memory_kv = ein("mi,oi->mo", memory, memory_project_t).astype(BF16)
    mem_key, mem_value = memory_kv[:, :width], memory_kv[:, width:]
    mem_bias = jnp.where(memory_mask[0][:, None] == 1, 0.0, -1e30).astype(F32)
    cross_att_t, cross_lse = attend_forward(mem_key, cross_t, mem_value.T, mem_bias, False)
    h2 = h1 + dot(cross_output_t, cross_att_t)
    a3 = norm_forward(h2, gains[2], biases[2]).astype(BF16)

    my_route = expert_ids[0, :, 0].astype(F32)[None, :]
    other_route = swap(my_route, "pass", 1)
    routes = (jnp.where(which == 0, my_route, other_route), jnp.where(which == 0, other_route, my_route))
    names = (core * experts + jnp.arange(experts)).astype(F32)
    masks = [(route == names[:, None])[None, :, None, :] for route in routes]
    shape4 = (rows_axis, experts, hidden, seq_len)

    def routed(values, mask):
        return jnp.where(mask, values.reshape(shape4), jnp.zeros((), values.dtype)).reshape(values.shape)

    pre_act = dot(weight_in, a3)
    activation = jax.nn.gelu(pre_act).astype(BF16)
    active = jnp.concatenate([routed(activation, mask) for mask in masks], axis=1)
    part = ein("fd,ft->dt", weight_out, active)
    y0, y1 = group_sum(part[:, :seq_len], part[:, seq_len:])
    block0, block1 = h2 + y0, h2 + y1
    final0 = norm_forward(block0, gains[3], biases[3]).astype(BF16)
    final1 = norm_forward(block1, gains[3], biases[3]).astype(BF16)
    block_out = jnp.where(which == 0, block0, block1).T[None]

    final_t = jnp.concatenate([final0, final1], axis=1)
    final_n = final_t.T
    valid = (jnp.arange(seq_len) < lengths[here]).astype(F32)
    half_weight = 0.5 * valid
    stats = jnp.concatenate(
        [jnp.full((1, 2 * seq_len), -1e30, F32), jnp.zeros((7, 2 * seq_len), F32)], axis=0
    )
    sums = jnp.zeros((8, width), F32)
    for g in range(GROUPS):
        stats, sums = first_sweep(words[g], final_t, stats, sums)

    def merge(left, axis):
        right = swap(left, axis, 1)
        top = jnp.maximum(left[0:1], right[0:1])
        total = left[1:] * jnp.exp(left[0:1] - top) + right[1:] * jnp.exp(right[0:1] - top)
        return jnp.concatenate([top, total], axis=0)

    merged = merge(merge(stats, "vocab"), "pass")
    lse = merged[0:1] + jnp.log(merged[1:2])
    drift = merged[2:3] / merged[1:2]
    weight2 = jnp.concatenate([half_weight, half_weight])[None, :]
    valid2 = weight2 > 0
    row_stats = jnp.concatenate(
        [
            jnp.where(valid2, lse + jnp.log(2.0), 1e30),
            2.0 - drift,
            (1.0 - SMOOTH) * weight2,
            jnp.zeros((5, 2 * seq_len), F32),
        ],
        axis=0,
    )
    shard_rows = embedding.shape[0]
    owner = targets // shard_rows
    in_quarter = (owner % 2 == core) & (owner // 2 % 2 == which)
    column = ((owner // 4) ^ here) * shard_rows + targets % shard_rows
    target = jnp.broadcast_to(jnp.where(in_quarter, column, -1)[None, :], (8, seq_len)).astype(jnp.int32)
    hidden_sum = jnp.sum(final_t.astype(F32) * weight2, axis=1)
    level = SMOOTH / VOCAB
    flat_grad = jnp.broadcast_to(-level * hidden_sum[None, :], (8, width))
    hits = jnp.zeros((8, seq_len), F32)
    acc = -level * sums[0][:, None] * weight2
    word_grads = []
    for g in range(GROUPS):
        grads, acc, hits = second_sweep(
            g * group_rows, words[g], final_t, final_n, row_stats, target, flat_grad, acc, hits
        )
        word_grads += [
            grads[k * shard_rows : (k + 1) * shard_rows] for k in range(per_group)
        ]
    embedding_grad = scatter_sum_xor(word_grads, "dp")
    loss = (
        0.25 * jnp.sum(weight2 * (lse + drift))
        - (1.0 - SMOOTH) * jnp.sum(half_weight * hits[0])
        - level * jnp.sum(hidden_sum * sums[0])
    )
    loss = jnp.broadcast_to(loss, (8, 128))
    for axis in ("vocab", "pass"):
        loss = loss + swap(loss, axis, 1)
    step = 1
    while step < rows_axis:
        loss = loss + swap(loss, "dp", step)
        step *= 2
    mean_loss = loss[0, 0] / jnp.sum(lengths).astype(F32)

    dh0, dh1 = group_sum(acc[:, :seq_len], acc[:, seq_len:])
    db0, gain0, bias0 = norm_backward(block0, gains[3], dh0)
    db1, gain1, bias1 = norm_backward(block1, gains[3], dh1)
    gain_three, bias_three = gain0 + gain1, bias0 + bias1
    dy = jnp.concatenate([db0, db1], axis=1).astype(BF16)
    d_act = dot(weight_out, dy)
    picked = routed(d_act[:, :seq_len], masks[0]) + routed(d_act[:, seq_len:], masks[1])
    unused, pull = jax.vjp(jax.nn.gelu, pre_act)
    du = pull(picked)[0].astype(BF16)
    da3_part = ein("fd,ft->dt", weight_in, du)
    in_grad = ein("ft,dt->fd", du, a3).reshape(rows_axis, experts, hidden, width)
    out_grad = ein("ft,dt->fd", active, dy).reshape(rows_axis, experts, hidden, width)
    expert_grad = scatter_sum_xor(
        [jnp.stack([in_grad[k], out_grad[k]]).astype(BF16) for k in range(rows_axis)], "dp"
    )
    expert_twin = swap(expert_grad, "vocab", 1)
    expert_grad = jnp.concatenate(
        [
            jnp.where(core == 0, expert_grad, expert_twin),
            jnp.where(core == 0, expert_twin, expert_grad),
        ],
        axis=1,
    ).transpose(0, 1, 3, 2)
    half = seq_len // 2
    left, right = group_sum(da3_part[:, :half], da3_part[:, half:])
    da3 = jnp.concatenate([left, right], axis=1)
    two_grad, gain_two, bias_two = norm_backward(h2, gains[2], da3)
    dh2 = db0 + db1 + two_grad

    cross_low = dh2.astype(BF16)
    cross_output_grad = ein("ot,it->oi", cross_low, cross_att_t)
    do_t = ein("oi,ot->it", cross_output_t, cross_low).astype(BF16)
    dq_t, dk, dv = attend_backward(
        mem_key, mem_key.T, mem_value, cross_t, cross_t.T, do_t, do_t.T, cross_lse, mem_bias, False
    )
    cross_query_grad = ein("ot,it->oi", dq_t, a2)
    pair_grad = jnp.concatenate([dk, dv], axis=1)
    memory_project_grad = ein("mo,mi->oi", pair_grad, memory)
    memory_grad = dot(pair_grad, memory_project_t)
    da2 = ein("oi,ot->it", cross_query_t, dq_t)
    one_grad, gain_one, bias_one = norm_backward(h1, gains[1], da2)
    dh1 = dh2 + one_grad
    self_low = dh1.astype(BF16)
    self_output_grad = ein("ot,it->oi", self_low, attended_t)
    so_t = ein("oi,ot->it", self_output_t, self_low).astype(BF16)
    sq_t, sk, sv = attend_backward(
        key_n, key_t, value_n, query_t, query_t.T, so_t, so_t.T, self_lse, no_bias, True
    )
    project_low = jnp.concatenate([sq_t, sk.T, sv.T], axis=0)
    self_project_grad = ein("ot,it->oi", project_low, a1)
    da1 = ein("oi,ot->it", project_t, project_low)
    zero_grad, gain_zero, bias_zero = norm_backward(tokens, gains[0], da1)
    inputs_grad = (dh1 + zero_grad).T

    norm_grads = jnp.stack(
        [gain_zero, gain_one, gain_two, gain_three, bias_zero, bias_one, bias_two, bias_three]
    )
    norm_grads = norm_grads.reshape(8, shards, norm_width).transpose(1, 0, 2).reshape(shards, 1, -1)
    norm_grads = jnp.pad(norm_grads, ((0, 0), (0, 15), (0, width - 8 * norm_width)))

    def shard_blocks(grads):
        return jnp.concatenate(
            [grad.reshape(shards, -1, width) for grad in grads] + [norm_grads], axis=1
        ).astype(BF16)

    stack = jnp.concatenate(
        [
            shard_blocks([self_project_grad, self_output_grad]),
            shard_blocks([cross_query_grad, memory_project_grad, cross_output_grad]),
        ]
    )
    order = core * shards + 2 * (jnp.arange(rows_axis) ^ here) + which
    blocks = pick_blocks(stack, order.astype(jnp.int32), BF16)
    layer_grad = scatter_sum_xor([blocks[k] for k in range(rows_axis)], "dp")
    layer_twin = swap(layer_grad, "vocab", 1)
    first = jnp.where(core == 0, layer_grad, layer_twin)
    second = jnp.where(core == 0, layer_twin, layer_grad)
    norm_out = first[half_rows, : 8 * norm_width].reshape(8, norm_width)
    first, second = first[:half_rows].T, second[:half_rows].T
    return (
        block_out,
        mean_loss,
        inputs_grad,
        memory_grad,
        norm_out[:4],
        norm_out[4:],
        first[:, : sizes[0]],
        first[:, sizes[0] :],
        second[:, : sizes[2]],
        second[:, sizes[2] : sizes[2] + sizes[3]],
        second[:, sizes[2] + sizes[3] :],
        expert_grad[0],
        expert_grad[1],
        embedding_grad,
    )


def solution(mesh):
    shared = P(None, ("dp", "pass"))
    placed = (
        P("dp", None),
        P("dp", None),
        P("pass", "dp", None),
        P("dp"),
        P(),
        P("dp", None),
        shared,
        shared,
        shared,
        shared,
        shared,
        shared,
        shared,
        P(None, None, ("dp", "pass")),
        P(None, None, ("dp", "pass")),
        P(("dp", "pass", "vocab"), None),
    )
    return jax.shard_map(
        local,
        mesh=mesh,
        in_specs=placed,
        out_specs=(
            P("pass", "dp", None),
            P(),
            P("dp", None),
            P("dp", None),
            shared,
            shared,
            shared,
            shared,
            shared,
            shared,
            shared,
            P(None, None, ("dp", "pass")),
            P(None, None, ("dp", "pass")),
            P(("dp", "pass", "vocab"), None),
        ),
        check_vma=False,
    )
```

```python
import functools

import jax
import jax.numpy as jnp
from jax import lax
from jax.experimental import pallas as pl
from jax.experimental.pallas import tpu as pltpu
from jax.sharding import PartitionSpec as P

HEADS = 8
VOCAB = 32000
GROUPS = 4
EPSILON = 1e-05
SMOOTH = 0.1
F32 = jnp.float32
BF16 = jnp.bfloat16
PARAMS = pltpu.CompilerParams(vmem_limit_bytes=56 * 1024 * 1024)
COST = pl.CostEstimate(flops=1000, bytes_accessed=1000, transcendentals=0)


def swap(block, axis, mask):
    count = lax.axis_size(axis)
    return lax.ppermute(block, axis, [(i, i ^ mask) for i in range(count)])


def after(value, mark):
    return value if mark is None else lax.optimization_barrier((value, mark))[0]


class Gather:
    def __init__(self, block, axis):
        self.block, self.axis, self.count = block, axis, lax.axis_size(axis)
        self.near, self.far = {}, {0: block}

    def send(self, steps, mark=None):
        if self.count == 8:
            block = after(self.block, mark)
            for g in steps:
                self.far[g] = swap(block, self.axis, 2 * g)

    def forward(self, steps, mark=None):
        if self.count == 8:
            for g in steps:
                self.near[g] = swap(after(self.far[g], mark), self.axis, 1)

    def forward_together(self, steps, mark=None):
        if self.count == 8:
            sent = swap(jnp.stack([after(self.far[g], mark) for g in steps]), self.axis, 1)
            for n, g in enumerate(steps):
                self.near[g] = sent[n]

    def arrived(self, far=(), near=()):
        return [self.far[g] for g in far] + [self.near[g] for g in near] if self.count == 8 else None

    def mark(self, g):
        return self.far[g] if self.count == 8 else None

    def result(self):
        if self.count == 8:
            return [part for g in range(4) for part in (self.far[g], self.near[g])]
        blocks, step = [self.block], 1
        while step < self.count:
            blocks = blocks + [swap(part, self.axis, step) for part in blocks]
            step *= 2
        return blocks


class ScatterSum:
    def __init__(self, axis):
        self.axis = axis
        self.count = lax.axis_size(axis)
        self.blocks, self.near, self.far, self.kept = {}, {}, {}, None

    def give(self, groups, fars, nears, split=0, mark=None):
        per_half = self.count // (2 * GROUPS)
        if self.count == 8:
            sent = swap(after(nears, mark), self.axis, 1)
        for n, g in enumerate(groups):
            if self.count == 8:
                self.blocks[2 * g], self.near[g] = fars[n], (sent, n)
                continue
            for half, array in enumerate((fars[n], nears[n])):
                for k, piece in enumerate(jnp.split(array, per_half, axis=split)):
                    self.blocks[(2 * g + half) * per_half + k] = piece

    def forward(self, groups, mark=None):
        if self.count == 8:
            for g in groups:
                sent, n = self.near[g]
                part = self.blocks[2 * g].astype(F32) + after(sent, mark)[n].astype(F32)
                if g:
                    self.far[g] = swap(part.astype(BF16), self.axis, 2 * g)
                else:
                    self.kept = part

    def arrived(self, far=(), near=()):
        return [self.far[g] for g in far] + [self.near[g][0] for g in near] if self.count == 8 else None

    def result(self, mark=None):
        if self.count == 8:
            total = self.kept
            for g in (1, 2, 3):
                total = total + after(self.far[g], mark).astype(F32)
            return total
        blocks = [self.blocks[k] for k in range(self.count)]
        step = self.count // 2
        while step >= 1:
            blocks = [
                blocks[k].astype(F32) + swap(blocks[k + step].astype(BF16), self.axis, step).astype(F32)
                for k in range(step)
            ]
            step //= 2
        return blocks[0]


def dot(left, right):
    return jnp.dot(left, right, preferred_element_type=F32)


def dot_nt(left, right):
    return lax.dot_general(left, right, (((1,), (1,)), ((), ())), preferred_element_type=F32)


def dot_tn(left, right):
    return lax.dot_general(left, right, (((0,), (0,)), ((), ())), preferred_element_type=F32)


def call(kernel, outs, *args, scalars=None, scratch=()):
    specs = [pl.BlockSpec(memory_space=pltpu.VMEM)] * len(args)
    if scalars is not None:
        specs = [pl.BlockSpec(memory_space=pltpu.SMEM)] + specs
        args = (scalars,) + args
    return pl.pallas_call(
        kernel,
        in_specs=specs,
        out_specs=[pl.BlockSpec(memory_space=pltpu.VMEM)] * len(outs),
        out_shape=[jax.ShapeDtypeStruct(shape, dtype) for shape, dtype in outs],
        scratch_shapes=[pltpu.VMEM(shape, dtype) for shape, dtype in scratch],
        compiler_params=PARAMS,
        cost_estimate=COST,
    )(*args)


def by_core(flag_ref, low_ref, high_ref, mine, other):
    @pl.when(flag_ref[0] == 0)
    def _():
        low_ref[...], high_ref[...] = mine, other

    @pl.when(flag_ref[0] != 0)
    def _():
        low_ref[...], high_ref[...] = other, mine


def pair_parts(value, h):
    head = value.shape[0] // 2
    rows = value[h * head : (h + 1) * head]
    zeros = jnp.zeros_like(rows)
    return rows, jnp.concatenate([zeros, rows] if h else [rows, zeros], axis=0)


def pair_rows(j, size, start=0):
    return pl.ds(pl.multiple_of(start + j * size, size), size)


def norm_forward(values, gain, bias):
    average = jnp.mean(values, axis=0, keepdims=True)
    centered = values - average
    scale = lax.rsqrt(jnp.mean(centered * centered, axis=0, keepdims=True) + EPSILON)
    return centered * scale * gain + bias


def norm_backward(values, gain, upstream):
    average = jnp.mean(values, axis=0, keepdims=True)
    centered = values - average
    scale = lax.rsqrt(jnp.mean(centered * centered, axis=0, keepdims=True) + EPSILON)
    unit = centered * scale
    grad = upstream * gain
    result = scale * (
        grad - jnp.mean(grad, axis=0, keepdims=True) - unit * jnp.mean(grad * unit, axis=0, keepdims=True)
    )
    return result, jnp.sum(upstream * unit, axis=1, keepdims=True), jnp.sum(upstream, axis=1, keepdims=True)


def norm_columns(j, gain_grad, bias_grad, width):
    lanes = lax.broadcasted_iota(jnp.int32, (gain_grad.shape[0], width), 1)
    return jnp.where(lanes == j, gain_grad, 0.0) + jnp.where(lanes == 4 + j, bias_grad, 0.0)


def column(norms_ref, j):
    return norms_ref[:, j : j + 1].astype(F32)


def causal_mask(tokens):
    shape = (tokens, tokens)
    return lax.broadcasted_iota(jnp.int32, shape, 0) <= lax.broadcasted_iota(jnp.int32, shape, 1)


def heads_forward(query, keys_n, value_t, masked, out_ref, lse_ref, j):
    head = query.shape[0] // 2
    for h in range(2):
        s = masked(dot(keys_n, pair_parts(query, h)[1]))
        m = jnp.max(s, axis=0, keepdims=True)
        e = jnp.exp(s - m)
        total = jnp.sum(e, axis=0, keepdims=True)
        p = (e * (1.0 / total)).astype(BF16)
        out_ref[pair_rows(2 * j + h, head), :] = dot(value_t[h * head : (h + 1) * head], p).astype(BF16)
        lse_ref[j, h : h + 1, :] = m + jnp.log(total)


def heads_backward(query, key_t, keys_n, values_n, upstream, lse, masked):
    head = query.shape[0] // 2
    dq, dk, dv = [], 0.0, 0.0
    for h in range(2):
        q_pad = pair_parts(query, h)[1]
        do_pad = pair_parts(upstream, h)[1]
        p = jnp.exp(masked(dot(keys_n, q_pad)) - lse[h : h + 1, :])
        pdp = p * dot(values_n, do_pad)
        total = jnp.sum(pdp, axis=0, keepdims=True)
        ds = (pdp - p * total).astype(BF16)
        dq.append(dot(pair_parts(key_t, h)[0], ds) * head**-0.5)
        dk = dk + dot(ds, q_pad.T)
        dv = dv + dot(p.astype(BF16), do_pad.T)
    return jnp.concatenate(dq, axis=0).astype(BF16), dk.astype(BF16), dv.astype(BF16)


def self_forward_kernel(
    x_ref, norms_ref, project_ref, output_ref, query_ref, a1_ref, qkv_ref, att_ref, lse_ref, h1_ref, a2_ref, cross_ref
):
    tokens, width = x_ref.shape
    pair = 2 * width // HEADS
    scale = jnp.asarray((pair // 2) ** -0.5, BF16)
    a1_ref[...] = norm_forward(x_ref[...].T.astype(F32), column(norms_ref, 0), column(norms_ref, 4)).astype(BF16)
    qkv_ref[...] = dot(project_ref[...], a1_ref[...]).astype(BF16)

    def step(j, carry):
        allowed = causal_mask(tokens)
        heads_forward(
            qkv_ref[pair_rows(j, pair), :] * scale,
            qkv_ref[pair_rows(j, pair, width), :].T,
            qkv_ref[pair_rows(j, pair, 2 * width), :],
            lambda s: jnp.where(allowed, s, -1e30),
            att_ref,
            lse_ref,
            j,
        )
        return carry

    lax.fori_loop(0, HEADS // 2, step, 0)
    h1_ref[...] = x_ref[...].T.astype(F32) + dot(output_ref[...], att_ref[...])
    a2_ref[...] = norm_forward(h1_ref[...], column(norms_ref, 1), column(norms_ref, 5)).astype(BF16)
    cross_ref[...] = dot(query_ref[...], a2_ref[...]).astype(BF16) * scale


def self_forward(x, norms, project, output, query):
    tokens, width = x.shape
    bf = ((width, tokens), BF16)
    return call(
        self_forward_kernel,
        [bf, ((3 * width, tokens), BF16), bf, ((HEADS // 2, 2, tokens), F32), ((width, tokens), F32), bf, bf],
        *(x, norms, project, output, query),
    )


def memory_keys_kernel(memory_ref, weight_ref, out_ref):
    out_ref[...] = dot_nt(memory_ref[...], weight_ref[...]).astype(BF16)


def cross_forward_kernel(
    cross_ref, kv_ref, bias_ref, h1_ref, norms_ref, output_ref, att_ref, lse_ref, h2_ref, a3_ref, an_ref
):
    width = cross_ref.shape[0]
    pair = 2 * width // HEADS

    def step(j, carry):
        heads_forward(
            cross_ref[pair_rows(j, pair), :],
            kv_ref[:, pair_rows(j, pair)],
            kv_ref[:, pair_rows(j, pair, width)].T,
            lambda s: s + bias_ref[...],
            att_ref,
            lse_ref,
            j,
        )
        return carry

    lax.fori_loop(0, HEADS // 2, step, 0)
    h2_ref[...] = h1_ref[...] + dot(output_ref[...], att_ref[...])
    a3_ref[...] = norm_forward(h2_ref[...], column(norms_ref, 2), column(norms_ref, 6)).astype(BF16)
    an_ref[...] = a3_ref[...].T


def cross_forward(cross, kv, bias, h1, norms, output):
    width, tokens = cross.shape
    bf = ((width, tokens), BF16)
    return call(
        cross_forward_kernel,
        [bf, ((HEADS // 2, 2, tokens), F32), ((width, tokens), F32), bf, ((tokens, width), BF16)],
        *(cross, kv, bias, h1, norms, output),
    )


def final_norm_kernel(
    flags_ref, h2_ref, part_ref, other_ref, last_ref, norms_ref, weight_ref, b0_ref, b1_ref, ft_ref, fn_ref, out_ref, flat_ref
):
    tokens = h2_ref.shape[1]
    other = jnp.concatenate([other_ref[...], last_ref[...]], axis=0)
    by_core(flags_ref, b0_ref, b1_ref, h2_ref[...] + part_ref[...], h2_ref[...] + other)
    for p, ref in enumerate((b0_ref, b1_ref)):
        final = norm_forward(ref[...], column(norms_ref, 3), column(norms_ref, 7)).astype(BF16)
        ft_ref[:, p * tokens : (p + 1) * tokens] = final
        fn_ref[p * tokens : (p + 1) * tokens, :] = final.T

        @pl.when(flags_ref[1] == p)
        def _():
            out_ref[...] = ref[...].T

    flat_ref[...] = dot(weight_ref[...], fn_ref[...]) * (-SMOOTH / VOCAB)


def final_norm(flags, h2, part, other, norms, weight):
    width, tokens = h2.shape
    full = ((width, tokens), F32)
    return call(
        final_norm_kernel,
        [full, full, ((width, 2 * tokens), BF16), ((2 * tokens, width), BF16), ((tokens, width), F32), ((8, width), F32)],
        *(h2, part, *other, norms, weight),
        scalars=flags,
    )


def final_back_kernel(
    flags_ref, b0_ref, b1_ref, part_ref, other_ref, last_ref, norms_ref, db_ref, dy_ref, dn_ref, cols_ref, d0_ref, d1_ref
):
    tokens = b0_ref.shape[1]
    other = jnp.concatenate([other_ref[...], last_ref[...]], axis=0)
    by_core(flags_ref, d0_ref, d1_ref, part_ref[...], other)
    total, cols = 0.0, 0.0
    for p, (block_ref, d_ref) in enumerate(((b0_ref, d0_ref), (b1_ref, d1_ref))):
        grad, *norm_grads = norm_backward(block_ref[...], column(norms_ref, 3), d_ref[...])
        low = grad.astype(BF16)
        dy_ref[:, p * tokens : (p + 1) * tokens] = low
        dn_ref[p * tokens : (p + 1) * tokens, :] = low.T
        total, cols = total + grad, cols + norm_columns(3, *norm_grads, cols_ref.shape[1])
    db_ref[...], cols_ref[...] = total, cols


def final_back(flags, b0, b1, part, other, norms):
    width, tokens = b0.shape
    full = ((width, tokens), F32)
    return call(
        final_back_kernel,
        [full, ((width, 2 * tokens), BF16), ((2 * tokens, width), BF16), ((width, norms.shape[1]), F32)],
        *(b0, b1, part, *other, norms),
        scalars=flags,
        scratch=[full, full],
    )


def cross_back_kernel(
    flags_ref,
    db_ref,
    mine_ref,
    other_ref,
    last_ref,
    h2_ref,
    norms_ref,
    cols_in_ref,
    output_ref,
    att_ref,
    cross_ref,
    kv_ref,
    lse_ref,
    bias_ref,
    a2_ref,
    query_ref,
    h1_ref,
    dh1_ref,
    out_grad_ref,
    query_grad_ref,
    dkv_ref,
    cols_ref,
    d_ref,
    do_ref,
    dq_ref,
):
    width, tokens = h2_ref.shape
    pair, half = 2 * width // HEADS, tokens // 2
    other = jnp.concatenate([other_ref[...], last_ref[...]], axis=0)
    by_core(flags_ref, d_ref.at[:, :half], d_ref.at[:, half:], mine_ref[...], other)
    grad, *two = norm_backward(h2_ref[...], column(norms_ref, 2), d_ref[...])
    d_ref[...] = db_ref[...] + grad
    low = d_ref[...].astype(BF16)
    out_grad_ref[...] = dot_nt(low, att_ref[...]).astype(BF16)
    do_ref[...] = dot_tn(output_ref[...], low).astype(BF16)

    def step(j, carry):
        rows, keys, values = pair_rows(j, pair), pair_rows(j, pair), pair_rows(j, pair, width)
        dq, dk, dv = heads_backward(
            cross_ref[rows, :],
            kv_ref[:, keys].T,
            kv_ref[:, keys],
            kv_ref[:, values],
            do_ref[rows, :],
            lse_ref[j],
            lambda s: s + bias_ref[...],
        )
        dq_ref[rows, :], dkv_ref[:, keys], dkv_ref[:, values] = dq, dk, dv
        return carry

    lax.fori_loop(0, HEADS // 2, step, 0)
    query_grad_ref[...] = dot_nt(dq_ref[...], a2_ref[...]).astype(BF16)
    grad, *one = norm_backward(h1_ref[...], column(norms_ref, 1), dot_tn(query_ref[...], dq_ref[...]))
    dh1_ref[...] = d_ref[...] + grad
    columns = cols_ref.shape[1]
    cols_ref[...] = cols_in_ref[...] + norm_columns(2, *two, columns) + norm_columns(1, *one, columns)


def cross_back(flags, *args):
    h2, norms, kv = args[4], args[5], args[10]
    width, tokens = h2.shape
    full, bf = ((width, tokens), F32), ((width, tokens), BF16)
    square = ((width, width), BF16)
    return call(
        cross_back_kernel,
        [full, square, square, (kv.shape, BF16), (norms.shape, F32)],
        *args,
        scalars=flags,
        scratch=[full, bf, bf],
    )


def memory_back_kernel(dkv_ref, memory_ref, weight_ref, weight_grad_ref, memory_grad_ref):
    weight_grad_ref[...] = dot_tn(dkv_ref[...], memory_ref[...]).astype(BF16)
    memory_grad_ref[...] = dot(dkv_ref[...], weight_ref[...])


def self_back_kernel(
    dh1_ref, output_ref, att_ref, qkv_ref, lse_ref, a1_ref, x_ref, project_ref, norms_ref, cols_ref,
    out_grad_ref, project_grad_ref, inputs_grad_ref, norm_grad_ref, do_ref, dqkv_ref
):
    width, tokens = dh1_ref.shape
    pair = 2 * width // HEADS
    scale = jnp.asarray((pair // 2) ** -0.5, BF16)
    low = dh1_ref[...].astype(BF16)
    out_grad_ref[...] = dot_nt(low, att_ref[...]).astype(BF16)
    do_ref[...] = dot_tn(output_ref[...], low).astype(BF16)

    def step(j, carry):
        allowed = causal_mask(tokens)
        rows, keys, values = pair_rows(j, pair), pair_rows(j, pair, width), pair_rows(j, pair, 2 * width)
        key_t = qkv_ref[keys, :]
        dq, dk, dv = heads_backward(
            qkv_ref[rows, :] * scale,
            key_t,
            key_t.T,
            qkv_ref[values, :].T,
            do_ref[rows, :],
            lse_ref[j],
            lambda s: jnp.where(allowed, s, -1e30),
        )
        dqkv_ref[rows, :], dqkv_ref[keys, :], dqkv_ref[values, :] = dq, dk.T, dv.T
        return carry

    lax.fori_loop(0, HEADS // 2, step, 0)
    project_grad_ref[...] = dot_nt(dqkv_ref[...], a1_ref[...]).astype(BF16)
    grad, *zero = norm_backward(
        x_ref[...].T.astype(F32), column(norms_ref, 0), dot_tn(project_ref[...], dqkv_ref[...])
    )
    inputs_grad_ref[...] = (dh1_ref[...] + grad).T
    columns = cols_ref.shape[1]
    norm_grad_ref[...] = jnp.zeros(norm_grad_ref.shape, BF16)
    norm_grad_ref[:, :columns] = (cols_ref[...] + norm_columns(0, *zero, columns)).astype(BF16)


def self_back(*args):
    width, tokens = args[0].shape
    square = ((width, width), BF16)
    return call(
        self_back_kernel,
        [square, ((3 * width, width), BF16), ((tokens, width), F32), square],
        *args,
        scratch=[((width, tokens), BF16), ((3 * width, tokens), BF16)],
    )


def row_blocks(rows):
    parts = -(-rows // 512)
    size = -(-rows // (16 * parts)) * 16
    return [(start, min(start + size, rows)) for start in range(0, rows, size)]


def first_sweep_kernel(base, count, *refs):
    words, rest = refs[:count], refs[count:]
    ht_ref, target_ref, stat_in_ref, sum_in_ref, stat_ref, sum_ref = rest
    half = ht_ref.shape[1] // 2
    top, mass, drift = stat_in_ref[0:1, :], stat_in_ref[1:2, :], stat_in_ref[2:3, :]
    hits = stat_in_ref[3:4, :half]
    sums = sum_in_ref[...]
    for word_ref in words:
        for start, end in row_blocks(word_ref.shape[0]):
            rows = word_ref[start:end, :]
            z = dot(rows, ht_ref[...])
            old, top = top, jnp.maximum(top, jnp.max(z, axis=0, keepdims=True))
            e = jnp.exp(z - top)
            z0, z1 = z[:, :half], z[:, half:]
            gap = z0 - z1
            moved = jnp.concatenate(
                [
                    jnp.sum(e[:, :half] * gap, axis=0, keepdims=True),
                    -jnp.sum(e[:, half:] * gap, axis=0, keepdims=True),
                ],
                axis=1,
            )
            spot = lax.broadcasted_iota(jnp.int32, (end - start, half), 0)
            hit = spot == target_ref[0:1, :] - (base + start)
            hits = hits + jnp.sum(jnp.where(hit, z0 + z1, 0.0), axis=0, keepdims=True)
            factor = jnp.exp(old - top)
            mass = mass * factor + jnp.sum(e, axis=0, keepdims=True)
            drift = drift * factor + moved
            sums = sums + dot(jnp.ones((8, end - start), BF16), rows)
        base += word_ref.shape[0]
    hits = jnp.concatenate([hits, jnp.zeros_like(hits)], axis=1)
    stat_ref[...] = jnp.concatenate([top, mass, drift, hits, jnp.zeros((4, 2 * half), F32)], axis=0)
    sum_ref[...] = sums


def first_sweep(base, words, ht, target, stats, sums):
    return call(
        functools.partial(first_sweep_kernel, base, len(words)),
        [(stats.shape, F32), (sums.shape, F32)],
        *(*words, ht, target, stats, sums),
    )


def second_sweep_kernel(bases, last, flags_ref, *refs):
    count = len(bases)
    words, rest = refs[: 2 * count], refs[2 * count :]
    ht_ref, hn_ref, row_ref, target_ref, flat_ref, acc_in_refs = *rest[:5], rest[5:7]
    fars, near_ref, outs = rest[7 : 7 + count], rest[7 + count], rest[8 + count : 10 + count]
    acc_refs = rest[10 + count :] if last else outs
    half = ht_ref.shape[1] // 2
    sources = acc_in_refs
    for n, word_ref in enumerate(words):
        base = bases[n // 2] + (n % 2) * word_ref.shape[0]
        for start, end in row_blocks(word_ref.shape[0]):
            rows = word_ref[start:end, :]
            z = dot(rows, ht_ref[...])
            z0, z1 = z[:, :half], z[:, half:]
            p0 = jnp.exp(z0 - row_ref[0:1, :half])
            p1 = jnp.exp(z1 - row_ref[0:1, half:])
            gap = z0 - z1
            spot = lax.broadcasted_iota(jnp.int32, (end - start, half), 0)
            hit = spot == target_ref[0:1, :] - (base + start)
            picked = jnp.where(hit, row_ref[2:3, :half], 0.0)
            g0 = p0 * (row_ref[1:2, :half] + gap) - p1 - picked
            g1 = p1 * (row_ref[1:2, half:] - gap) - p0 - picked
            dz = jnp.concatenate([g0.astype(BF16), g1.astype(BF16)], axis=1)
            grad = (dot(dz, hn_ref[...]) + flat_ref[0:1, :]).astype(BF16)
            if n % 2:
                near_ref[n // 2, start:end, :] = grad
            else:
                fars[n // 2][start:end, :] = grad
            part = lax.dot_general(rows, dz, (((0,), (0,)), ((), ())), preferred_element_type=F32)
            acc_refs[0][...] = sources[0][...] + part[:, :half]
            acc_refs[1][...] = sources[1][...] + part[:, half:]
            sources = acc_refs
    if last:
        give_parts(flags_ref, [ref[...] for ref in acc_refs], *outs)


def second_sweep(flags, bases, words, ht, hn, row_stats, target, flat, accs, last):
    count = len(bases)
    far_shape = words[0].shape
    full = (accs[0].shape, F32)
    outs = call(
        functools.partial(second_sweep_kernel, bases, last),
        [(far_shape, BF16)] * count + [((count,) + far_shape, BF16), full, (accs[0].shape, BF16) if last else full],
        *(*words, ht, hn, row_stats, target, flat, *accs),
        scalars=flags,
        scratch=[full, full] if last else [],
    )
    return outs[:count], outs[count], outs[count + 1 :]


def gelu_parts(u):
    scale, cubic = 0.7978845608028654, 0.044715
    t = jnp.tanh(scale * (u + cubic * (u * u * u)))
    value = 0.5 * u * (1.0 + t)
    slope = 0.5 * (1.0 + t) + (0.5 * scale) * u * (1.0 - t * t) * (1.0 + (3.0 * cubic) * (u * u))
    return value, slope


def expert_rows(block_ref, which):
    return jnp.concatenate([block_ref[which, e] for e in range(block_ref.shape[1])], axis=0)


def expert_masks(route_ref, experts, hidden, tokens):
    names = lax.broadcasted_iota(jnp.int32, (experts * hidden, tokens), 0) // hidden
    return [names == route_ref[p : p + 1, :] for p in range(2)]


def give_parts(flags_ref, parts, mine_ref, theirs_ref):
    @pl.when(flags_ref[0] == 0)
    def _():
        mine_ref[...], theirs_ref[...] = parts[0], parts[1].astype(BF16)

    @pl.when(flags_ref[0] != 0)
    def _():
        mine_ref[...], theirs_ref[...] = parts[1], parts[0].astype(BF16)


def expert_forward_kernel(count, first, last, *refs):
    flags_ref, blocks, (a3_ref, route_ref) = refs[0], refs[1 : count + 1], refs[count + 1 : count + 3]
    ins, outs = refs[count + 3 : -2], refs[-2:]
    tokens = a3_ref.shape[1]
    accs = [0.0, 0.0] if first else [ref[...] for ref in ins]
    for block_ref in blocks:
        masks = expert_masks(route_ref, block_ref.shape[1], block_ref.shape[2], tokens)
        u = dot(expert_rows(block_ref, 0), a3_ref[...])
        g = gelu_parts(u)[0]
        w_out = expert_rows(block_ref, 1).T
        accs = [acc + dot(w_out, jnp.where(mask, g, 0.0).astype(BF16)) for acc, mask in zip(accs, masks)]
    if last:
        give_parts(flags_ref, accs, *outs)
    else:
        outs[0][...], outs[1][...] = accs


def expert_forward(flags, blocks, a3, route, accs, last):
    full = (a3.shape, F32)
    return call(
        functools.partial(expert_forward_kernel, len(blocks), not accs, last),
        [full, (a3.shape, BF16) if last else full],
        *(*blocks, a3, route, *accs),
        scalars=flags,
    )


def expert_backward_kernel(groups, flags_ref, *refs):
    blocks, rest = refs[: 2 * groups], refs[2 * groups :]
    a3_ref, an_ref, dy_ref, dn_ref, route_ref = rest[:5]
    fars, near_ref, mine_ref, theirs_ref, acc_ref = rest[5 : 5 + groups], *rest[5 + groups :]
    tokens = a3_ref.shape[1]
    for n, block_ref in enumerate(blocks):
        experts, hidden = block_ref.shape[1:3]
        masks = expert_masks(route_ref, experts, hidden, tokens)
        w_in = expert_rows(block_ref, 0)
        u = dot(w_in, a3_ref[...])
        g, slope = gelu_parts(u)
        d_act = dot(expert_rows(block_ref, 1), dy_ref[...])
        active = jnp.concatenate([jnp.where(mask, g, 0.0) for mask in masks], axis=1).astype(BF16)
        routed = jnp.where(masks[0], d_act[:, :tokens], 0.0) + jnp.where(masks[1], d_act[:, tokens:], 0.0)
        du = (routed * slope).astype(BF16)
        for matrix, grad in enumerate((dot(du, an_ref[...]), dot(active, dn_ref[...]))):
            grad = grad.astype(BF16)
            for e in range(experts):
                piece = grad[e * hidden : (e + 1) * hidden]
                if n % 2:
                    near_ref[n // 2, matrix, e] = piece
                else:
                    fars[n // 2][matrix, e] = piece
        part = dot(w_in.T, du)
        acc_ref[...] = part if n == 0 else acc_ref[...] + part
    half = tokens // 2
    give_parts(flags_ref, (acc_ref[:, :half], acc_ref[:, half:]), mine_ref, theirs_ref)


def expert_backward(flags, blocks, a3, a3_n, dy, dy_n, route):
    groups = len(blocks) // 2
    shape = blocks[0].shape
    half = (a3.shape[0], a3.shape[1] // 2)
    outs = call(
        functools.partial(expert_backward_kernel, groups),
        [(shape, BF16)] * groups + [((groups,) + shape, BF16), (half, F32), (half, BF16)],
        *(*blocks, a3, a3_n, dy, dy_n, route),
        scalars=flags,
        scratch=[(a3.shape, F32)],
    )
    return outs[:groups], outs[groups], outs[groups + 1 :]


def unpack_kernel(sizes, order_ref, mine_ref, twin_ref, *outs):
    count, half = mine_ref.shape[0], mine_ref.shape[1]

    def write(low_ref, high_ref):
        for j in range(count):
            source = order_ref[j]
            full = jnp.concatenate([low_ref[source], high_ref[source]], axis=0)
            start = 0
            for size, out in zip(sizes, outs):
                out[j * size : (j + 1) * size, :] = full[start : start + size]
                start += size

    pl.when(order_ref[count] == 0)(lambda: write(mine_ref, twin_ref))
    pl.when(order_ref[count] != 0)(lambda: write(twin_ref, mine_ref))


def unpack(mine, twin, order, core, sizes):
    count, half, width = mine.shape
    if any(size % 16 for size in sizes):
        low, high = jnp.where(core == 0, mine, twin), jnp.where(core == 0, twin, mine)
        full = jnp.concatenate([low, high], axis=1)[order]
        ends = [sum(sizes[: n + 1]) for n in range(len(sizes))]
        return [full[:, end - size : end].reshape(-1, width) for size, end in zip(sizes, ends)]
    return pl.pallas_call(
        functools.partial(unpack_kernel, sizes),
        in_specs=[pl.BlockSpec(memory_space=pltpu.SMEM)] + 2 * [pl.BlockSpec(memory_space=pltpu.VMEM)],
        out_specs=[pl.BlockSpec(memory_space=pltpu.VMEM)] * len(sizes),
        out_shape=[jax.ShapeDtypeStruct((count * size, width), mine.dtype) for size in sizes],
        compiler_params=PARAMS,
        cost_estimate=COST,
    )(jnp.concatenate([order, core[None]]).astype(jnp.int32), mine, twin)


def pack_kernel(sizes, order_ref, *refs):
    out_ref = refs[-1]
    count, half, width = out_ref.shape

    def write(core):
        for k in range(count):
            source = order_ref[k]
            start = -core * half
            for size, ref in zip(sizes, refs[:-1]):
                low, high = max(start, 0), min(start + size, half)
                if low < high:
                    rows = pl.ds(pl.multiple_of(source * size, 16) + (low - start), high - low)
                    out_ref[k, low:high, :] = ref[rows, :].astype(BF16)
                start += size
            low = max(start, 0)
            if low < half:
                out_ref[k, low:, :] = jnp.zeros((half - low, width), BF16)

    pl.when(order_ref[count] == 0)(lambda: write(0))
    pl.when(order_ref[count] != 0)(lambda: write(1))


def pack(grads, order, core, sizes, half):
    width = grads[0].shape[1]
    shards = grads[0].shape[0] // sizes[0]
    if any(size % 16 for size in sizes):
        full = jnp.concatenate([grad.reshape(shards, -1, width) for grad in grads], axis=1)
        full = jnp.pad(full, ((0, 0), (0, 2 * half - full.shape[1]), (0, 0)))[order].astype(BF16)
        return jnp.where(core == 0, full[:, :half], full[:, half:])
    return pl.pallas_call(
        functools.partial(pack_kernel, sizes),
        in_specs=[pl.BlockSpec(memory_space=pltpu.SMEM)]
        + len(grads) * [pl.BlockSpec(memory_space=pltpu.VMEM)],
        out_specs=pl.BlockSpec(memory_space=pltpu.VMEM),
        out_shape=jax.ShapeDtypeStruct((order.shape[0], half, width), BF16),
        compiler_params=PARAMS,
        cost_estimate=COST,
    )(jnp.concatenate([order, core[None]]).astype(jnp.int32), *grads)


def group_sum(mine, theirs):
    chip = (mine + swap(theirs, "vocab", 1).astype(F32)).astype(BF16)
    part = chip.astype(F32) + swap(chip, "pass", 1).astype(F32)
    half = part.shape[0] // 2
    return part, (swap(part[:half], "vocab", 1), swap(part[half:], "vocab", 1)), chip


def local(
    inputs,
    memory,
    expert_ids,
    targets,
    lengths,
    memory_mask,
    norm_gain,
    norm_bias,
    self_project,
    self_output,
    cross_query,
    memory_project,
    cross_output,
    expert_in,
    expert_out,
    embedding,
):
    seq_len, width = inputs.shape
    rows_axis = lax.axis_size("dp")
    here = lax.axis_index("dp")
    which = lax.axis_index("pass")
    core = lax.axis_index("vocab")
    shards = 2 * rows_axis

    sizes = [matrix.shape[1] for matrix in (self_project, self_output, cross_query, memory_project, cross_output)]
    norm_width = norm_gain.shape[1]
    norms = jnp.pad(jnp.concatenate([norm_gain, norm_bias], axis=0).T, ((0, 0), (0, width - 8)))
    sizes = (*sizes, norm_width)
    order = 2 * (jnp.arange(shards) // 2 ^ here) + (jnp.arange(shards) % 2 ^ which)

    def core_rows(matrices):
        rows = jnp.concatenate(matrices, axis=0)
        half = -(-rows.shape[0] // 32) * 16
        rows = jnp.pad(rows, ((0, 2 * half - rows.shape[0]), (0, 0)))
        return jnp.where(core == 0, rows[:half], rows[half:])

    mine = core_rows(
        [jnp.concatenate([self_project, self_output, cross_query, memory_project, cross_output], axis=1).T, norms]
    )
    pack_half = mine.shape[0]
    layer_gather = Gather(jnp.stack([mine, swap(mine, "pass", 1)]), "dp")
    layer_gather.send((1, 2, 3))
    layer_gather.forward((0, 1, 2, 3))
    mine = jnp.concatenate(layer_gather.result())
    project_t, self_output_t, cross_query_t, memory_project_t, cross_output_t, norms = unpack(
        mine, swap(mine, "vocab", 1), order, core, sizes
    )
    norms = norms[:, : min(width, 128)]
    flags = jnp.stack([core, which]).astype(jnp.int32)

    experts = expert_in.shape[0] // 2
    hidden = expert_in.shape[2]

    def core_half(weights):
        halves = weights.reshape(2, experts, width, hidden)
        return jnp.where(core == 0, halves[0], halves[1]).transpose(0, 2, 1)

    expert_block = jnp.stack([core_half(expert_in), core_half(expert_out)])
    expert_gather = Gather(expert_block, "dp")
    expert_gather.send((2, 1, 3), layer_gather.mark(3))
    expert_gather.forward((0,), project_t)
    word_gather = Gather(embedding, "dp")

    a1, qkv_t, attended_t, self_lse, h1, a2, cross_t = self_forward(
        inputs, norms, project_t, self_output_t, cross_query_t
    )
    cross_t = after(cross_t, expert_gather.arrived(near=(0,)))
    (memory_kv,) = call(
        memory_keys_kernel, [((memory.shape[0], 2 * width), BF16)], memory, memory_project_t
    )
    mem_bias = jnp.where(memory_mask[0][:, None] == 1, 0.0, -1e30).astype(F32)
    cross_att_t, cross_lse, h2, a3, a3_n = cross_forward(cross_t, memory_kv, mem_bias, h1, norms, cross_output_t)

    expert_gather.forward_together((2, 1, 3), a3)
    word_gather.send((2, 1, 3), (expert_gather.mark(3), a3))
    word_gather.forward((0,), expert_gather.arrived(near=(2,)))
    my_route = expert_ids[0, :, 0].astype(F32)[None, :]
    other_route = swap(my_route, "pass", 1)
    routes = jnp.concatenate([my_route, other_route] + [my_route] * 6, axis=0)
    routes = jnp.where(which == 0, routes, jnp.roll(routes, -1, axis=0).at[1].set(my_route[0]))
    route = (routes - (core * experts).astype(F32)).astype(jnp.int32)
    per_half = rows_axis // (2 * GROUPS)

    def halves(parts, axis):
        parts = [parts[n * per_half : (n + 1) * per_half] for n in range(2 * GROUPS)]
        return [part[0] if per_half == 1 else jnp.concatenate(part, axis=axis) for part in parts]

    expert_parts = halves(expert_gather.result(), 2)
    parts = ()
    for blocks in (expert_parts[:2], expert_parts[2:]):
        parts = expert_forward(flags, blocks, a3, route, parts, len(blocks) > 2)
    parts = after(parts, word_gather.arrived(far=(2, 1)))
    word_gather.forward((2, 1))
    y_part, y_other, mark = group_sum(*parts)
    word_gather.forward((3,), y_part)
    words = halves(word_gather.result(), 0)
    half_words = words[0].shape[0]

    valid = (jnp.arange(seq_len) < lengths[here]).astype(F32)
    half_weight = 0.5 * valid
    weight2 = jnp.concatenate([half_weight, half_weight])[None, :]
    block0, block1, final_t, final_n, block_out, flat_grad = final_norm(
        flags, h2, y_part, y_other, norms, jnp.broadcast_to(weight2, (8, 2 * seq_len)).astype(BF16)
    )
    shard_rows = embedding.shape[0]
    owner = targets // shard_rows
    in_quarter = (owner % 2 == core) & (owner // 2 % 2 == which)
    place = ((owner // 4) ^ here) * shard_rows + targets % shard_rows
    target = jnp.broadcast_to(jnp.where(in_quarter, place, -1)[None, :], (8, seq_len)).astype(jnp.int32)
    stats = jnp.concatenate(
        [jnp.full((1, 2 * seq_len), -1e30, F32), jnp.zeros((7, 2 * seq_len), F32)], axis=0
    )
    sums = jnp.zeros((8, width), F32)
    for g in (0, 2, 1, 3):
        stats, sums = first_sweep(
            2 * g * half_words, words[2 * g : 2 * g + 2], final_t, target, stats, sums
        )
    hits = stats[3, :seq_len]

    def merge(left, axis):
        right = swap(left, axis, 1)
        top = jnp.maximum(left[0:1], right[0:1])
        total = left[1:] * jnp.exp(left[0:1] - top) + right[1:] * jnp.exp(right[0:1] - top)
        return jnp.concatenate([top, total], axis=0)

    merged = merge(merge(stats, "vocab"), "pass")
    lse = merged[0:1] + jnp.log(merged[1:2])
    drift = merged[2:3] / merged[1:2]
    row_stats = jnp.concatenate(
        [
            jnp.where(weight2 > 0, lse + jnp.log(2.0), 1e30),
            2.0 - drift,
            (1.0 - SMOOTH) * weight2,
            jnp.zeros((5, 2 * seq_len), F32),
        ],
        axis=0,
    )
    accs = [(-SMOOTH / VOCAB) * sums[0][:, None] * half_weight[None, :]] * 2
    word_sum = ScatterSum("dp")
    loss = (
        0.25 * jnp.sum(weight2 * (lse + drift))
        - (1.0 - SMOOTH) * jnp.sum(half_weight * hits)
        + jnp.sum(flat_grad[0] * sums[0])
    )
    loss = jnp.broadcast_to(loss, (8, 128))
    first_loss = loss = loss + swap(loss, "dp", 1)
    step = 2
    while step < rows_axis:
        loss = loss + swap(loss, "dp", step)
        step *= 2
    for axis in ("vocab", "pass"):
        loss = loss + swap(loss, axis, 1)
    mean_loss = loss[0, 0] / jnp.sum(lengths).astype(F32)
    for groups in ((2,), (3, 1), (0,)):
        fars, nears, accs = second_sweep(
            flags,
            [2 * g * half_words for g in groups],
            [words[2 * g + n] for g in groups for n in range(2)],
            *(final_t, final_n, row_stats, target, flat_grad, accs, groups[0] == 0),
        )
        if groups[0]:
            word_sum.give(groups, fars, nears, mark=first_loss if groups[0] == 2 else None)
        if groups[0] == 3:
            accs = (after(accs[0], loss), accs[1])
    accs = after(accs, word_sum.arrived(near=(2,)))
    word_sum.forward((2,))

    dh_part, dh_other, mark = group_sum(*accs)
    db, dy, dy_n, cols = final_back(flags, block0, block1, dh_part, dh_other, norms)
    expert_sum = ScatterSum("dp")
    last_words = fars, nears
    *expert_grads, parts = expert_backward(flags, expert_parts, a3, a3_n, dy, dy_n, route)
    parts = after(parts, word_sum.arrived(far=(2,), near=(3, 1)))
    word_sum.forward((3, 1))
    expert_sum.give((0, 1, 2, 3), *expert_grads, 2)
    word_sum.give((0,), *last_words, mark=expert_sum.arrived(near=(0,)))
    da_part, da_other, mark = group_sum(*parts)

    dh1, cross_output_grad, cross_query_grad, pair_grad, cols = cross_back(
        flags,
        *(db, da_part, *da_other, h2, norms, cols, cross_output_t, cross_att_t, cross_t, memory_kv),
        *(cross_lse, mem_bias, a2, cross_query_t, h1),
    )
    dh1 = after(dh1, expert_sum.arrived(near=(0,)))
    expert_sum.forward((2, 3, 1, 0))
    memory_project_grad, memory_grad = call(
        memory_back_kernel,
        [((2 * width, width), BF16), (memory.shape, F32)],
        *(pair_grad, memory, memory_project_t),
    )
    self_output_grad, self_project_grad, inputs_grad, norm_grads = self_back(
        dh1, self_output_t, attended_t, qkv_t, self_lse, a1, inputs, project_t, norms, cols
    )
    self_project_grad = after(self_project_grad, word_sum.arrived(far=(3, 1)))
    evens = jnp.concatenate([jnp.arange(0, rows_axis, 2), jnp.arange(1, rows_axis, 2)])
    pack_order = 2 * ((evens if rows_axis == 8 else jnp.arange(rows_axis)) ^ here) + which
    blocks = pack(
        [self_project_grad, self_output_grad, cross_query_grad, memory_project_grad, cross_output_grad, norm_grads],
        pack_order,
        core,
        sizes,
        pack_half,
    )
    layer_sum = ScatterSum("dp")
    if rows_axis == 8:
        layer_sum.give((0, 1), [blocks[g] for g in range(2)], blocks[4:6])
        layer_sum.give((2, 3), [blocks[g] for g in range(2, 4)], blocks[6:])
        layer_sum.forward((2, 3, 1, 0), expert_sum.arrived(far=(2, 3, 1)))
        word_sum.forward((0,), expert_sum.arrived(far=(2, 3, 1)))
    else:
        layer_sum.blocks = {k: blocks[k] for k in range(rows_axis)}
    embedding_grad = word_sum.result()
    expert_grad = expert_sum.result()
    expert_twin = swap(expert_grad, "vocab", 1)
    expert_grad = jnp.concatenate(
        [
            jnp.where(core == 0, expert_grad, expert_twin),
            jnp.where(core == 0, expert_twin, expert_grad),
        ],
        axis=1,
    ).transpose(0, 1, 3, 2)
    layer_grad = layer_sum.result()
    twin = swap(layer_grad, "vocab", 1)
    layer_grad = jnp.concatenate(
        [jnp.where(core == 0, layer_grad, twin), jnp.where(core == 0, twin, layer_grad)], axis=0
    ).T
    ends = [sum(sizes[: n + 1]) for n in range(len(sizes))]
    layer_grads = [layer_grad[:, end - size : end] for size, end in zip(sizes, ends)]
    norm_out = layer_grads[5][:8]
    return (
        block_out[None],
        mean_loss,
        inputs_grad,
        memory_grad,
        norm_out[:4],
        norm_out[4:],
        *layer_grads[:5],
        expert_grad[0],
        expert_grad[1],
        embedding_grad,
    )


def solution(mesh):
    shared = P(None, ("dp", "pass"))
    placed = (
        P("dp", None),
        P("dp", None),
        P("pass", "dp", None),
        P("dp"),
        P(),
        P("dp", None),
        shared,
        shared,
        shared,
        shared,
        shared,
        shared,
        shared,
        P(None, None, ("dp", "pass")),
        P(None, None, ("dp", "pass")),
        P(("dp", "pass", "vocab"), None),
    )
    return jax.shard_map(
        local,
        mesh=mesh,
        in_specs=placed,
        out_specs=(
            P("pass", "dp", None),
            P(),
            P("dp", None),
            P("dp", None),
            shared,
            shared,
            shared,
            shared,
            shared,
            shared,
            shared,
            P(None, None, ("dp", "pass")),
            P(None, None, ("dp", "pass")),
            P(("dp", "pass", "vocab"), None),
        ),
        check_vma=False,
    )
```

```python
import functools

import jax
import jax.numpy as jnp
from jax import lax
from jax.experimental import pallas as pl
from jax.experimental.pallas import tpu as pltpu
from jax.sharding import PartitionSpec as P

HEADS = 8
VOCAB = 32000
GROUPS = 4
EPSILON = 1e-05
SMOOTH = 0.1
F32 = jnp.float32
BF16 = jnp.bfloat16
PARAMS = pltpu.CompilerParams(vmem_limit_bytes=56 * 1024 * 1024)
COST = pl.CostEstimate(flops=1000, bytes_accessed=1000, transcendentals=0)


def swap(block, axis, mask):
    count = lax.axis_size(axis)
    return lax.ppermute(block, axis, [(i, i ^ mask) for i in range(count)])


def after(value, mark):
    return value if mark is None else lax.optimization_barrier((value, mark))[0]


class Gather:
    def __init__(self, block, axis):
        self.block, self.axis, self.count = block, axis, lax.axis_size(axis)
        self.near, self.far = {}, {0: block}

    def send(self, steps, mark=None):
        if self.count == 8:
            block = after(self.block, mark)
            for g in steps:
                self.far[g] = swap(block, self.axis, 2 * g)

    def forward(self, steps, mark=None):
        if self.count == 8:
            for g in steps:
                self.near[g] = swap(after(self.far[g], mark), self.axis, 1)

    def forward_together(self, steps, mark=None):
        if self.count == 8:
            sent = swap(jnp.stack([after(self.far[g], mark) for g in steps]), self.axis, 1)
            for n, g in enumerate(steps):
                self.near[g] = sent[n]

    def arrived(self, far=(), near=()):
        return [self.far[g] for g in far] + [self.near[g] for g in near] if self.count == 8 else None

    def mark(self, g):
        return self.far[g] if self.count == 8 else None

    def result(self):
        if self.count == 8:
            return [part for g in range(4) for part in (self.far.get(g), self.near.get(g))]
        blocks, step = [self.block], 1
        while step < self.count:
            blocks = blocks + [swap(part, self.axis, step) for part in blocks]
            step *= 2
        return blocks


class ScatterSum:
    def __init__(self, axis):
        self.axis = axis
        self.count = lax.axis_size(axis)
        self.blocks, self.fars, self.near, self.step, self.sent, self.last = {}, {}, {}, None, None, None

    def give(self, groups, fars, nears, split=0, mark=None):
        per_half = self.count // (2 * GROUPS)
        if self.count == 8:
            if isinstance(nears, (list, tuple)):
                nears = [swap(after(near, mark), self.axis, 1) for near in nears]
                self.near.update({g: (near, None) for g, near in zip(groups, nears)})
            else:
                sent = swap(after(nears, mark), self.axis, 1)
                self.near.update({g: (sent, n) for n, g in enumerate(groups)})
            self.fars.update(dict(zip(groups, fars)))
            return
        for n, g in enumerate(groups):
            for half, array in enumerate((fars[n], nears[n])):
                for k, piece in enumerate(jnp.split(array, per_half, axis=split)):
                    self.blocks[(2 * g + half) * per_half + k] = piece

    def joined(self, g, mark=None):
        sent, n = self.near[g]
        sent = after(sent, mark)
        return self.fars[g].astype(F32) + (sent if n is None else sent[n]).astype(F32)

    def second(self, groups=None, mark=None):
        if self.count == 8:
            parts = [self.joined(g, mark).astype(BF16) for g in groups or (1, 3)]
            if groups:
                self.step = {**(self.step or {}), **{g: swap(part, self.axis, 2) for g, part in zip(groups, parts)}}
            else:
                self.sent = sent = swap(jnp.stack(parts), self.axis, 2)
                self.step = {1: sent[0], 3: sent[1]}

    def third(self, mark=None):
        if self.count == 8:
            step = after(self.step[3], mark)
            self.last = swap((self.joined(2) + step.astype(F32)).astype(BF16), self.axis, 4)

    def arrived(self, near=()):
        return [self.near[g][0] for g in near] if self.count == 8 else None

    def result(self, mark=None):
        if self.count == 8:
            last = after(self.last, mark)
            return self.joined(0) + self.step[1].astype(F32) + last.astype(F32)
        blocks = [self.blocks[k] for k in range(self.count)]
        step = self.count // 2
        while step >= 1:
            blocks = [
                blocks[k].astype(F32) + swap(blocks[k + step].astype(BF16), self.axis, step).astype(F32)
                for k in range(step)
            ]
            step //= 2
        return blocks[0]


def dot(left, right):
    return jnp.dot(left, right, preferred_element_type=F32)


def dot_nt(left, right):
    return lax.dot_general(left, right, (((1,), (1,)), ((), ())), preferred_element_type=F32)


def dot_tn(left, right):
    return lax.dot_general(left, right, (((0,), (0,)), ((), ())), preferred_element_type=F32)


def call(kernel, outs, *args, scalars=None, scratch=()):
    specs = [pl.BlockSpec(memory_space=pltpu.VMEM)] * len(args)
    if scalars is not None:
        specs = [pl.BlockSpec(memory_space=pltpu.SMEM)] + specs
        args = (scalars,) + args
    return pl.pallas_call(
        kernel,
        in_specs=specs,
        out_specs=[pl.BlockSpec(memory_space=pltpu.VMEM)] * len(outs),
        out_shape=[jax.ShapeDtypeStruct(shape, dtype) for shape, dtype in outs],
        scratch_shapes=[pltpu.VMEM(shape, dtype) for shape, dtype in scratch],
        compiler_params=PARAMS,
        cost_estimate=COST,
    )(*args)


def by_core(flag_ref, low_ref, high_ref, mine, other):
    @pl.when(flag_ref[0] == 0)
    def _():
        low_ref[...], high_ref[...] = mine, other

    @pl.when(flag_ref[0] != 0)
    def _():
        low_ref[...], high_ref[...] = other, mine


def pair_parts(value, h):
    head = value.shape[0] // 2
    rows = value[h * head : (h + 1) * head]
    zeros = jnp.zeros_like(rows)
    return rows, jnp.concatenate([zeros, rows] if h else [rows, zeros], axis=0)


def pair_rows(j, size, start=0):
    return pl.ds(pl.multiple_of(start + j * size, size), size)


def norm_forward(values, gain, bias):
    average = jnp.mean(values, axis=0, keepdims=True)
    centered = values - average
    scale = lax.rsqrt(jnp.mean(centered * centered, axis=0, keepdims=True) + EPSILON)
    return centered * scale * gain + bias


def norm_backward(values, gain, upstream):
    average = jnp.mean(values, axis=0, keepdims=True)
    centered = values - average
    scale = lax.rsqrt(jnp.mean(centered * centered, axis=0, keepdims=True) + EPSILON)
    unit = centered * scale
    grad = upstream * gain
    result = scale * (
        grad - jnp.mean(grad, axis=0, keepdims=True) - unit * jnp.mean(grad * unit, axis=0, keepdims=True)
    )
    return result, jnp.sum(upstream * unit, axis=1, keepdims=True), jnp.sum(upstream, axis=1, keepdims=True)


def norm_columns(j, gain_grad, bias_grad, width):
    lanes = lax.broadcasted_iota(jnp.int32, (gain_grad.shape[0], width), 1)
    return jnp.where(lanes == j, gain_grad, 0.0) + jnp.where(lanes == 4 + j, bias_grad, 0.0)


def column(norms_ref, j):
    return norms_ref[:, j : j + 1].astype(F32)


def causal_mask(tokens):
    shape = (tokens, tokens)
    return lax.broadcasted_iota(jnp.int32, shape, 0) <= lax.broadcasted_iota(jnp.int32, shape, 1)


def heads_forward(query, keys_n, value_t, masked, out_ref, lse_ref, j):
    head = query.shape[0] // 2
    for h in range(2):
        s = masked(dot(keys_n, pair_parts(query, h)[1]))
        m = jnp.max(s, axis=0, keepdims=True)
        e = jnp.exp(s - m)
        total = jnp.sum(e, axis=0, keepdims=True)
        p = (e * (1.0 / total)).astype(BF16)
        out_ref[pair_rows(2 * j + h, head), :] = dot(value_t[h * head : (h + 1) * head], p).astype(BF16)
        lse_ref[j, h : h + 1, :] = m + jnp.log(total)


def heads_backward(query, key_t, keys_n, values_n, upstream, lse, masked):
    head = query.shape[0] // 2
    dq, dk, dv = [], 0.0, 0.0
    for h in range(2):
        q_pad = pair_parts(query, h)[1]
        do_pad = pair_parts(upstream, h)[1]
        p = jnp.exp(masked(dot(keys_n, q_pad)) - lse[h : h + 1, :])
        pdp = p * dot(values_n, do_pad)
        total = jnp.sum(pdp, axis=0, keepdims=True)
        ds = (pdp - p * total).astype(BF16)
        dq.append(dot(pair_parts(key_t, h)[0], ds) * head**-0.5)
        dk = dk + dot(ds, q_pad.T)
        dv = dv + dot(p.astype(BF16), do_pad.T)
    return jnp.concatenate(dq, axis=0).astype(BF16), dk.astype(BF16), dv.astype(BF16)


def self_forward_kernel(
    x_ref, norms_ref, project_ref, output_ref, query_ref, a1_ref, qkv_ref, att_ref, lse_ref, h1_ref, a2_ref, cross_ref
):
    tokens, width = x_ref.shape
    pair = 2 * width // HEADS
    scale = jnp.asarray((pair // 2) ** -0.5, BF16)
    a1_ref[...] = norm_forward(x_ref[...].T.astype(F32), column(norms_ref, 0), column(norms_ref, 4)).astype(BF16)
    qkv_ref[...] = dot(project_ref[...], a1_ref[...]).astype(BF16)

    def step(j, carry):
        allowed = causal_mask(tokens)
        heads_forward(
            qkv_ref[pair_rows(j, pair), :] * scale,
            qkv_ref[pair_rows(j, pair, width), :].T,
            qkv_ref[pair_rows(j, pair, 2 * width), :],
            lambda s: jnp.where(allowed, s, -1e30),
            att_ref,
            lse_ref,
            j,
        )
        return carry

    lax.fori_loop(0, HEADS // 2, step, 0)
    h1_ref[...] = x_ref[...].T.astype(F32) + dot(output_ref[...], att_ref[...])
    a2_ref[...] = norm_forward(h1_ref[...], column(norms_ref, 1), column(norms_ref, 5)).astype(BF16)
    cross_ref[...] = dot(query_ref[...], a2_ref[...]).astype(BF16) * scale


def self_forward(x, norms, project, output, query):
    tokens, width = x.shape
    bf = ((width, tokens), BF16)
    return call(
        self_forward_kernel,
        [bf, ((3 * width, tokens), BF16), bf, ((HEADS // 2, 2, tokens), F32), ((width, tokens), F32), bf, bf],
        *(x, norms, project, output, query),
    )


def memory_keys_kernel(memory_ref, weight_ref, out_ref):
    out_ref[...] = dot_nt(memory_ref[...], weight_ref[...]).astype(BF16)


def cross_forward_kernel(
    cross_ref, kv_ref, bias_ref, h1_ref, norms_ref, output_ref, att_ref, lse_ref, h2_ref, a3_ref, an_ref
):
    width = cross_ref.shape[0]
    pair = 2 * width // HEADS

    def step(j, carry):
        heads_forward(
            cross_ref[pair_rows(j, pair), :],
            kv_ref[:, pair_rows(j, pair)],
            kv_ref[:, pair_rows(j, pair, width)].T,
            lambda s: s + bias_ref[...],
            att_ref,
            lse_ref,
            j,
        )
        return carry

    lax.fori_loop(0, HEADS // 2, step, 0)
    h2_ref[...] = h1_ref[...] + dot(output_ref[...], att_ref[...])
    a3_ref[...] = norm_forward(h2_ref[...], column(norms_ref, 2), column(norms_ref, 6)).astype(BF16)
    an_ref[...] = a3_ref[...].T


def cross_forward(cross, kv, bias, h1, norms, output):
    width, tokens = cross.shape
    bf = ((width, tokens), BF16)
    return call(
        cross_forward_kernel,
        [bf, ((HEADS // 2, 2, tokens), F32), ((width, tokens), F32), bf, ((tokens, width), BF16)],
        *(cross, kv, bias, h1, norms, output),
    )


def final_norm_kernel(
    flags_ref, h2_ref, part_ref, other_ref, last_ref, norms_ref, weight_ref, b0_ref, b1_ref, ft_ref, fn_ref, out_ref, flat_ref
):
    tokens = h2_ref.shape[1]
    other = jnp.concatenate([other_ref[...], last_ref[...]], axis=0)
    by_core(flags_ref, b0_ref, b1_ref, h2_ref[...] + part_ref[...], h2_ref[...] + other)
    for p, ref in enumerate((b0_ref, b1_ref)):
        final = norm_forward(ref[...], column(norms_ref, 3), column(norms_ref, 7)).astype(BF16)
        ft_ref[:, p * tokens : (p + 1) * tokens] = final
        fn_ref[p * tokens : (p + 1) * tokens, :] = final.T

        @pl.when(flags_ref[1] == p)
        def _():
            out_ref[...] = ref[...].T

    flat_ref[...] = dot(weight_ref[...], fn_ref[...]) * (-SMOOTH / VOCAB)


def final_norm(flags, h2, part, other, norms, weight):
    width, tokens = h2.shape
    full = ((width, tokens), F32)
    return call(
        final_norm_kernel,
        [full, full, ((width, 2 * tokens), BF16), ((2 * tokens, width), BF16), ((tokens, width), F32), ((8, width), F32)],
        *(h2, part, *other, norms, weight),
        scalars=flags,
    )


def final_back_kernel(
    flags_ref, b0_ref, b1_ref, part_ref, other_ref, last_ref, norms_ref, db_ref, dy_ref, dn_ref, cols_ref, d0_ref, d1_ref
):
    tokens = b0_ref.shape[1]
    other = jnp.concatenate([other_ref[...], last_ref[...]], axis=0)
    by_core(flags_ref, d0_ref, d1_ref, part_ref[...], other)
    total, cols = 0.0, 0.0
    for p, (block_ref, d_ref) in enumerate(((b0_ref, d0_ref), (b1_ref, d1_ref))):
        grad, *norm_grads = norm_backward(block_ref[...], column(norms_ref, 3), d_ref[...])
        low = grad.astype(BF16)
        dy_ref[:, p * tokens : (p + 1) * tokens] = low
        dn_ref[p * tokens : (p + 1) * tokens, :] = low.T
        total, cols = total + grad, cols + norm_columns(3, *norm_grads, cols_ref.shape[1])
    db_ref[...], cols_ref[...] = total, cols


def final_back(flags, b0, b1, part, other, norms):
    width, tokens = b0.shape
    full = ((width, tokens), F32)
    return call(
        final_back_kernel,
        [full, ((width, 2 * tokens), BF16), ((2 * tokens, width), BF16), ((width, norms.shape[1]), F32)],
        *(b0, b1, part, *other, norms),
        scalars=flags,
        scratch=[full, full],
    )


def cross_back_kernel(
    flags_ref,
    db_ref,
    mine_ref,
    other_ref,
    last_ref,
    h2_ref,
    norms_ref,
    cols_in_ref,
    output_ref,
    att_ref,
    cross_ref,
    kv_ref,
    lse_ref,
    bias_ref,
    a2_ref,
    query_ref,
    h1_ref,
    dh1_ref,
    out_grad_ref,
    query_grad_ref,
    dkv_ref,
    cols_ref,
    d_ref,
    do_ref,
    dq_ref,
):
    width, tokens = h2_ref.shape
    pair, half = 2 * width // HEADS, tokens // 2
    other = jnp.concatenate([other_ref[...], last_ref[...]], axis=0)
    by_core(flags_ref, d_ref.at[:, :half], d_ref.at[:, half:], mine_ref[...], other)
    grad, *two = norm_backward(h2_ref[...], column(norms_ref, 2), d_ref[...])
    d_ref[...] = db_ref[...] + grad
    low = d_ref[...].astype(BF16)
    out_grad_ref[...] = dot_nt(low, att_ref[...]).astype(BF16)
    do_ref[...] = dot_tn(output_ref[...], low).astype(BF16)

    def step(j, carry):
        rows, keys, values = pair_rows(j, pair), pair_rows(j, pair), pair_rows(j, pair, width)
        dq, dk, dv = heads_backward(
            cross_ref[rows, :],
            kv_ref[:, keys].T,
            kv_ref[:, keys],
            kv_ref[:, values],
            do_ref[rows, :],
            lse_ref[j],
            lambda s: s + bias_ref[...],
        )
        dq_ref[rows, :], dkv_ref[:, keys], dkv_ref[:, values] = dq, dk, dv
        return carry

    lax.fori_loop(0, HEADS // 2, step, 0)
    query_grad_ref[...] = dot_nt(dq_ref[...], a2_ref[...]).astype(BF16)
    grad, *one = norm_backward(h1_ref[...], column(norms_ref, 1), dot_tn(query_ref[...], dq_ref[...]))
    dh1_ref[...] = d_ref[...] + grad
    columns = cols_ref.shape[1]
    cols_ref[...] = cols_in_ref[...] + norm_columns(2, *two, columns) + norm_columns(1, *one, columns)


def cross_back(flags, *args):
    h2, norms, kv = args[4], args[5], args[10]
    width, tokens = h2.shape
    full, bf = ((width, tokens), F32), ((width, tokens), BF16)
    square = ((width, width), BF16)
    return call(
        cross_back_kernel,
        [full, square, square, (kv.shape, BF16), (norms.shape, F32)],
        *args,
        scalars=flags,
        scratch=[full, bf, bf],
    )


def memory_back_kernel(dkv_ref, memory_ref, weight_ref, weight_grad_ref, memory_grad_ref):
    weight_grad_ref[...] = dot_tn(dkv_ref[...], memory_ref[...]).astype(BF16)
    memory_grad_ref[...] = dot(dkv_ref[...], weight_ref[...])


def self_back_kernel(
    dh1_ref, output_ref, att_ref, qkv_ref, lse_ref, a1_ref, x_ref, project_ref, norms_ref, cols_ref,
    out_grad_ref, project_grad_ref, inputs_grad_ref, norm_grad_ref, do_ref, dqkv_ref
):
    width, tokens = dh1_ref.shape
    pair = 2 * width // HEADS
    scale = jnp.asarray((pair // 2) ** -0.5, BF16)
    low = dh1_ref[...].astype(BF16)
    out_grad_ref[...] = dot_nt(low, att_ref[...]).astype(BF16)
    do_ref[...] = dot_tn(output_ref[...], low).astype(BF16)

    def step(j, carry):
        allowed = causal_mask(tokens)
        rows, keys, values = pair_rows(j, pair), pair_rows(j, pair, width), pair_rows(j, pair, 2 * width)
        key_t = qkv_ref[keys, :]
        dq, dk, dv = heads_backward(
            qkv_ref[rows, :] * scale,
            key_t,
            key_t.T,
            qkv_ref[values, :].T,
            do_ref[rows, :],
            lse_ref[j],
            lambda s: jnp.where(allowed, s, -1e30),
        )
        dqkv_ref[rows, :], dqkv_ref[keys, :], dqkv_ref[values, :] = dq, dk.T, dv.T
        return carry

    lax.fori_loop(0, HEADS // 2, step, 0)
    project_grad_ref[...] = dot_nt(dqkv_ref[...], a1_ref[...]).astype(BF16)
    grad, *zero = norm_backward(
        x_ref[...].T.astype(F32), column(norms_ref, 0), dot_tn(project_ref[...], dqkv_ref[...])
    )
    inputs_grad_ref[...] = (dh1_ref[...] + grad).T
    columns = cols_ref.shape[1]
    norm_grad_ref[...] = jnp.zeros(norm_grad_ref.shape, BF16)
    norm_grad_ref[:, :columns] = (cols_ref[...] + norm_columns(0, *zero, columns)).astype(BF16)


def self_back(*args):
    width, tokens = args[0].shape
    square = ((width, width), BF16)
    return call(
        self_back_kernel,
        [square, ((3 * width, width), BF16), ((tokens, width), F32), square],
        *args,
        scratch=[((width, tokens), BF16), ((3 * width, tokens), BF16)],
    )


def row_blocks(rows):
    parts = -(-rows // 512)
    size = -(-rows // (16 * parts)) * 16
    return [(start, min(start + size, rows)) for start in range(0, rows, size)]


def first_sweep_kernel(base, count, *refs):
    words, rest = refs[:count], refs[count:]
    ht_ref, target_ref, stat_in_ref, sum_in_ref, stat_ref, sum_ref = rest
    half = ht_ref.shape[1] // 2
    top, mass, drift = stat_in_ref[0:1, :], stat_in_ref[1:2, :], stat_in_ref[2:3, :]
    hits = stat_in_ref[3:4, :half]
    sums = sum_in_ref[...]
    for word_ref in words:
        for start, end in row_blocks(word_ref.shape[0]):
            rows = word_ref[start:end, :]
            z = dot(rows, ht_ref[...])
            old, top = top, jnp.maximum(top, jnp.max(z, axis=0, keepdims=True))
            e = jnp.exp(z - top)
            z0, z1 = z[:, :half], z[:, half:]
            gap = z0 - z1
            moved = jnp.concatenate(
                [
                    jnp.sum(e[:, :half] * gap, axis=0, keepdims=True),
                    -jnp.sum(e[:, half:] * gap, axis=0, keepdims=True),
                ],
                axis=1,
            )
            spot = lax.broadcasted_iota(jnp.int32, (end - start, half), 0)
            hit = spot == target_ref[0:1, :] - (base + start)
            hits = hits + jnp.sum(jnp.where(hit, z0 + z1, 0.0), axis=0, keepdims=True)
            factor = jnp.exp(old - top)
            mass = mass * factor + jnp.sum(e, axis=0, keepdims=True)
            drift = drift * factor + moved
            sums = sums + dot(jnp.ones((8, end - start), BF16), rows)
        base += word_ref.shape[0]
    hits = jnp.concatenate([hits, jnp.zeros_like(hits)], axis=1)
    stat_ref[...] = jnp.concatenate([top, mass, drift, hits, jnp.zeros((4, 2 * half), F32)], axis=0)
    sum_ref[...] = sums


def first_sweep(base, words, ht, target, stats, sums):
    return call(
        functools.partial(first_sweep_kernel, base, len(words)),
        [(stats.shape, F32), (sums.shape, F32)],
        *(*words, ht, target, stats, sums),
    )


def merge_stats(left, right):
    top = jnp.maximum(left[0:1], right[0:1])
    total = left[1:] * jnp.exp(left[0:1] - top) + right[1:] * jnp.exp(right[0:1] - top)
    return jnp.concatenate([top, total], axis=0)


def stats_result(stats):
    return stats[0:1] + jnp.log(stats[1:2]), stats[2:3] / stats[1:2]


def second_sweep_kernel(bases, last, flags_ref, *refs):
    count = len(bases)
    words, rest = refs[: 2 * count], refs[2 * count :]
    ht_ref, hn_ref, left_ref, right_ref, weight_ref, target_ref, flat_ref, acc_in_refs = *rest[:7], rest[7:9]
    fars, nears, outs = rest[9 : 9 + count], rest[9 + count : 9 + 2 * count], rest[9 + 2 * count : 11 + 2 * count]
    acc_refs = rest[11 + 2 * count :] if last else outs
    lse, drift = stats_result(merge_stats(left_ref[...], right_ref[...]))
    weight = weight_ref[0:1, :]
    offset, slant = jnp.where(weight > 0, lse + 0.6931471805599453, 1e30), 2.0 - drift
    target_weight = (1.0 - SMOOTH) * weight[:, : weight.shape[1] // 2]
    half = ht_ref.shape[1] // 2
    sources = acc_in_refs
    for n, word_ref in enumerate(words):
        base = bases[n // 2] + (n % 2) * word_ref.shape[0]
        for start, end in row_blocks(word_ref.shape[0]):
            rows = word_ref[start:end, :]
            z = dot(rows, ht_ref[...])
            z0, z1 = z[:, :half], z[:, half:]
            p0 = jnp.exp(z0 - offset[:, :half])
            p1 = jnp.exp(z1 - offset[:, half:])
            gap = z0 - z1
            spot = lax.broadcasted_iota(jnp.int32, (end - start, half), 0)
            hit = spot == target_ref[0:1, :] - (base + start)
            picked = jnp.where(hit, target_weight, 0.0)
            g0 = p0 * (slant[:, :half] + gap) - p1 - picked
            g1 = p1 * (slant[:, half:] - gap) - p0 - picked
            dz = jnp.concatenate([g0.astype(BF16), g1.astype(BF16)], axis=1)
            grad = (dot(dz, hn_ref[...]) + flat_ref[0:1, :]).astype(BF16)
            (nears if n % 2 else fars)[n // 2][start:end, :] = grad
            part = lax.dot_general(rows, dz, (((0,), (0,)), ((), ())), preferred_element_type=F32)
            acc_refs[0][...] = sources[0][...] + part[:, :half]
            acc_refs[1][...] = sources[1][...] + part[:, half:]
            sources = acc_refs
    if last:
        give_parts(flags_ref, [ref[...] for ref in acc_refs], *outs)


def second_sweep(flags, bases, words, ht, hn, stats, weight, target, flat, accs, last):
    count = len(bases)
    far_shape = words[0].shape
    full = (accs[0].shape, F32)
    outs = call(
        functools.partial(second_sweep_kernel, bases, last),
        [(far_shape, BF16)] * (2 * count) + [full, (accs[0].shape, BF16) if last else full],
        *(*words, ht, hn, *stats, weight, target, flat, *accs),
        scalars=flags,
        scratch=[full, full] if last else [],
    )
    return outs[:count], outs[count : 2 * count], outs[2 * count :]


def gelu_parts(u):
    scale, cubic = 0.7978845608028654, 0.044715
    t = jnp.tanh(scale * (u + cubic * (u * u * u)))
    value = 0.5 * u * (1.0 + t)
    slope = 0.5 * (1.0 + t) + (0.5 * scale) * u * (1.0 - t * t) * (1.0 + (3.0 * cubic) * (u * u))
    return value, slope


def expert_rows(block_ref, which):
    return jnp.concatenate([block_ref[which, e] for e in range(block_ref.shape[1])], axis=0)


def expert_masks(route_ref, experts, hidden, tokens):
    names = lax.broadcasted_iota(jnp.int32, (experts * hidden, tokens), 0) // hidden
    return [names == route_ref[p : p + 1, :] for p in range(2)]


def give_parts(flags_ref, parts, mine_ref, theirs_ref):
    @pl.when(flags_ref[0] == 0)
    def _():
        mine_ref[...], theirs_ref[...] = parts[0], parts[1].astype(BF16)

    @pl.when(flags_ref[0] != 0)
    def _():
        mine_ref[...], theirs_ref[...] = parts[1], parts[0].astype(BF16)


def expert_forward_kernel(count, first, last, *refs):
    flags_ref, blocks, (a3_ref, route_ref) = refs[0], refs[1 : count + 1], refs[count + 1 : count + 3]
    ins, outs = refs[count + 3 : -2], refs[-2:]
    tokens = a3_ref.shape[1]
    accs = [0.0, 0.0] if first else [ref[...] for ref in ins]
    for block_ref in blocks:
        masks = expert_masks(route_ref, block_ref.shape[1], block_ref.shape[2], tokens)
        u = dot(expert_rows(block_ref, 0), a3_ref[...])
        g = gelu_parts(u)[0]
        w_out = expert_rows(block_ref, 1).T
        accs = [acc + dot(w_out, jnp.where(mask, g, 0.0).astype(BF16)) for acc, mask in zip(accs, masks)]
    if last:
        give_parts(flags_ref, accs, *outs)
    else:
        outs[0][...], outs[1][...] = accs


def expert_forward(flags, blocks, a3, route, accs, last):
    full = (a3.shape, F32)
    return call(
        functools.partial(expert_forward_kernel, len(blocks), not accs, last),
        [full, (a3.shape, BF16) if last else full],
        *(*blocks, a3, route, *accs),
        scalars=flags,
    )


def expert_backward_kernel(groups, flags_ref, *refs):
    blocks, rest = refs[: 2 * groups], refs[2 * groups :]
    a3_ref, an_ref, dy_ref, dn_ref, route_ref = rest[:5]
    fars, nears, (mine_ref, theirs_ref, acc_ref) = rest[5 : 5 + groups], rest[5 + groups : 7 + groups], rest[7 + groups :]
    tokens = a3_ref.shape[1]
    for n, block_ref in enumerate(blocks):
        experts, hidden = block_ref.shape[1:3]
        masks = expert_masks(route_ref, experts, hidden, tokens)
        w_in = expert_rows(block_ref, 0)
        u = dot(w_in, a3_ref[...])
        g, slope = gelu_parts(u)
        d_act = dot(expert_rows(block_ref, 1), dy_ref[...])
        active = jnp.concatenate([jnp.where(mask, g, 0.0) for mask in masks], axis=1).astype(BF16)
        routed = jnp.where(masks[0], d_act[:, :tokens], 0.0) + jnp.where(masks[1], d_act[:, tokens:], 0.0)
        du = (routed * slope).astype(BF16)
        for matrix, grad in enumerate((dot(du, an_ref[...]), dot(active, dn_ref[...]))):
            grad = grad.astype(BF16)
            for e in range(experts):
                piece = grad[e * hidden : (e + 1) * hidden]
                if n % 2:
                    nears[n // 2 % 2][n // 4, matrix, e] = piece
                else:
                    fars[n // 2][matrix, e] = piece
        part = dot(w_in.T, du)
        acc_ref[...] = part if n == 0 else acc_ref[...] + part
    half = tokens // 2
    give_parts(flags_ref, (acc_ref[:, :half], acc_ref[:, half:]), mine_ref, theirs_ref)


def expert_backward(flags, blocks, a3, a3_n, dy, dy_n, route):
    groups = len(blocks) // 2
    shape = blocks[0].shape
    half = (a3.shape[0], a3.shape[1] // 2)
    outs = call(
        functools.partial(expert_backward_kernel, groups),
        [(shape, BF16)] * groups + [((groups // 2,) + shape, BF16)] * 2 + [(half, F32), (half, BF16)],
        *(*blocks, a3, a3_n, dy, dy_n, route),
        scalars=flags,
        scratch=[(a3.shape, F32)],
    )
    return outs[:groups], outs[groups : groups + 2], outs[groups + 2 :]


def unpack_kernel(sizes, order_ref, mine_ref, twin_ref, *outs):
    count, half = mine_ref.shape[0], mine_ref.shape[1]

    def write(low_ref, high_ref):
        for j in range(count):
            source = order_ref[j]
            full = jnp.concatenate([low_ref[source], high_ref[source]], axis=0)
            start = 0
            for size, out in zip(sizes, outs):
                out[j * size : (j + 1) * size, :] = full[start : start + size]
                start += size

    pl.when(order_ref[count] == 0)(lambda: write(mine_ref, twin_ref))
    pl.when(order_ref[count] != 0)(lambda: write(twin_ref, mine_ref))


def unpack(mine, twin, order, core, sizes):
    count, half, width = mine.shape
    if any(size % 16 for size in sizes):
        low, high = jnp.where(core == 0, mine, twin), jnp.where(core == 0, twin, mine)
        full = jnp.concatenate([low, high], axis=1)[order]
        ends = [sum(sizes[: n + 1]) for n in range(len(sizes))]
        return [full[:, end - size : end].reshape(-1, width) for size, end in zip(sizes, ends)]
    return pl.pallas_call(
        functools.partial(unpack_kernel, sizes),
        in_specs=[pl.BlockSpec(memory_space=pltpu.SMEM)] + 2 * [pl.BlockSpec(memory_space=pltpu.VMEM)],
        out_specs=[pl.BlockSpec(memory_space=pltpu.VMEM)] * len(sizes),
        out_shape=[jax.ShapeDtypeStruct((count * size, width), mine.dtype) for size in sizes],
        compiler_params=PARAMS,
        cost_estimate=COST,
    )(jnp.concatenate([order, core[None]]).astype(jnp.int32), mine, twin)


def pack_kernel(sizes, order_ref, *refs):
    out_ref = refs[-1]
    count, half, width = out_ref.shape

    def write(core):
        for k in range(count):
            source = order_ref[k]
            start = -core * half
            for size, ref in zip(sizes, refs[:-1]):
                low, high = max(start, 0), min(start + size, half)
                if low < high:
                    rows = pl.ds(pl.multiple_of(source * size, 16) + (low - start), high - low)
                    out_ref[k, low:high, :] = ref[rows, :].astype(BF16)
                start += size
            low = max(start, 0)
            if low < half:
                out_ref[k, low:, :] = jnp.zeros((half - low, width), BF16)

    pl.when(order_ref[count] == 0)(lambda: write(0))
    pl.when(order_ref[count] != 0)(lambda: write(1))


def pack(grads, order, core, sizes, half):
    width = grads[0].shape[1]
    shards = grads[0].shape[0] // sizes[0]
    if any(size % 16 for size in sizes):
        full = jnp.concatenate([grad.reshape(shards, -1, width) for grad in grads], axis=1)
        full = jnp.pad(full, ((0, 0), (0, 2 * half - full.shape[1]), (0, 0)))[order].astype(BF16)
        return jnp.where(core == 0, full[:, :half], full[:, half:])
    return pl.pallas_call(
        functools.partial(pack_kernel, sizes),
        in_specs=[pl.BlockSpec(memory_space=pltpu.SMEM)]
        + len(grads) * [pl.BlockSpec(memory_space=pltpu.VMEM)],
        out_specs=pl.BlockSpec(memory_space=pltpu.VMEM),
        out_shape=jax.ShapeDtypeStruct((order.shape[0], half, width), BF16),
        compiler_params=PARAMS,
        cost_estimate=COST,
    )(jnp.concatenate([order, core[None]]).astype(jnp.int32), *grads)


def group_sum(mine, theirs):
    chip = (mine + swap(theirs, "vocab", 1).astype(F32)).astype(BF16)
    part = chip.astype(F32) + swap(chip, "pass", 1).astype(F32)
    half = part.shape[0] // 2
    return part, (swap(part[:half], "vocab", 1), swap(part[half:], "vocab", 1)), chip


def local(
    inputs,
    memory,
    expert_ids,
    targets,
    lengths,
    memory_mask,
    norm_gain,
    norm_bias,
    self_project,
    self_output,
    cross_query,
    memory_project,
    cross_output,
    expert_in,
    expert_out,
    embedding,
):
    seq_len, width = inputs.shape
    rows_axis = lax.axis_size("dp")
    here = lax.axis_index("dp")
    which = lax.axis_index("pass")
    core = lax.axis_index("vocab")
    shards = 2 * rows_axis

    sizes = [matrix.shape[1] for matrix in (self_project, self_output, cross_query, memory_project, cross_output)]
    norm_width = norm_gain.shape[1]
    norms = jnp.pad(jnp.concatenate([norm_gain, norm_bias], axis=0).T, ((0, 0), (0, width - 8)))
    sizes = (*sizes, norm_width)

    def core_rows(matrices):
        rows = jnp.concatenate(matrices, axis=0)
        half = -(-rows.shape[0] // 32) * 16
        rows = jnp.pad(rows, ((0, 2 * half - rows.shape[0]), (0, 0)))
        return jnp.where(core == 0, rows[:half], rows[half:])

    mine = core_rows(
        [jnp.concatenate([self_project, self_output, cross_query, memory_project, cross_output], axis=1).T, norms]
    )
    pack_half = mine.shape[0]
    experts = expert_in.shape[0] // 2
    hidden = expert_in.shape[2]

    def core_half(weights):
        halves = weights.reshape(2, experts, width, hidden)
        return jnp.where(core == 0, halves[0], halves[1]).transpose(0, 2, 1)

    expert_block = jnp.stack([core_half(expert_in), core_half(expert_out)])
    expert_gather = Gather(expert_block, "dp")
    layer_gather = Gather(mine, "dp")
    layer_gather.send((2, 3, 1))
    layer_gather.forward((0,))
    layer_gather.forward_together((1, 2, 3))
    expert_gather.forward((0,), layer_gather.arrived(far=(1, 2, 3)))
    parts = layer_gather.result()
    if rows_axis == 8:
        parts = parts[0::2] + parts[1::2]
        mine = [jnp.stack(parts[:4]), jnp.stack(parts[4:])]
        block_order = (0, 2, 4, 6, 1, 3, 5, 7)
    else:
        mine, block_order = [jnp.stack(parts)], range(rows_axis)
    mine = jnp.concatenate([array for part in mine for array in (part, swap(part, "pass", 1))])
    mine = after(mine, expert_gather.arrived(near=(0,)))
    position = {}
    for n, k in enumerate(block_order):
        part, place = divmod(n, 4) if rows_axis == 8 else (0, n)
        size = 4 if rows_axis == 8 else rows_axis
        position[k] = part * 2 * size + place, part * 2 * size + size + place
    where = jnp.array([position[k] for k in range(rows_axis)], jnp.int32)
    order = where[jnp.arange(shards) // 2 ^ here, jnp.arange(shards) % 2 ^ which]
    project_t, self_output_t, cross_query_t, memory_project_t, cross_output_t, norms = unpack(
        mine, swap(mine, "vocab", 1), order, core, sizes
    )
    norms = norms[:, : min(width, 128)]
    flags = jnp.stack([core, which]).astype(jnp.int32)

    expert_gather.send((2, 1, 3), layer_gather.mark(3))
    word_gather = Gather(embedding, "dp")
    word_gather.forward((0,), expert_gather.arrived(near=(0,)))

    a1, qkv_t, attended_t, self_lse, h1, a2, cross_t = self_forward(
        inputs, norms, project_t, self_output_t, cross_query_t
    )
    (memory_kv,) = call(
        memory_keys_kernel, [((memory.shape[0], 2 * width), BF16)], memory, memory_project_t
    )
    mem_bias = jnp.where(memory_mask[0][:, None] == 1, 0.0, -1e30).astype(F32)
    cross_att_t, cross_lse, h2, a3, a3_n = cross_forward(cross_t, memory_kv, mem_bias, h1, norms, cross_output_t)
    expert_gather.forward_together((2, 1, 3), (a3, word_gather.arrived(near=(0,))))
    word_gather.send((2, 1), (expert_gather.arrived(far=(1, 2, 3)), a3))

    my_route = expert_ids[0, :, 0].astype(F32)[None, :]
    other_route = swap(my_route, "pass", 1)
    routes = jnp.concatenate([my_route, other_route] + [my_route] * 6, axis=0)
    routes = jnp.where(which == 0, routes, jnp.roll(routes, -1, axis=0).at[1].set(my_route[0]))
    route = (routes - (core * experts).astype(F32)).astype(jnp.int32)
    per_half = rows_axis // (2 * GROUPS)

    def halves(parts, axis):
        parts = [parts[n * per_half : (n + 1) * per_half] for n in range(2 * GROUPS)]
        return [part[0] if per_half == 1 else jnp.concatenate(part, axis=axis) for part in parts]

    expert_parts = halves(expert_gather.result(), 2)
    parts = ()
    for place in (0, 1):
        parts = expert_forward(flags, expert_parts[place::2], a3, route, parts, place == 1)
    parts = after(parts, word_gather.arrived(far=(2, 1)))
    word_gather.forward((2, 1))
    y_part, y_other, mark = group_sum(*parts)
    word_gather.send((3,), word_gather.arrived(far=(2, 1)))
    half_words = embedding.shape[0] * per_half

    valid = (jnp.arange(seq_len) < lengths[here]).astype(F32)
    half_weight = 0.5 * valid
    weight2 = jnp.concatenate([half_weight, half_weight])[None, :]
    block0, block1, final_t, final_n, block_out, flat_grad = final_norm(
        flags, h2, y_part, y_other, norms, jnp.broadcast_to(weight2, (8, 2 * seq_len)).astype(BF16)
    )
    shard_rows = embedding.shape[0]
    owner = targets // shard_rows
    in_quarter = (owner % 2 == core) & (owner // 2 % 2 == which)
    place = ((owner // 4) ^ here) * shard_rows + targets % shard_rows
    target = jnp.broadcast_to(jnp.where(in_quarter, place, -1)[None, :], (8, seq_len)).astype(jnp.int32)
    stats = jnp.concatenate(
        [jnp.full((1, 2 * seq_len), -1e30, F32), jnp.zeros((7, 2 * seq_len), F32)], axis=0
    )
    sums = jnp.zeros((8, width), F32)
    for g in (0, 2, 1, 3):
        if g == 1:
            word_gather.forward((3,), stats)
        words = halves(word_gather.result(), 0)
        stats, sums = first_sweep(
            2 * g * half_words, words[2 * g : 2 * g + 2], final_t, target, stats, sums
        )
    hits = stats[3, :seq_len]

    stats = merge_stats(stats, swap(stats, "vocab", 1))
    stats = stats, swap(stats, "pass", 1)
    lse, drift = stats_result(merge_stats(*stats))
    weight8 = jnp.broadcast_to(weight2, (8, 2 * seq_len))
    accs = [(-SMOOTH / VOCAB) * sums[0][:, None] * half_weight[None, :]] * 2
    word_sum = ScatterSum("dp")
    loss = (
        0.25 * jnp.sum(weight2 * (lse + drift))
        - (1.0 - SMOOTH) * jnp.sum(half_weight * hits)
        + jnp.sum(flat_grad[0] * sums[0])
    )
    loss = jnp.broadcast_to(loss, (8, 128))
    loss_mark = loss
    if rows_axis == 8:
        stack = jnp.stack([loss] + [swap(loss, "dp", 2 * g) for g in (1, 2, 3)])
        loss = sum(lax.dynamic_index_in_dim(stack, here // 2 ^ z, 0, False) for z in range(4))
        loss_mark = loss
        loss = loss + swap(loss, "dp", 1)
    step = 1
    while rows_axis != 8 and step < rows_axis:
        loss = loss + swap(loss, "dp", step)
        step *= 2
    loss_end = loss
    for axis in ("vocab", "pass"):
        loss = loss + swap(loss, axis, 1)
    mean_loss = loss[0, 0] / jnp.sum(lengths).astype(F32)
    for groups in ((3,), (1, 2, 0)):
        fars, nears, accs = second_sweep(
            flags,
            [2 * g * half_words for g in groups],
            [words[2 * g + n] for g in groups for n in range(2)],
            *(final_t, final_n, stats, weight8, target, flat_grad, accs, groups[-1] == 0),
        )
        if groups[-1]:
            word_sum.give(groups, fars, nears, mark=loss_mark)
    word_sum.give((2, 1), fars[1::-1], nears[1::-1])
    accs = after(accs, (word_sum.arrived(near=(3,)), loss_end))
    word_sum.second((3,))

    dh_part, dh_other, mark = group_sum(*accs)
    db, dy, dy_n, cols = final_back(flags, block0, block1, dh_part, dh_other, norms)
    expert_sum = ScatterSum("dp")
    last_words = fars, nears
    *expert_grads, parts = expert_backward(flags, expert_parts, a3, a3_n, dy, dy_n, route)
    mark = (word_sum.arrived(near=(2,)), word_sum.step)
    word_sum.second((1,), parts)
    for start in (1, 0):
        expert_sum.give((start, start + 2), expert_grads[0][start::2], expert_grads[1][start], 2, mark)
    da_part, da_other, mark = group_sum(*parts)
    word_sum.third(parts)

    dh1, cross_output_grad, cross_query_grad, pair_grad, cols = cross_back(
        flags,
        *(db, da_part, *da_other, h2, norms, cols, cross_output_t, cross_att_t, cross_t, memory_kv),
        *(cross_lse, mem_bias, a2, cross_query_t, h1),
    )
    memory_project_grad, memory_grad = call(
        memory_back_kernel,
        [((2 * width, width), BF16), (memory.shape, F32)],
        *(pair_grad, memory, memory_project_t),
    )
    self_output_grad, self_project_grad, inputs_grad, norm_grads = self_back(
        dh1, self_output_t, attended_t, qkv_t, self_lse, a1, inputs, project_t, norms, cols
    )
    expert_sum.second(None, (inputs_grad, word_sum.step, word_sum.last))
    expert_sum.third()
    evens = jnp.concatenate([jnp.arange(0, rows_axis, 2), jnp.arange(1, rows_axis, 2)])
    pack_order = 2 * ((evens if rows_axis == 8 else jnp.arange(rows_axis)) ^ here) + which
    blocks = pack(
        [self_project_grad, self_output_grad, cross_query_grad, memory_project_grad, cross_output_grad, norm_grads],
        pack_order,
        core,
        sizes,
        pack_half,
    )
    layer_sum = ScatterSum("dp")
    if rows_axis == 8:
        layer_sum.give((0, 1, 2, 3), [blocks[g] for g in range(4)], blocks[4:])
        layer_sum.second()
        word_sum.give((0,), last_words[0][2:], last_words[1][2:], mark=layer_sum.arrived(near=(0,)))
        layer_sum.third((expert_sum.last, word_sum.arrived(near=(0,))))
    else:
        layer_sum.blocks = {k: blocks[k] for k in range(rows_axis)}
    if rows_axis != 8:
        word_sum.give((0,), last_words[0][2:], last_words[1][2:])
    embedding_grad = word_sum.result()
    expert_grad = expert_sum.result()
    expert_twin = swap(expert_grad, "vocab", 1)
    expert_grad = jnp.concatenate(
        [
            jnp.where(core == 0, expert_grad, expert_twin),
            jnp.where(core == 0, expert_twin, expert_grad),
        ],
        axis=1,
    ).transpose(0, 1, 3, 2)
    layer_grad = layer_sum.result()
    twin = swap(layer_grad, "vocab", 1)
    layer_grad = jnp.concatenate(
        [jnp.where(core == 0, layer_grad, twin), jnp.where(core == 0, twin, layer_grad)], axis=0
    ).T
    ends = [sum(sizes[: n + 1]) for n in range(len(sizes))]
    layer_grads = [layer_grad[:, end - size : end] for size, end in zip(sizes, ends)]
    norm_out = layer_grads[5][:8]
    return (
        block_out[None],
        mean_loss,
        inputs_grad,
        memory_grad,
        norm_out[:4],
        norm_out[4:],
        *layer_grads[:5],
        expert_grad[0],
        expert_grad[1],
        embedding_grad,
    )


def solution(mesh):
    shared = P(None, ("dp", "pass"))
    placed = (
        P("dp", None),
        P("dp", None),
        P("pass", "dp", None),
        P("dp"),
        P(),
        P("dp", None),
        shared,
        shared,
        shared,
        shared,
        shared,
        shared,
        shared,
        P(None, None, ("dp", "pass")),
        P(None, None, ("dp", "pass")),
        P(("dp", "pass", "vocab"), None),
    )
    return jax.shard_map(
        local,
        mesh=mesh,
        in_specs=placed,
        out_specs=(
            P("pass", "dp", None),
            P(),
            P("dp", None),
            P("dp", None),
            shared,
            shared,
            shared,
            shared,
            shared,
            shared,
            shared,
            P(None, None, ("dp", "pass")),
            P(None, None, ("dp", "pass")),
            P(("dp", "pass", "vocab"), None),
        ),
        check_vma=False,
    )
```

```python
import functools

import jax
import jax.numpy as jnp
from jax import lax
from jax.experimental import pallas as pl
from jax.experimental.pallas import tpu as pltpu
from jax.sharding import PartitionSpec as P

HEADS = 8
VOCAB = 32000
GROUPS = 4
EPSILON = 1e-05
SMOOTH = 0.1
F32 = jnp.float32
BF16 = jnp.bfloat16
PARAMS = pltpu.CompilerParams(vmem_limit_bytes=56 * 1024 * 1024)
COST = pl.CostEstimate(flops=1000, bytes_accessed=1000, transcendentals=0)


def swap(block, axis, mask):
    count = lax.axis_size(axis)
    return lax.ppermute(block, axis, [(i, i ^ mask) for i in range(count)])


def after(value, mark):
    return value if mark is None else lax.optimization_barrier((value, mark))[0]


class Gather:
    def __init__(self, block, axis):
        self.block, self.axis, self.count = block, axis, lax.axis_size(axis)
        self.near, self.far = {}, {0: block}

    def send(self, steps, mark=None):
        if self.count == 8:
            block = after(self.block, mark)
            for g in steps:
                self.far[g] = swap(block, self.axis, 2 * g)

    def forward(self, steps, mark=None):
        if self.count == 8:
            for g in steps:
                self.near[g] = swap(after(self.far[g], mark), self.axis, 1)

    def forward_together(self, steps, mark=None):
        if self.count == 8:
            sent = swap(jnp.stack([after(self.far[g], mark) for g in steps]), self.axis, 1)
            for n, g in enumerate(steps):
                self.near[g] = sent[n]

    def relay(self, mark=None):
        if self.count == 8:
            self.far[3] = swap(after(self.far[2], mark), self.axis, 2)

    def arrived(self, far=(), near=()):
        return [self.far[g] for g in far] + [self.near[g] for g in near] if self.count == 8 else None

    def mark(self, g):
        return self.far[g] if self.count == 8 else None

    def result(self):
        if self.count == 8:
            return [part for g in range(4) for part in (self.far.get(g), self.near.get(g))]
        blocks, step = [self.block], 1
        while step < self.count:
            blocks = blocks + [swap(part, self.axis, step) for part in blocks]
            step *= 2
        return blocks


class ScatterSum:
    def __init__(self, axis):
        self.axis = axis
        self.count = lax.axis_size(axis)
        self.blocks, self.fars, self.near, self.step, self.sent, self.last = {}, {}, {}, None, None, None

    def give(self, groups, fars, nears, split=0, mark=None):
        per_half = self.count // (2 * GROUPS)
        if self.count == 8:
            if isinstance(nears, (list, tuple)):
                nears = [swap(after(near, mark), self.axis, 1) for near in nears]
                self.near.update({g: (near, None) for g, near in zip(groups, nears)})
            else:
                sent = swap(after(nears, mark), self.axis, 1)
                self.near.update({g: (sent, n) for n, g in enumerate(groups)})
            self.fars.update(dict(zip(groups, fars)))
            return
        for n, g in enumerate(groups):
            for half, array in enumerate((fars[n], nears[n])):
                for k, piece in enumerate(jnp.split(array, per_half, axis=split)):
                    self.blocks[(2 * g + half) * per_half + k] = piece

    def joined(self, g, mark=None):
        sent, n = self.near[g]
        sent = after(sent, mark)
        return self.fars[g].astype(F32) + (sent if n is None else sent[n]).astype(F32)

    def second(self, groups=None, mark=None):
        if self.count == 8:
            parts = [self.joined(g, mark).astype(BF16) for g in groups or (1, 3)]
            if groups:
                self.step = {**(self.step or {}), **{g: swap(part, self.axis, 2) for g, part in zip(groups, parts)}}
            else:
                self.sent = sent = swap(jnp.stack(parts), self.axis, 2)
                self.step = {1: sent[0], 3: sent[1]}

    def third(self, mark=None):
        if self.count == 8:
            step = after(self.step[3], mark)
            self.last = swap((self.joined(2) + step.astype(F32)).astype(BF16), self.axis, 4)

    def arrived(self, near=()):
        return [self.near[g][0] for g in near] if self.count == 8 else None

    def result(self, mark=None):
        if self.count == 8:
            last = after(self.last, mark)
            return self.joined(0) + self.step[1].astype(F32) + last.astype(F32)
        blocks = [self.blocks[k] for k in range(self.count)]
        step = self.count // 2
        while step >= 1:
            blocks = [
                blocks[k].astype(F32) + swap(blocks[k + step].astype(BF16), self.axis, step).astype(F32)
                for k in range(step)
            ]
            step //= 2
        return blocks[0]


def dot(left, right):
    return jnp.dot(left, right, preferred_element_type=F32)


def dot_nt(left, right):
    return lax.dot_general(left, right, (((1,), (1,)), ((), ())), preferred_element_type=F32)


def dot_tn(left, right):
    return lax.dot_general(left, right, (((0,), (0,)), ((), ())), preferred_element_type=F32)


def call(kernel, outs, *args, scalars=None, scratch=()):
    specs = [pl.BlockSpec(memory_space=pltpu.VMEM)] * len(args)
    if scalars is not None:
        specs = [pl.BlockSpec(memory_space=pltpu.SMEM)] + specs
        args = (scalars,) + args
    return pl.pallas_call(
        kernel,
        in_specs=specs,
        out_specs=[pl.BlockSpec(memory_space=pltpu.VMEM)] * len(outs),
        out_shape=[jax.ShapeDtypeStruct(shape, dtype) for shape, dtype in outs],
        scratch_shapes=[pltpu.VMEM(shape, dtype) for shape, dtype in scratch],
        compiler_params=PARAMS,
        cost_estimate=COST,
    )(*args)


def by_core(flag_ref, low_ref, high_ref, mine, other):
    @pl.when(flag_ref[0] == 0)
    def _():
        low_ref[...], high_ref[...] = mine, other

    @pl.when(flag_ref[0] != 0)
    def _():
        low_ref[...], high_ref[...] = other, mine


def pair_parts(value, h):
    head = value.shape[0] // 2
    rows = value[h * head : (h + 1) * head]
    zeros = jnp.zeros_like(rows)
    return rows, jnp.concatenate([zeros, rows] if h else [rows, zeros], axis=0)


def pair_rows(j, size, start=0):
    return pl.ds(pl.multiple_of(start + j * size, size), size)


def norm_forward(values, gain, bias):
    average = jnp.mean(values, axis=0, keepdims=True)
    centered = values - average
    scale = lax.rsqrt(jnp.mean(centered * centered, axis=0, keepdims=True) + EPSILON)
    return centered * scale * gain + bias


def norm_backward(values, gain, upstream):
    average = jnp.mean(values, axis=0, keepdims=True)
    centered = values - average
    scale = lax.rsqrt(jnp.mean(centered * centered, axis=0, keepdims=True) + EPSILON)
    unit = centered * scale
    grad = upstream * gain
    result = scale * (
        grad - jnp.mean(grad, axis=0, keepdims=True) - unit * jnp.mean(grad * unit, axis=0, keepdims=True)
    )
    return result, jnp.sum(upstream * unit, axis=1, keepdims=True), jnp.sum(upstream, axis=1, keepdims=True)


def norm_columns(j, gain_grad, bias_grad, width):
    lanes = lax.broadcasted_iota(jnp.int32, (gain_grad.shape[0], width), 1)
    return jnp.where(lanes == j, gain_grad, 0.0) + jnp.where(lanes == 4 + j, bias_grad, 0.0)


def column(norms_ref, j):
    return norms_ref[:, j : j + 1].astype(F32)


def causal_mask(tokens):
    shape = (tokens, tokens)
    return lax.broadcasted_iota(jnp.int32, shape, 0) <= lax.broadcasted_iota(jnp.int32, shape, 1)


def heads_forward(query, keys_n, value_t, masked, out_ref, lse_ref, j):
    head = query.shape[0] // 2
    for h in range(2):
        s = masked(dot(keys_n, pair_parts(query, h)[1]))
        m = jnp.max(s, axis=0, keepdims=True)
        e = jnp.exp(s - m)
        total = jnp.sum(e, axis=0, keepdims=True)
        p = (e * (1.0 / total)).astype(BF16)
        out_ref[pair_rows(2 * j + h, head), :] = dot(value_t[h * head : (h + 1) * head], p).astype(BF16)
        lse_ref[j, h : h + 1, :] = m + jnp.log(total)


def heads_backward(query, key_t, keys_n, values_n, upstream, lse, masked):
    head = query.shape[0] // 2
    dq, dk, dv = [], 0.0, 0.0
    for h in range(2):
        q_pad = pair_parts(query, h)[1]
        do_pad = pair_parts(upstream, h)[1]
        p = jnp.exp(masked(dot(keys_n, q_pad)) - lse[h : h + 1, :])
        pdp = p * dot(values_n, do_pad)
        total = jnp.sum(pdp, axis=0, keepdims=True)
        ds = (pdp - p * total).astype(BF16)
        dq.append(dot(pair_parts(key_t, h)[0], ds) * head**-0.5)
        dk = dk + dot(ds, q_pad.T)
        dv = dv + dot(p.astype(BF16), do_pad.T)
    return jnp.concatenate(dq, axis=0).astype(BF16), dk.astype(BF16), dv.astype(BF16)


def self_forward_kernel(
    x_ref, norms_ref, project_ref, output_ref, query_ref, a1_ref, qkv_ref, att_ref, lse_ref, h1_ref, a2_ref, cross_ref
):
    tokens, width = x_ref.shape
    pair = 2 * width // HEADS
    scale = jnp.asarray((pair // 2) ** -0.5, BF16)
    a1_ref[...] = norm_forward(x_ref[...].T.astype(F32), column(norms_ref, 0), column(norms_ref, 4)).astype(BF16)
    qkv_ref[...] = dot(project_ref[...], a1_ref[...]).astype(BF16)

    def step(j, carry):
        allowed = causal_mask(tokens)
        heads_forward(
            qkv_ref[pair_rows(j, pair), :] * scale,
            qkv_ref[pair_rows(j, pair, width), :].T,
            qkv_ref[pair_rows(j, pair, 2 * width), :],
            lambda s: jnp.where(allowed, s, -1e30),
            att_ref,
            lse_ref,
            j,
        )
        return carry

    lax.fori_loop(0, HEADS // 2, step, 0)
    h1_ref[...] = x_ref[...].T.astype(F32) + dot(output_ref[...], att_ref[...])
    a2_ref[...] = norm_forward(h1_ref[...], column(norms_ref, 1), column(norms_ref, 5)).astype(BF16)
    cross_ref[...] = dot(query_ref[...], a2_ref[...]).astype(BF16) * scale


def self_forward(x, norms, project, output, query):
    tokens, width = x.shape
    bf = ((width, tokens), BF16)
    return call(
        self_forward_kernel,
        [bf, ((3 * width, tokens), BF16), bf, ((HEADS // 2, 2, tokens), F32), ((width, tokens), F32), bf, bf],
        *(x, norms, project, output, query),
    )


def memory_keys_kernel(memory_ref, weight_ref, out_ref):
    out_ref[...] = dot_nt(memory_ref[...], weight_ref[...]).astype(BF16)


def cross_forward_kernel(
    cross_ref, kv_ref, bias_ref, h1_ref, norms_ref, output_ref, att_ref, lse_ref, h2_ref, a3_ref, an_ref
):
    width = cross_ref.shape[0]
    pair = 2 * width // HEADS

    def step(j, carry):
        heads_forward(
            cross_ref[pair_rows(j, pair), :],
            kv_ref[:, pair_rows(j, pair)],
            kv_ref[:, pair_rows(j, pair, width)].T,
            lambda s: s + bias_ref[...],
            att_ref,
            lse_ref,
            j,
        )
        return carry

    lax.fori_loop(0, HEADS // 2, step, 0)
    h2_ref[...] = h1_ref[...] + dot(output_ref[...], att_ref[...])
    a3_ref[...] = norm_forward(h2_ref[...], column(norms_ref, 2), column(norms_ref, 6)).astype(BF16)
    an_ref[...] = a3_ref[...].T


def cross_forward(cross, kv, bias, h1, norms, output):
    width, tokens = cross.shape
    bf = ((width, tokens), BF16)
    return call(
        cross_forward_kernel,
        [bf, ((HEADS // 2, 2, tokens), F32), ((width, tokens), F32), bf, ((tokens, width), BF16)],
        *(cross, kv, bias, h1, norms, output),
    )


def final_norm_kernel(
    flags_ref, h2_ref, part_ref, other_ref, last_ref, norms_ref, weight_ref, b0_ref, b1_ref, ft_ref, fn_ref, out_ref, flat_ref
):
    tokens = h2_ref.shape[1]
    other = jnp.concatenate([other_ref[...], last_ref[...]], axis=0)
    by_core(flags_ref, b0_ref, b1_ref, h2_ref[...] + part_ref[...], h2_ref[...] + other)
    for p, ref in enumerate((b0_ref, b1_ref)):
        final = norm_forward(ref[...], column(norms_ref, 3), column(norms_ref, 7)).astype(BF16)
        ft_ref[:, p * tokens : (p + 1) * tokens] = final
        fn_ref[p * tokens : (p + 1) * tokens, :] = final.T

        @pl.when(flags_ref[1] == p)
        def _():
            out_ref[...] = ref[...].T

    flat_ref[...] = dot(weight_ref[...], fn_ref[...]) * (-SMOOTH / VOCAB)


def final_norm(flags, h2, part, other, norms, weight):
    width, tokens = h2.shape
    full = ((width, tokens), F32)
    return call(
        final_norm_kernel,
        [full, full, ((width, 2 * tokens), BF16), ((2 * tokens, width), BF16), ((tokens, width), F32), ((8, width), F32)],
        *(h2, part, *other, norms, weight),
        scalars=flags,
    )


def final_back_kernel(
    flags_ref, b0_ref, b1_ref, part_ref, other_ref, last_ref, norms_ref, db_ref, dy_ref, dn_ref, cols_ref, d0_ref, d1_ref
):
    tokens = b0_ref.shape[1]
    other = jnp.concatenate([other_ref[...], last_ref[...]], axis=0)
    by_core(flags_ref, d0_ref, d1_ref, part_ref[...], other)
    total, cols = 0.0, 0.0
    for p, (block_ref, d_ref) in enumerate(((b0_ref, d0_ref), (b1_ref, d1_ref))):
        grad, *norm_grads = norm_backward(block_ref[...], column(norms_ref, 3), d_ref[...])
        low = grad.astype(BF16)
        dy_ref[:, p * tokens : (p + 1) * tokens] = low
        dn_ref[p * tokens : (p + 1) * tokens, :] = low.T
        total, cols = total + grad, cols + norm_columns(3, *norm_grads, cols_ref.shape[1])
    db_ref[...], cols_ref[...] = total, cols


def final_back(flags, b0, b1, part, other, norms):
    width, tokens = b0.shape
    full = ((width, tokens), F32)
    return call(
        final_back_kernel,
        [full, ((width, 2 * tokens), BF16), ((2 * tokens, width), BF16), ((width, norms.shape[1]), F32)],
        *(b0, b1, part, *other, norms),
        scalars=flags,
        scratch=[full, full],
    )


def cross_back_kernel(
    flags_ref,
    db_ref,
    mine_ref,
    other_ref,
    last_ref,
    h2_ref,
    norms_ref,
    cols_in_ref,
    output_ref,
    att_ref,
    cross_ref,
    kv_ref,
    lse_ref,
    bias_ref,
    a2_ref,
    query_ref,
    h1_ref,
    dh1_ref,
    out_grad_ref,
    query_grad_ref,
    dkv_ref,
    cols_ref,
    d_ref,
    do_ref,
    dq_ref,
):
    width, tokens = h2_ref.shape
    pair, half = 2 * width // HEADS, tokens // 2
    other = jnp.concatenate([other_ref[...], last_ref[...]], axis=0)
    by_core(flags_ref, d_ref.at[:, :half], d_ref.at[:, half:], mine_ref[...], other)
    grad, *two = norm_backward(h2_ref[...], column(norms_ref, 2), d_ref[...])
    d_ref[...] = db_ref[...] + grad
    low = d_ref[...].astype(BF16)
    out_grad_ref[...] = dot_nt(low, att_ref[...]).astype(BF16)
    do_ref[...] = dot_tn(output_ref[...], low).astype(BF16)

    def step(j, carry):
        rows, keys, values = pair_rows(j, pair), pair_rows(j, pair), pair_rows(j, pair, width)
        dq, dk, dv = heads_backward(
            cross_ref[rows, :],
            kv_ref[:, keys].T,
            kv_ref[:, keys],
            kv_ref[:, values],
            do_ref[rows, :],
            lse_ref[j],
            lambda s: s + bias_ref[...],
        )
        dq_ref[rows, :], dkv_ref[:, keys], dkv_ref[:, values] = dq, dk, dv
        return carry

    lax.fori_loop(0, HEADS // 2, step, 0)
    query_grad_ref[...] = dot_nt(dq_ref[...], a2_ref[...]).astype(BF16)
    grad, *one = norm_backward(h1_ref[...], column(norms_ref, 1), dot_tn(query_ref[...], dq_ref[...]))
    dh1_ref[...] = d_ref[...] + grad
    columns = cols_ref.shape[1]
    cols_ref[...] = cols_in_ref[...] + norm_columns(2, *two, columns) + norm_columns(1, *one, columns)


def cross_back(flags, *args):
    h2, norms, kv = args[4], args[5], args[10]
    width, tokens = h2.shape
    full, bf = ((width, tokens), F32), ((width, tokens), BF16)
    square = ((width, width), BF16)
    return call(
        cross_back_kernel,
        [full, square, square, (kv.shape, BF16), (norms.shape, F32)],
        *args,
        scalars=flags,
        scratch=[full, bf, bf],
    )


def memory_weight_kernel(dkv_ref, memory_ref, out_ref):
    out_ref[...] = dot_tn(dkv_ref[...], memory_ref[...]).astype(BF16)


def memory_back_kernel(dkv_ref, weight_ref, out_ref):
    out_ref[...] = dot(dkv_ref[...], weight_ref[...])


def self_back_kernel(
    dh1_ref, output_ref, att_ref, qkv_ref, lse_ref, a1_ref, x_ref, project_ref, norms_ref, cols_ref,
    out_grad_ref, project_grad_ref, inputs_grad_ref, norm_grad_ref, do_ref, dqkv_ref
):
    width, tokens = dh1_ref.shape
    pair = 2 * width // HEADS
    scale = jnp.asarray((pair // 2) ** -0.5, BF16)
    low = dh1_ref[...].astype(BF16)
    out_grad_ref[...] = dot_nt(low, att_ref[...]).astype(BF16)
    do_ref[...] = dot_tn(output_ref[...], low).astype(BF16)

    def step(j, carry):
        allowed = causal_mask(tokens)
        rows, keys, values = pair_rows(j, pair), pair_rows(j, pair, width), pair_rows(j, pair, 2 * width)
        key_t = qkv_ref[keys, :]
        dq, dk, dv = heads_backward(
            qkv_ref[rows, :] * scale,
            key_t,
            key_t.T,
            qkv_ref[values, :].T,
            do_ref[rows, :],
            lse_ref[j],
            lambda s: jnp.where(allowed, s, -1e30),
        )
        dqkv_ref[rows, :], dqkv_ref[keys, :], dqkv_ref[values, :] = dq, dk.T, dv.T
        return carry

    lax.fori_loop(0, HEADS // 2, step, 0)
    project_grad_ref[...] = dot_nt(dqkv_ref[...], a1_ref[...]).astype(BF16)
    grad, *zero = norm_backward(
        x_ref[...].T.astype(F32), column(norms_ref, 0), dot_tn(project_ref[...], dqkv_ref[...])
    )
    inputs_grad_ref[...] = (dh1_ref[...] + grad).T
    columns = cols_ref.shape[1]
    norm_grad_ref[...] = jnp.zeros(norm_grad_ref.shape, BF16)
    norm_grad_ref[:, :columns] = (cols_ref[...] + norm_columns(0, *zero, columns)).astype(BF16)


def self_back(*args):
    width, tokens = args[0].shape
    square = ((width, width), BF16)
    return call(
        self_back_kernel,
        [square, ((3 * width, width), BF16), ((tokens, width), F32), square],
        *args,
        scratch=[((width, tokens), BF16), ((3 * width, tokens), BF16)],
    )


def row_blocks(rows, most=512):
    parts = -(-rows // most)
    size = -(-rows // (16 * parts)) * 16
    return [(start, min(start + size, rows)) for start in range(0, rows, size)]


def first_sweep_kernel(base, count, *refs):
    words, rest = refs[:count], refs[count:]
    ht_ref, target_ref, stat_in_ref, sum_in_ref, stat_ref, sum_ref = rest
    half = ht_ref.shape[1] // 2
    top, mass, drift = stat_in_ref[0:1, :], stat_in_ref[1:2, :], stat_in_ref[2:3, :]
    hits = stat_in_ref[3:4, :half]
    sums = sum_in_ref[...]
    for word_ref in words:
        for start, end in row_blocks(word_ref.shape[0], 128):
            rows = word_ref[start:end, :]
            z = dot(rows, ht_ref[...])
            old, top = top, jnp.maximum(top, jnp.max(z, axis=0, keepdims=True))
            e = jnp.exp(z - top)
            z0, z1 = z[:, :half], z[:, half:]
            gap = z0 - z1
            moved = jnp.concatenate(
                [
                    jnp.sum(e[:, :half] * gap, axis=0, keepdims=True),
                    -jnp.sum(e[:, half:] * gap, axis=0, keepdims=True),
                ],
                axis=1,
            )
            spot = lax.broadcasted_iota(jnp.int32, (end - start, half), 0)
            hit = spot == target_ref[0:1, :] - (base + start)
            hits = hits + jnp.sum(jnp.where(hit, z0 + z1, 0.0), axis=0, keepdims=True)
            factor = jnp.exp(old - top)
            mass = mass * factor + jnp.sum(e, axis=0, keepdims=True)
            drift = drift * factor + moved
            sums = sums + dot(jnp.ones((8, end - start), BF16), rows)
        base += word_ref.shape[0]
    hits = jnp.concatenate([hits, jnp.zeros_like(hits)], axis=1)
    stat_ref[...] = jnp.concatenate([top, mass, drift, hits, jnp.zeros((4, 2 * half), F32)], axis=0)
    sum_ref[...] = sums


def first_sweep(base, words, ht, target, stats, sums):
    return call(
        functools.partial(first_sweep_kernel, base, len(words)),
        [(stats.shape, F32), (sums.shape, F32)],
        *(*words, ht, target, stats, sums),
    )


def merge_stats(left, right):
    top = jnp.maximum(left[0:1], right[0:1])
    total = left[1:] * jnp.exp(left[0:1] - top) + right[1:] * jnp.exp(right[0:1] - top)
    return jnp.concatenate([top, total], axis=0)


def stats_result(stats):
    return stats[0:1] + jnp.log(stats[1:2]), stats[2:3] / stats[1:2]


def second_sweep_kernel(bases, last, flags_ref, *refs):
    count = len(bases)
    words, rest = refs[: 2 * count], refs[2 * count :]
    ht_ref, hn_ref, left_ref, right_ref, weight_ref, target_ref, flat_ref, acc_in_refs = *rest[:7], rest[7:9]
    fars, nears, outs = rest[9 : 9 + count], rest[9 + count : 9 + 2 * count], rest[9 + 2 * count : 11 + 2 * count]
    acc_refs = rest[11 + 2 * count :] if last else outs
    lse, drift = stats_result(merge_stats(left_ref[...], right_ref[...]))
    weight = weight_ref[0:1, :]
    offset, slant = jnp.where(weight > 0, lse + 0.6931471805599453, 1e30), 2.0 - drift
    target_weight = (1.0 - SMOOTH) * weight[:, : weight.shape[1] // 2]
    half = ht_ref.shape[1] // 2
    sources = acc_in_refs
    pieces = [
        (n, word_ref, start, end) for n, word_ref in enumerate(words) for start, end in row_blocks(word_ref.shape[0])
    ]
    z = dot(pieces[0][1][pieces[0][2] : pieces[0][3], :], ht_ref[...])
    for index, (n, word_ref, start, end) in enumerate(pieces):
        later = None
        if index + 1 < len(pieces):
            _, next_ref, low, high = pieces[index + 1]
            later = dot(next_ref[low:high, :], ht_ref[...])
        base = bases[n // 2] + (n % 2) * word_ref.shape[0]
        rows = word_ref[start:end, :]
        z0, z1 = z[:, :half], z[:, half:]
        p0 = jnp.exp(z0 - offset[:, :half])
        p1 = jnp.exp(z1 - offset[:, half:])
        gap = z0 - z1
        spot = lax.broadcasted_iota(jnp.int32, (end - start, half), 0)
        hit = spot == target_ref[0:1, :] - (base + start)
        picked = jnp.where(hit, target_weight, 0.0)
        g0 = p0 * (slant[:, :half] + gap) - p1 - picked
        g1 = p1 * (slant[:, half:] - gap) - p0 - picked
        dz = jnp.concatenate([g0.astype(BF16), g1.astype(BF16)], axis=1)
        grad = (dot(dz, hn_ref[...]) + flat_ref[0:1, :]).astype(BF16)
        (nears if n % 2 else fars)[n // 2][start:end, :] = grad
        part = lax.dot_general(rows, dz, (((0,), (0,)), ((), ())), preferred_element_type=F32)
        acc_refs[0][...] = sources[0][...] + part[:, :half]
        acc_refs[1][...] = sources[1][...] + part[:, half:]
        sources = acc_refs
        z = later
    if last:
        give_parts(flags_ref, [ref[...] for ref in acc_refs], *outs)


def second_sweep(flags, bases, words, ht, hn, stats, weight, target, flat, accs, last):
    count = len(bases)
    far_shape = words[0].shape
    full = (accs[0].shape, F32)
    outs = call(
        functools.partial(second_sweep_kernel, bases, last),
        [(far_shape, BF16)] * (2 * count) + [full, (accs[0].shape, BF16) if last else full],
        *(*words, ht, hn, *stats, weight, target, flat, *accs),
        scalars=flags,
        scratch=[full, full] if last else [],
    )
    return outs[:count], outs[count : 2 * count], outs[2 * count :]


def gelu_parts(u):
    scale, cubic = 0.7978845608028654, 0.044715
    t = jnp.tanh(scale * (u + cubic * (u * u * u)))
    value = 0.5 * u * (1.0 + t)
    slope = 0.5 * (1.0 + t) + (0.5 * scale) * u * (1.0 - t * t) * (1.0 + (3.0 * cubic) * (u * u))
    return value, slope


def expert_rows(block_ref, which):
    return jnp.concatenate([block_ref[which, e] for e in range(block_ref.shape[1])], axis=0)


def expert_masks(route_ref, experts, hidden, tokens):
    names = lax.broadcasted_iota(jnp.int32, (experts * hidden, tokens), 0) // hidden
    return [names == route_ref[p : p + 1, :] for p in range(2)]


def give_parts(flags_ref, parts, mine_ref, theirs_ref):
    @pl.when(flags_ref[0] == 0)
    def _():
        mine_ref[...], theirs_ref[...] = parts[0], parts[1].astype(BF16)

    @pl.when(flags_ref[0] != 0)
    def _():
        mine_ref[...], theirs_ref[...] = parts[1], parts[0].astype(BF16)


def expert_forward_kernel(count, first, last, *refs):
    flags_ref, blocks, (a3_ref, route_ref) = refs[0], refs[1 : count + 1], refs[count + 1 : count + 3]
    ins, outs = refs[count + 3 : -2], refs[-2:]
    tokens = a3_ref.shape[1]
    accs = [0.0, 0.0] if first else [ref[...] for ref in ins]
    for block_ref in blocks:
        masks = expert_masks(route_ref, block_ref.shape[1], block_ref.shape[2], tokens)
        u = dot(expert_rows(block_ref, 0), a3_ref[...])
        g = gelu_parts(u)[0]
        w_out = expert_rows(block_ref, 1).T
        accs = [acc + dot(w_out, jnp.where(mask, g, 0.0).astype(BF16)) for acc, mask in zip(accs, masks)]
    if last:
        give_parts(flags_ref, accs, *outs)
    else:
        outs[0][...], outs[1][...] = accs


def expert_forward(flags, blocks, a3, route, accs, last):
    full = (a3.shape, F32)
    return call(
        functools.partial(expert_forward_kernel, len(blocks), not accs, last),
        [full, (a3.shape, BF16) if last else full],
        *(*blocks, a3, route, *accs),
        scalars=flags,
    )


def expert_backward_kernel(groups, flags_ref, *refs):
    blocks, rest = refs[: 2 * groups], refs[2 * groups :]
    a3_ref, an_ref, dy_ref, dn_ref, route_ref = rest[:5]
    fars, nears, (mine_ref, theirs_ref, acc_ref) = rest[5 : 5 + groups], rest[5 + groups : 7 + groups], rest[7 + groups :]
    tokens = a3_ref.shape[1]
    for n, block_ref in enumerate(blocks):
        experts, hidden = block_ref.shape[1:3]
        masks = expert_masks(route_ref, experts, hidden, tokens)
        w_in = expert_rows(block_ref, 0)
        u = dot(w_in, a3_ref[...])
        g, slope = gelu_parts(u)
        d_act = dot(expert_rows(block_ref, 1), dy_ref[...])
        active = jnp.concatenate([jnp.where(mask, g, 0.0) for mask in masks], axis=1).astype(BF16)
        routed = jnp.where(masks[0], d_act[:, :tokens], 0.0) + jnp.where(masks[1], d_act[:, tokens:], 0.0)
        du = (routed * slope).astype(BF16)
        for matrix, grad in enumerate((dot(du, an_ref[...]), dot(active, dn_ref[...]))):
            grad = grad.astype(BF16)
            for e in range(experts):
                piece = grad[e * hidden : (e + 1) * hidden]
                if n % 2:
                    nears[n // 2 % 2][n // 4, matrix, e] = piece
                else:
                    fars[n // 2][matrix, e] = piece
        part = dot(w_in.T, du)
        acc_ref[...] = part if n == 0 else acc_ref[...] + part
    half = tokens // 2
    give_parts(flags_ref, (acc_ref[:, :half], acc_ref[:, half:]), mine_ref, theirs_ref)


def expert_backward(flags, blocks, a3, a3_n, dy, dy_n, route):
    groups = len(blocks) // 2
    shape = blocks[0].shape
    half = (a3.shape[0], a3.shape[1] // 2)
    outs = call(
        functools.partial(expert_backward_kernel, groups),
        [(shape, BF16)] * groups + [((groups // 2,) + shape, BF16)] * 2 + [(half, F32), (half, BF16)],
        *(*blocks, a3, a3_n, dy, dy_n, route),
        scalars=flags,
        scratch=[(a3.shape, F32)],
    )
    return outs[:groups], outs[groups : groups + 2], outs[groups + 2 :]


def unpack_kernel(sizes, order_ref, mine_ref, twin_ref, *outs):
    count, half = mine_ref.shape[0], mine_ref.shape[1]

    def write(low_ref, high_ref):
        for j in range(count):
            source = order_ref[j]
            full = jnp.concatenate([low_ref[source], high_ref[source]], axis=0)
            start = 0
            for size, out in zip(sizes, outs):
                out[j * size : (j + 1) * size, :] = full[start : start + size]
                start += size

    pl.when(order_ref[count] == 0)(lambda: write(mine_ref, twin_ref))
    pl.when(order_ref[count] != 0)(lambda: write(twin_ref, mine_ref))


def unpack(mine, twin, order, core, sizes):
    count, half, width = mine.shape
    if any(size % 16 for size in sizes):
        low, high = jnp.where(core == 0, mine, twin), jnp.where(core == 0, twin, mine)
        full = jnp.concatenate([low, high], axis=1)[order]
        ends = [sum(sizes[: n + 1]) for n in range(len(sizes))]
        return [full[:, end - size : end].reshape(-1, width) for size, end in zip(sizes, ends)]
    return pl.pallas_call(
        functools.partial(unpack_kernel, sizes),
        in_specs=[pl.BlockSpec(memory_space=pltpu.SMEM)] + 2 * [pl.BlockSpec(memory_space=pltpu.VMEM)],
        out_specs=[pl.BlockSpec(memory_space=pltpu.VMEM)] * len(sizes),
        out_shape=[jax.ShapeDtypeStruct((count * size, width), mine.dtype) for size in sizes],
        compiler_params=PARAMS,
        cost_estimate=COST,
    )(jnp.concatenate([order, core[None]]).astype(jnp.int32), mine, twin)


def pack_kernel(sizes, order_ref, *refs):
    out_ref = refs[-1]
    count, half, width = out_ref.shape

    def write(core):
        for k in range(count):
            source = order_ref[k]
            start = -core * half
            for size, ref in zip(sizes, refs[:-1]):
                low, high = max(start, 0), min(start + size, half)
                if low < high:
                    rows = pl.ds(pl.multiple_of(source * size, 16) + (low - start), high - low)
                    out_ref[k, low:high, :] = ref[rows, :].astype(BF16)
                start += size
            low = max(start, 0)
            if low < half:
                out_ref[k, low:, :] = jnp.zeros((half - low, width), BF16)

    pl.when(order_ref[count] == 0)(lambda: write(0))
    pl.when(order_ref[count] != 0)(lambda: write(1))


def pack(grads, order, core, sizes, half):
    width = grads[0].shape[1]
    shards = grads[0].shape[0] // sizes[0]
    if any(size % 16 for size in sizes):
        full = jnp.concatenate([grad.reshape(shards, -1, width) for grad in grads], axis=1)
        full = jnp.pad(full, ((0, 0), (0, 2 * half - full.shape[1]), (0, 0)))[order].astype(BF16)
        return jnp.where(core == 0, full[:, :half], full[:, half:])
    return pl.pallas_call(
        functools.partial(pack_kernel, sizes),
        in_specs=[pl.BlockSpec(memory_space=pltpu.SMEM)]
        + len(grads) * [pl.BlockSpec(memory_space=pltpu.VMEM)],
        out_specs=pl.BlockSpec(memory_space=pltpu.VMEM),
        out_shape=jax.ShapeDtypeStruct((order.shape[0], half, width), BF16),
        compiler_params=PARAMS,
        cost_estimate=COST,
    )(jnp.concatenate([order, core[None]]).astype(jnp.int32), *grads)


def group_sum(mine, theirs):
    chip = (mine + swap(theirs, "vocab", 1).astype(F32)).astype(BF16)
    part = chip.astype(F32) + swap(chip, "pass", 1).astype(F32)
    half = part.shape[0] // 2
    return part, (swap(part[:half], "vocab", 1), swap(part[half:], "vocab", 1)), chip


def local(
    inputs,
    memory,
    expert_ids,
    targets,
    lengths,
    memory_mask,
    norm_gain,
    norm_bias,
    self_project,
    self_output,
    cross_query,
    memory_project,
    cross_output,
    expert_in,
    expert_out,
    embedding,
):
    seq_len, width = inputs.shape
    rows_axis = lax.axis_size("dp")
    here = lax.axis_index("dp")
    which = lax.axis_index("pass")
    core = lax.axis_index("vocab")
    shards = 2 * rows_axis

    sizes = [matrix.shape[1] for matrix in (self_project, self_output, cross_query, memory_project, cross_output)]
    norm_width = norm_gain.shape[1]
    norms = jnp.pad(jnp.concatenate([norm_gain, norm_bias], axis=0).T, ((0, 0), (0, width - 8)))
    sizes = (*sizes, norm_width)

    def core_rows(matrices):
        rows = jnp.concatenate(matrices, axis=0)
        half = -(-rows.shape[0] // 32) * 16
        rows = jnp.pad(rows, ((0, 2 * half - rows.shape[0]), (0, 0)))
        return jnp.where(core == 0, rows[:half], rows[half:])

    mine = core_rows(
        [jnp.concatenate([self_project, self_output, cross_query, memory_project, cross_output], axis=1).T, norms]
    )
    pack_half = mine.shape[0]
    experts = expert_in.shape[0] // 2
    hidden = expert_in.shape[2]

    def core_half(weights):
        halves = weights.reshape(2, experts, width, hidden)
        return jnp.where(core == 0, halves[0], halves[1]).transpose(0, 2, 1)

    expert_block = jnp.stack([core_half(expert_in), core_half(expert_out)])
    expert_gather = Gather(expert_block, "dp")
    layer_gather = Gather(mine, "dp")
    layer_gather.send((2, 3, 1))
    layer_gather.forward((0,))
    layer_gather.forward_together((1, 2, 3))
    expert_gather.forward((0,), layer_gather.arrived(far=(1, 2, 3)))
    parts = layer_gather.result()
    if rows_axis == 8:
        parts = parts[0::2] + parts[1::2]
        mine = [jnp.stack(parts[:4]), jnp.stack(parts[4:])]
        block_order = (0, 2, 4, 6, 1, 3, 5, 7)
    else:
        mine, block_order = [jnp.stack(parts)], range(rows_axis)
    mine = [array for part in mine for array in (part, swap(part, "pass", 1))]
    twin = jnp.concatenate([swap(part, "vocab", 1) for part in mine])
    mine = after(jnp.concatenate(mine), expert_gather.arrived(near=(0,)))
    position = {}
    for n, k in enumerate(block_order):
        part, place = divmod(n, 4) if rows_axis == 8 else (0, n)
        size = 4 if rows_axis == 8 else rows_axis
        position[k] = part * 2 * size + place, part * 2 * size + size + place
    where = jnp.array([position[k] for k in range(rows_axis)], jnp.int32)
    order = where[jnp.arange(shards) // 2 ^ here, jnp.arange(shards) % 2 ^ which]
    project_t, self_output_t, cross_query_t, memory_project_t, cross_output_t, norms = unpack(
        mine, twin, order, core, sizes
    )
    norms = norms[:, : min(width, 128)]
    flags = jnp.stack([core, which]).astype(jnp.int32)

    expert_gather.send((2, 1), layer_gather.mark(3))
    word_gather = Gather(embedding, "dp")
    word_gather.forward((0,), expert_gather.arrived(near=(0,)))

    a1, qkv_t, attended_t, self_lse, h1, a2, cross_t = self_forward(
        inputs, norms, project_t, self_output_t, cross_query_t
    )
    mark = h1, expert_gather.arrived(far=(1, 2)), word_gather.arrived(near=(0,))
    expert_gather.relay(mark)
    expert_gather.forward_together((2, 1), mark)
    word_gather.send((2, 1), mark)
    (memory_kv,) = call(
        memory_keys_kernel, [((memory.shape[0], 2 * width), BF16)], memory, memory_project_t
    )
    mem_bias = jnp.where(memory_mask[0][:, None] == 1, 0.0, -1e30).astype(F32)
    cross_att_t, cross_lse, h2, a3, a3_n = cross_forward(cross_t, memory_kv, mem_bias, h1, norms, cross_output_t)
    expert_gather.forward((3,), (a3, expert_gather.arrived(near=(1, 2))))

    my_route = expert_ids[0, :, 0].astype(F32)[None, :]
    other_route = swap(my_route, "pass", 1)
    routes = jnp.concatenate([my_route, other_route] + [my_route] * 6, axis=0)
    routes = jnp.where(which == 0, routes, jnp.roll(routes, -1, axis=0).at[1].set(my_route[0]))
    route = (routes - (core * experts).astype(F32)).astype(jnp.int32)
    per_half = rows_axis // (2 * GROUPS)

    def halves(parts, axis):
        parts = [parts[n * per_half : (n + 1) * per_half] for n in range(2 * GROUPS)]
        return [part[0] if per_half == 1 else jnp.concatenate(part, axis=axis) for part in parts]

    expert_parts = halves(expert_gather.result(), 2)
    parts = ()
    for place in (0, 1):
        parts = expert_forward(flags, expert_parts[place::2], a3, route, parts, place == 1)
    parts = after(parts, word_gather.arrived(far=(1, 2)))
    word_gather.relay()
    word_gather.forward((1, 2))
    y_part, y_other, mark = group_sum(*parts)
    y_part = after(y_part, word_gather.arrived(near=(1,)))
    half_words = embedding.shape[0] * per_half

    valid = (jnp.arange(seq_len) < lengths[here]).astype(F32)
    half_weight = 0.5 * valid
    weight2 = jnp.concatenate([half_weight, half_weight])[None, :]
    block0, block1, final_t, final_n, block_out, flat_grad = final_norm(
        flags, h2, y_part, y_other, norms, jnp.broadcast_to(weight2, (8, 2 * seq_len)).astype(BF16)
    )
    shard_rows = embedding.shape[0]
    owner = targets // shard_rows
    in_quarter = (owner % 2 == core) & (owner // 2 % 2 == which)
    place = ((owner // 4) ^ here) * shard_rows + targets % shard_rows
    target = jnp.broadcast_to(jnp.where(in_quarter, place, -1)[None, :], (8, seq_len)).astype(jnp.int32)
    word_gather.forward((3,), final_t)
    stats = jnp.concatenate(
        [jnp.full((1, 2 * seq_len), -1e30, F32), jnp.zeros((7, 2 * seq_len), F32)], axis=0
    )
    sums = jnp.zeros((8, width), F32)
    for g in (0, 1, 2, 3):
        words = halves(word_gather.result(), 0)
        stats, sums = first_sweep(
            2 * g * half_words, words[2 * g : 2 * g + 2], final_t, target, stats, sums
        )
    hits = stats[3, :seq_len]

    stats = merge_stats(stats, swap(stats, "vocab", 1))
    stats = stats, swap(stats, "pass", 1)
    lse, drift = stats_result(merge_stats(*stats))
    weight8 = jnp.broadcast_to(weight2, (8, 2 * seq_len))
    accs = [(-SMOOTH / VOCAB) * sums[0][:, None] * half_weight[None, :]] * 2
    word_sum = ScatterSum("dp")
    loss = (
        0.25 * jnp.sum(weight2 * (lse + drift))
        - (1.0 - SMOOTH) * jnp.sum(half_weight * hits)
        + jnp.sum(flat_grad[0] * sums[0])
    )
    loss = jnp.broadcast_to(loss, (8, 128))
    loss_mark = loss
    if rows_axis == 8:
        stack = jnp.stack([loss] + [swap(loss, "dp", 2 * g) for g in (1, 2, 3)])
        loss = sum(lax.dynamic_index_in_dim(stack, here // 2 ^ z, 0, False) for z in range(4))
        loss_mark = loss
        loss = loss + swap(loss, "dp", 1)
    step = 1
    while rows_axis != 8 and step < rows_axis:
        loss = loss + swap(loss, "dp", step)
        step *= 2
    loss_end = loss
    for axis in ("vocab", "pass"):
        loss = loss + swap(loss, axis, 1)
    mean_loss = loss[0, 0] / jnp.sum(lengths).astype(F32)
    for groups in ((3,), (1, 2, 0)):
        fars, nears, accs = second_sweep(
            flags,
            [2 * g * half_words for g in groups],
            [words[2 * g + n] for g in groups for n in range(2)],
            *(final_t, final_n, stats, weight8, target, flat_grad, accs, groups[-1] == 0),
        )
        if groups[-1]:
            word_sum.give(groups, fars, nears, mark=loss_mark)
    word_sum.give((2, 1), fars[1::-1], nears[1::-1])
    accs = after(accs, (word_sum.arrived(near=(3,)), loss_end))
    word_sum.second((3,))

    dh_part, dh_other, mark = group_sum(*accs)
    db, dy, dy_n, cols = final_back(flags, block0, block1, dh_part, dh_other, norms)
    expert_sum = ScatterSum("dp")
    last_words = fars, nears
    *expert_grads, parts = expert_backward(flags, expert_parts, a3, a3_n, dy, dy_n, route)
    mark = (word_sum.arrived(near=(2,)), word_sum.step)
    word_sum.second((1,), parts)
    for start in (1, 0):
        expert_sum.give((start, start + 2), expert_grads[0][start::2], expert_grads[1][start], 2, mark)
    da_part, da_other, mark = group_sum(*parts)
    word_sum.third(parts)

    dh1, cross_output_grad, cross_query_grad, pair_grad, cols = cross_back(
        flags,
        *(db, da_part, *da_other, h2, norms, cols, cross_output_t, cross_att_t, cross_t, memory_kv),
        *(cross_lse, mem_bias, a2, cross_query_t, h1),
    )
    (memory_project_grad,) = call(memory_weight_kernel, [((2 * width, width), BF16)], pair_grad, memory)
    self_output_grad, self_project_grad, inputs_grad, norm_grads = self_back(
        dh1, self_output_t, attended_t, qkv_t, self_lse, a1, inputs, project_t, norms, cols
    )
    expert_sum.second(None, (inputs_grad, word_sum.step, word_sum.last))
    expert_sum.third()
    evens = jnp.concatenate([jnp.arange(0, rows_axis, 2), jnp.arange(1, rows_axis, 2)])
    pack_order = 2 * ((evens if rows_axis == 8 else jnp.arange(rows_axis)) ^ here) + which
    blocks = pack(
        [self_project_grad, self_output_grad, cross_query_grad, memory_project_grad, cross_output_grad, norm_grads],
        pack_order,
        core,
        sizes,
        pack_half,
    )
    (memory_grad,) = call(
        memory_back_kernel, [(memory.shape, F32)], after(pair_grad, blocks), memory_project_t
    )
    layer_sum = ScatterSum("dp")
    if rows_axis == 8:
        layer_sum.give((0, 1, 2, 3), [blocks[g] for g in range(4)], blocks[4:])
        layer_sum.second()
        word_sum.give((0,), last_words[0][2:], last_words[1][2:], mark=layer_sum.arrived(near=(0,)))
        layer_sum.third((expert_sum.last, word_sum.arrived(near=(0,))))
    else:
        layer_sum.blocks = {k: blocks[k] for k in range(rows_axis)}
    if rows_axis != 8:
        word_sum.give((0,), last_words[0][2:], last_words[1][2:])
    embedding_grad = word_sum.result()
    expert_grad = expert_sum.result()
    expert_twin = swap(expert_grad, "vocab", 1)
    expert_grad = jnp.concatenate(
        [
            jnp.where(core == 0, expert_grad, expert_twin),
            jnp.where(core == 0, expert_twin, expert_grad),
        ],
        axis=1,
    ).transpose(0, 1, 3, 2)
    layer_grad = layer_sum.result()
    twin = swap(layer_grad, "vocab", 1)
    layer_grad = jnp.concatenate(
        [jnp.where(core == 0, layer_grad, twin), jnp.where(core == 0, twin, layer_grad)], axis=0
    ).T
    ends = [sum(sizes[: n + 1]) for n in range(len(sizes))]
    layer_grads = [layer_grad[:, end - size : end] for size, end in zip(sizes, ends)]
    norm_out = layer_grads[5][:8]
    return (
        block_out[None],
        mean_loss,
        inputs_grad,
        memory_grad,
        norm_out[:4],
        norm_out[4:],
        *layer_grads[:5],
        expert_grad[0],
        expert_grad[1],
        embedding_grad,
    )


def solution(mesh):
    shared = P(None, ("dp", "pass"))
    placed = (
        P("dp", None),
        P("dp", None),
        P("pass", "dp", None),
        P("dp"),
        P(),
        P("dp", None),
        shared,
        shared,
        shared,
        shared,
        shared,
        shared,
        shared,
        P(None, None, ("dp", "pass")),
        P(None, None, ("dp", "pass")),
        P(("dp", "pass", "vocab"), None),
    )
    return jax.shard_map(
        local,
        mesh=mesh,
        in_specs=placed,
        out_specs=(
            P("pass", "dp", None),
            P(),
            P("dp", None),
            P("dp", None),
            shared,
            shared,
            shared,
            shared,
            shared,
            shared,
            shared,
            P(None, None, ("dp", "pass")),
            P(None, None, ("dp", "pass")),
            P(("dp", "pass", "vocab"), None),
        ),
        check_vma=False,
    )
```

```python
import functools

import jax
import jax.numpy as jnp
from jax import lax
from jax.experimental import pallas as pl
from jax.experimental.pallas import tpu as pltpu
from jax.sharding import PartitionSpec as P

HEADS = 8
VOCAB = 32000
GROUPS = 4
EPSILON = 1e-05
SMOOTH = 0.1
F32 = jnp.float32
BF16 = jnp.bfloat16
PARAMS = pltpu.CompilerParams(vmem_limit_bytes=56 * 1024 * 1024)
COST = pl.CostEstimate(flops=1000, bytes_accessed=1000, transcendentals=0)


def swap(block, axis, mask):
    count = lax.axis_size(axis)
    return lax.ppermute(block, axis, [(i, i ^ mask) for i in range(count)])


def after(value, mark):
    return value if mark is None else lax.optimization_barrier((value, mark))[0]


class Gather:
    def __init__(self, block, axis):
        self.block, self.axis, self.count = block, axis, lax.axis_size(axis)
        self.near, self.far = {}, {0: block}

    def send(self, steps, mark=None):
        if self.count == 8:
            block = after(self.block, mark)
            for g in steps:
                self.far[g] = swap(block, self.axis, 2 * g)

    def forward(self, steps, mark=None):
        if self.count == 8:
            for g in steps:
                self.near[g] = swap(after(self.far[g], mark), self.axis, 1)

    def forward_together(self, steps, mark=None):
        if self.count == 8:
            sent = swap(jnp.stack([after(self.far[g], mark) for g in steps]), self.axis, 1)
            for n, g in enumerate(steps):
                self.near[g] = sent[n]

    def relay(self, mark=None):
        if self.count == 8:
            self.far[3] = swap(after(self.far[2], mark), self.axis, 2)

    def arrived(self, far=(), near=()):
        return [self.far[g] for g in far] + [self.near[g] for g in near] if self.count == 8 else None

    def mark(self, g):
        return self.far[g] if self.count == 8 else None

    def result(self):
        if self.count == 8:
            return [part for g in range(4) for part in (self.far.get(g), self.near.get(g))]
        blocks, step = [self.block], 1
        while step < self.count:
            blocks = blocks + [swap(part, self.axis, step) for part in blocks]
            step *= 2
        return blocks


class ScatterSum:
    def __init__(self, axis):
        self.axis = axis
        self.count = lax.axis_size(axis)
        self.blocks, self.fars, self.near, self.step, self.sent, self.last = {}, {}, {}, None, None, None

    def give(self, groups, fars, nears, split=0, mark=None):
        per_half = self.count // (2 * GROUPS)
        if self.count == 8:
            if isinstance(nears, (list, tuple)):
                nears = [swap(after(near, mark), self.axis, 1) for near in nears]
                self.near.update({g: (near, None) for g, near in zip(groups, nears)})
            else:
                sent = swap(after(nears, mark), self.axis, 1)
                self.near.update({g: (sent, n) for n, g in enumerate(groups)})
            self.fars.update(dict(zip(groups, fars)))
            return
        for n, g in enumerate(groups):
            for half, array in enumerate((fars[n], nears[n])):
                for k, piece in enumerate(jnp.split(array, per_half, axis=split)):
                    self.blocks[(2 * g + half) * per_half + k] = piece

    def joined(self, g, mark=None):
        sent, n = self.near[g]
        sent = after(sent, mark)
        return self.fars[g].astype(F32) + (sent if n is None else sent[n]).astype(F32)

    def second(self, groups=None, mark=None):
        if self.count == 8:
            parts = [self.joined(g, mark).astype(BF16) for g in groups or (1, 3)]
            if groups:
                self.step = {**(self.step or {}), **{g: swap(part, self.axis, 2) for g, part in zip(groups, parts)}}
            else:
                self.sent = sent = swap(jnp.stack(parts), self.axis, 2)
                self.step = {1: sent[0], 3: sent[1]}

    def third(self, mark=None):
        if self.count == 8:
            step = after(self.step[3], mark)
            self.last = swap((self.joined(2) + step.astype(F32)).astype(BF16), self.axis, 4)

    def arrived(self, near=()):
        return [self.near[g][0] for g in near] if self.count == 8 else None

    def result(self, mark=None):
        if self.count == 8:
            last = after(self.last, mark)
            return self.joined(0) + self.step[1].astype(F32) + last.astype(F32)
        blocks = [self.blocks[k] for k in range(self.count)]
        step = self.count // 2
        while step >= 1:
            blocks = [
                blocks[k].astype(F32) + swap(blocks[k + step].astype(BF16), self.axis, step).astype(F32)
                for k in range(step)
            ]
            step //= 2
        return blocks[0]


def dot(left, right):
    return jnp.dot(left, right, preferred_element_type=F32)


def dot_nt(left, right):
    return lax.dot_general(left, right, (((1,), (1,)), ((), ())), preferred_element_type=F32)


def dot_tn(left, right):
    return lax.dot_general(left, right, (((0,), (0,)), ((), ())), preferred_element_type=F32)


def call(kernel, outs, *args, scalars=None, scratch=()):
    specs = [pl.BlockSpec(memory_space=pltpu.VMEM)] * len(args)
    if scalars is not None:
        specs = [pl.BlockSpec(memory_space=pltpu.SMEM)] + specs
        args = (scalars,) + args
    return pl.pallas_call(
        kernel,
        in_specs=specs,
        out_specs=[pl.BlockSpec(memory_space=pltpu.VMEM)] * len(outs),
        out_shape=[jax.ShapeDtypeStruct(shape, dtype) for shape, dtype in outs],
        scratch_shapes=[pltpu.VMEM(shape, dtype) for shape, dtype in scratch],
        compiler_params=PARAMS,
        cost_estimate=COST,
    )(*args)


def by_core(flag_ref, low_ref, high_ref, mine, other):
    @pl.when(flag_ref[0] == 0)
    def _():
        low_ref[...], high_ref[...] = mine, other

    @pl.when(flag_ref[0] != 0)
    def _():
        low_ref[...], high_ref[...] = other, mine


def pair_parts(value, h):
    head = value.shape[0] // 2
    rows = value[h * head : (h + 1) * head]
    zeros = jnp.zeros_like(rows)
    return rows, jnp.concatenate([zeros, rows] if h else [rows, zeros], axis=0)


def pair_rows(j, size, start=0):
    return pl.ds(pl.multiple_of(start + j * size, size), size)


def norm_forward(values, gain, bias):
    average = jnp.mean(values, axis=0, keepdims=True)
    centered = values - average
    scale = lax.rsqrt(jnp.mean(centered * centered, axis=0, keepdims=True) + EPSILON)
    return centered * scale * gain + bias


def norm_backward(values, gain, upstream):
    average = jnp.mean(values, axis=0, keepdims=True)
    centered = values - average
    scale = lax.rsqrt(jnp.mean(centered * centered, axis=0, keepdims=True) + EPSILON)
    unit = centered * scale
    grad = upstream * gain
    result = scale * (
        grad - jnp.mean(grad, axis=0, keepdims=True) - unit * jnp.mean(grad * unit, axis=0, keepdims=True)
    )
    return result, jnp.sum(upstream * unit, axis=1, keepdims=True), jnp.sum(upstream, axis=1, keepdims=True)


def norm_columns(j, gain_grad, bias_grad, width):
    lanes = lax.broadcasted_iota(jnp.int32, (gain_grad.shape[0], width), 1)
    return jnp.where(lanes == j, gain_grad, 0.0) + jnp.where(lanes == 4 + j, bias_grad, 0.0)


def column(norms_ref, j):
    return norms_ref[:, j : j + 1].astype(F32)


def causal_mask(tokens):
    shape = (tokens, tokens)
    return lax.broadcasted_iota(jnp.int32, shape, 0) <= lax.broadcasted_iota(jnp.int32, shape, 1)


def heads_forward(query, keys_n, value_t, masked, out_ref, lse_ref, j):
    head = query.shape[0] // 2
    for h in range(2):
        s = masked(dot(keys_n, pair_parts(query, h)[1]))
        m = jnp.max(s, axis=0, keepdims=True)
        e = jnp.exp(s - m)
        total = jnp.sum(e, axis=0, keepdims=True)
        p = (e * (1.0 / total)).astype(BF16)
        out_ref[pair_rows(2 * j + h, head), :] = dot(value_t[h * head : (h + 1) * head], p).astype(BF16)
        lse_ref[j, h : h + 1, :] = m + jnp.log(total)


def heads_backward(query, key_t, keys_n, values_n, upstream, lse, masked):
    head = query.shape[0] // 2
    dq, dk, dv = [], 0.0, 0.0
    for h in range(2):
        q_pad = pair_parts(query, h)[1]
        do_pad = pair_parts(upstream, h)[1]
        p = jnp.exp(masked(dot(keys_n, q_pad)) - lse[h : h + 1, :])
        pdp = p * dot(values_n, do_pad)
        total = jnp.sum(pdp, axis=0, keepdims=True)
        ds = (pdp - p * total).astype(BF16)
        dq.append(dot(pair_parts(key_t, h)[0], ds) * head**-0.5)
        dk = dk + dot(ds, q_pad.T)
        dv = dv + dot(p.astype(BF16), do_pad.T)
    return jnp.concatenate(dq, axis=0).astype(BF16), dk.astype(BF16), dv.astype(BF16)


def self_forward_kernel(
    x_ref, norms_ref, project_ref, output_ref, query_ref, a1_ref, qkv_ref, att_ref, lse_ref, h1_ref, a2_ref, cross_ref
):
    tokens, width = x_ref.shape
    pair = 2 * width // HEADS
    scale = jnp.asarray((pair // 2) ** -0.5, BF16)
    a1_ref[...] = norm_forward(x_ref[...].T.astype(F32), column(norms_ref, 0), column(norms_ref, 4)).astype(BF16)
    qkv_ref[...] = dot(project_ref[...], a1_ref[...]).astype(BF16)

    def step(j, carry):
        allowed = causal_mask(tokens)
        heads_forward(
            qkv_ref[pair_rows(j, pair), :] * scale,
            qkv_ref[pair_rows(j, pair, width), :].T,
            qkv_ref[pair_rows(j, pair, 2 * width), :],
            lambda s: jnp.where(allowed, s, -1e30),
            att_ref,
            lse_ref,
            j,
        )
        return carry

    lax.fori_loop(0, HEADS // 2, step, 0)
    h1_ref[...] = x_ref[...].T.astype(F32) + dot(output_ref[...], att_ref[...])
    a2_ref[...] = norm_forward(h1_ref[...], column(norms_ref, 1), column(norms_ref, 5)).astype(BF16)
    cross_ref[...] = dot(query_ref[...], a2_ref[...]).astype(BF16) * scale


def self_forward(x, norms, project, output, query):
    tokens, width = x.shape
    bf = ((width, tokens), BF16)
    return call(
        self_forward_kernel,
        [bf, ((3 * width, tokens), BF16), bf, ((HEADS // 2, 2, tokens), F32), ((width, tokens), F32), bf, bf],
        *(x, norms, project, output, query),
    )


def memory_keys_kernel(memory_ref, weight_ref, out_ref):
    out_ref[...] = dot_nt(memory_ref[...], weight_ref[...]).astype(BF16)


def cross_forward_kernel(
    cross_ref, kv_ref, bias_ref, h1_ref, norms_ref, output_ref, att_ref, lse_ref, h2_ref, a3_ref, an_ref
):
    width = cross_ref.shape[0]
    pair = 2 * width // HEADS

    def step(j, carry):
        heads_forward(
            cross_ref[pair_rows(j, pair), :],
            kv_ref[:, pair_rows(j, pair)],
            kv_ref[:, pair_rows(j, pair, width)].T,
            lambda s: s + bias_ref[...],
            att_ref,
            lse_ref,
            j,
        )
        return carry

    lax.fori_loop(0, HEADS // 2, step, 0)
    h2_ref[...] = h1_ref[...] + dot(output_ref[...], att_ref[...])
    a3_ref[...] = norm_forward(h2_ref[...], column(norms_ref, 2), column(norms_ref, 6)).astype(BF16)
    an_ref[...] = a3_ref[...].T


def cross_forward(cross, kv, bias, h1, norms, output):
    width, tokens = cross.shape
    bf = ((width, tokens), BF16)
    return call(
        cross_forward_kernel,
        [bf, ((HEADS // 2, 2, tokens), F32), ((width, tokens), F32), bf, ((tokens, width), BF16)],
        *(cross, kv, bias, h1, norms, output),
    )


def final_norm_kernel(
    flags_ref, h2_ref, part_ref, other_ref, last_ref, norms_ref, weight_ref, b0_ref, b1_ref, ft_ref, fn_ref, out_ref, flat_ref
):
    tokens = h2_ref.shape[1]
    other = jnp.concatenate([other_ref[...], last_ref[...]], axis=0)
    by_core(flags_ref, b0_ref, b1_ref, h2_ref[...] + part_ref[...], h2_ref[...] + other)
    for p, ref in enumerate((b0_ref, b1_ref)):
        final = norm_forward(ref[...], column(norms_ref, 3), column(norms_ref, 7)).astype(BF16)
        ft_ref[:, p * tokens : (p + 1) * tokens] = final
        fn_ref[p * tokens : (p + 1) * tokens, :] = final.T

        @pl.when(flags_ref[1] == p)
        def _():
            out_ref[...] = ref[...].T

    flat_ref[...] = dot(weight_ref[...], fn_ref[...]) * (-SMOOTH / VOCAB)


def final_norm(flags, h2, part, other, norms, weight):
    width, tokens = h2.shape
    full = ((width, tokens), F32)
    return call(
        final_norm_kernel,
        [full, full, ((width, 2 * tokens), BF16), ((2 * tokens, width), BF16), ((tokens, width), F32), ((8, width), F32)],
        *(h2, part, *other, norms, weight),
        scalars=flags,
    )


def final_back_kernel(
    flags_ref, b0_ref, b1_ref, part_ref, other_ref, last_ref, norms_ref, db_ref, dy_ref, dn_ref, cols_ref, d0_ref, d1_ref
):
    tokens = b0_ref.shape[1]
    other = jnp.concatenate([other_ref[...], last_ref[...]], axis=0)
    by_core(flags_ref, d0_ref, d1_ref, part_ref[...], other)
    total, cols = 0.0, 0.0
    for p, (block_ref, d_ref) in enumerate(((b0_ref, d0_ref), (b1_ref, d1_ref))):
        grad, *norm_grads = norm_backward(block_ref[...], column(norms_ref, 3), d_ref[...])
        low = grad.astype(BF16)
        dy_ref[:, p * tokens : (p + 1) * tokens] = low
        dn_ref[p * tokens : (p + 1) * tokens, :] = low.T
        total, cols = total + grad, cols + norm_columns(3, *norm_grads, cols_ref.shape[1])
    db_ref[...], cols_ref[...] = total, cols


def final_back(flags, b0, b1, part, other, norms):
    width, tokens = b0.shape
    full = ((width, tokens), F32)
    return call(
        final_back_kernel,
        [full, ((width, 2 * tokens), BF16), ((2 * tokens, width), BF16), ((width, norms.shape[1]), F32)],
        *(b0, b1, part, *other, norms),
        scalars=flags,
        scratch=[full, full],
    )


def cross_back_kernel(
    flags_ref,
    db_ref,
    mine_ref,
    other_ref,
    last_ref,
    h2_ref,
    norms_ref,
    cols_in_ref,
    output_ref,
    att_ref,
    cross_ref,
    kv_ref,
    lse_ref,
    bias_ref,
    a2_ref,
    query_ref,
    h1_ref,
    dh1_ref,
    out_grad_ref,
    query_grad_ref,
    dkv_ref,
    cols_ref,
    d_ref,
    do_ref,
    dq_ref,
):
    width, tokens = h2_ref.shape
    pair, half = 2 * width // HEADS, tokens // 2
    other = jnp.concatenate([other_ref[...], last_ref[...]], axis=0)
    by_core(flags_ref, d_ref.at[:, :half], d_ref.at[:, half:], mine_ref[...], other)
    grad, *two = norm_backward(h2_ref[...], column(norms_ref, 2), d_ref[...])
    d_ref[...] = db_ref[...] + grad
    low = d_ref[...].astype(BF16)
    out_grad_ref[...] = dot_nt(low, att_ref[...]).astype(BF16)
    do_ref[...] = dot_tn(output_ref[...], low).astype(BF16)

    def step(j, carry):
        rows, keys, values = pair_rows(j, pair), pair_rows(j, pair), pair_rows(j, pair, width)
        dq, dk, dv = heads_backward(
            cross_ref[rows, :],
            kv_ref[:, keys].T,
            kv_ref[:, keys],
            kv_ref[:, values],
            do_ref[rows, :],
            lse_ref[j],
            lambda s: s + bias_ref[...],
        )
        dq_ref[rows, :], dkv_ref[:, keys], dkv_ref[:, values] = dq, dk, dv
        return carry

    lax.fori_loop(0, HEADS // 2, step, 0)
    query_grad_ref[...] = dot_nt(dq_ref[...], a2_ref[...]).astype(BF16)
    grad, *one = norm_backward(h1_ref[...], column(norms_ref, 1), dot_tn(query_ref[...], dq_ref[...]))
    dh1_ref[...] = d_ref[...] + grad
    columns = cols_ref.shape[1]
    cols_ref[...] = cols_in_ref[...] + norm_columns(2, *two, columns) + norm_columns(1, *one, columns)


def cross_back(flags, *args):
    h2, norms, kv = args[4], args[5], args[10]
    width, tokens = h2.shape
    full, bf = ((width, tokens), F32), ((width, tokens), BF16)
    square = ((width, width), BF16)
    return call(
        cross_back_kernel,
        [full, square, square, (kv.shape, BF16), (norms.shape, F32)],
        *args,
        scalars=flags,
        scratch=[full, bf, bf],
    )


def memory_weight_kernel(dkv_ref, memory_ref, out_ref):
    out_ref[...] = dot_tn(dkv_ref[...], memory_ref[...]).astype(BF16)


def memory_back_kernel(dkv_ref, weight_ref, out_ref):
    out_ref[...] = dot(dkv_ref[...], weight_ref[...])


def self_back_kernel(
    dh1_ref, output_ref, att_ref, qkv_ref, lse_ref, a1_ref, x_ref, project_ref, norms_ref, cols_ref,
    out_grad_ref, project_grad_ref, inputs_grad_ref, norm_grad_ref, do_ref, dqkv_ref
):
    width, tokens = dh1_ref.shape
    pair = 2 * width // HEADS
    scale = jnp.asarray((pair // 2) ** -0.5, BF16)
    low = dh1_ref[...].astype(BF16)
    out_grad_ref[...] = dot_nt(low, att_ref[...]).astype(BF16)
    do_ref[...] = dot_tn(output_ref[...], low).astype(BF16)

    def step(j, carry):
        allowed = causal_mask(tokens)
        rows, keys, values = pair_rows(j, pair), pair_rows(j, pair, width), pair_rows(j, pair, 2 * width)
        key_t = qkv_ref[keys, :]
        dq, dk, dv = heads_backward(
            qkv_ref[rows, :] * scale,
            key_t,
            key_t.T,
            qkv_ref[values, :].T,
            do_ref[rows, :],
            lse_ref[j],
            lambda s: jnp.where(allowed, s, -1e30),
        )
        dqkv_ref[rows, :], dqkv_ref[keys, :], dqkv_ref[values, :] = dq, dk.T, dv.T
        return carry

    lax.fori_loop(0, HEADS // 2, step, 0)
    project_grad_ref[...] = dot_nt(dqkv_ref[...], a1_ref[...]).astype(BF16)
    grad, *zero = norm_backward(
        x_ref[...].T.astype(F32), column(norms_ref, 0), dot_tn(project_ref[...], dqkv_ref[...])
    )
    inputs_grad_ref[...] = (dh1_ref[...] + grad).T
    columns = cols_ref.shape[1]
    norm_grad_ref[...] = jnp.zeros(norm_grad_ref.shape, BF16)
    norm_grad_ref[:, :columns] = (cols_ref[...] + norm_columns(0, *zero, columns)).astype(BF16)


def self_back(*args):
    width, tokens = args[0].shape
    square = ((width, width), BF16)
    return call(
        self_back_kernel,
        [square, ((3 * width, width), BF16), ((tokens, width), F32), square],
        *args,
        scratch=[((width, tokens), BF16), ((3 * width, tokens), BF16)],
    )


def row_blocks(rows, most=512):
    parts = -(-rows // most)
    size = -(-rows // (16 * parts)) * 16
    return [(start, min(start + size, rows)) for start in range(0, rows, size)]


def first_sweep_kernel(base, count, *refs):
    words, rest = refs[:count], refs[count:]
    ht_ref, target_ref, stat_in_ref, sum_in_ref, stat_ref, sum_ref = rest
    half = ht_ref.shape[1] // 2
    top, mass, drift = stat_in_ref[0:1, :], stat_in_ref[1:2, :], stat_in_ref[2:3, :]
    hits = stat_in_ref[3:4, :half]
    sums = sum_in_ref[...]
    for word_ref in words:
        for start, end in row_blocks(word_ref.shape[0], 128):
            rows = word_ref[start:end, :]
            z = dot(rows, ht_ref[...])
            old, top = top, jnp.maximum(top, jnp.max(z, axis=0, keepdims=True))
            e = jnp.exp(z - top)
            z0, z1 = z[:, :half], z[:, half:]
            gap = z0 - z1
            moved = jnp.concatenate(
                [
                    jnp.sum(e[:, :half] * gap, axis=0, keepdims=True),
                    -jnp.sum(e[:, half:] * gap, axis=0, keepdims=True),
                ],
                axis=1,
            )
            spot = lax.broadcasted_iota(jnp.int32, (end - start, half), 0)
            hit = spot == target_ref[0:1, :] - (base + start)
            hits = hits + jnp.sum(jnp.where(hit, z0 + z1, 0.0), axis=0, keepdims=True)
            factor = jnp.exp(old - top)
            mass = mass * factor + jnp.sum(e, axis=0, keepdims=True)
            drift = drift * factor + moved
            sums = sums + dot(jnp.ones((8, end - start), BF16), rows)
        base += word_ref.shape[0]
    hits = jnp.concatenate([hits, jnp.zeros_like(hits)], axis=1)
    stat_ref[...] = jnp.concatenate([top, mass, drift, hits, jnp.zeros((4, 2 * half), F32)], axis=0)
    sum_ref[...] = sums


def first_sweep(base, words, ht, target, stats, sums):
    return call(
        functools.partial(first_sweep_kernel, base, len(words)),
        [(stats.shape, F32), (sums.shape, F32)],
        *(*words, ht, target, stats, sums),
    )


def merge_stats(left, right):
    top = jnp.maximum(left[0:1], right[0:1])
    total = left[1:] * jnp.exp(left[0:1] - top) + right[1:] * jnp.exp(right[0:1] - top)
    return jnp.concatenate([top, total], axis=0)


def stats_result(stats):
    return stats[0:1] + jnp.log(stats[1:2]), stats[2:3] / stats[1:2]


def second_sweep_kernel(bases, first, last, flags_ref, *refs):
    count = len(bases)
    words, rest = refs[: 2 * count], refs[2 * count :]
    ht_ref, hn_ref, left_ref, right_ref, weight_ref, target_ref, flat_ref, acc_in_refs = *rest[:7], rest[7:9]
    fars, nears, outs = rest[9 : 9 + count], rest[9 + count : 9 + 2 * count], rest[9 + 2 * count : 11 + 2 * count]
    acc_refs = rest[11 + 2 * count :] if last else outs
    lse, drift = stats_result(merge_stats(left_ref[...], right_ref[...]))
    weight = weight_ref[0:1, :]
    offset, slant = jnp.where(weight > 0, lse + 0.6931471805599453, 1e30), 2.0 - drift
    target_weight = (1.0 - SMOOTH) * weight[:, : weight.shape[1] // 2]
    half = ht_ref.shape[1] // 2
    if first:
        start_value = acc_in_refs[0][...].T[:, 0:1] * (weight[:, : weight.shape[1] // 2] * (-SMOOTH / VOCAB))
        acc_refs[0][...], acc_refs[1][...] = start_value, start_value
    sources = acc_refs if first else acc_in_refs
    pieces = [
        (n, word_ref, start, end) for n, word_ref in enumerate(words) for start, end in row_blocks(word_ref.shape[0])
    ]
    z = dot(pieces[0][1][pieces[0][2] : pieces[0][3], :], ht_ref[...])
    for index, (n, word_ref, start, end) in enumerate(pieces):
        later = None
        if index + 1 < len(pieces):
            _, next_ref, low, high = pieces[index + 1]
            later = dot(next_ref[low:high, :], ht_ref[...])
        base = bases[n // 2] + (n % 2) * word_ref.shape[0]
        rows = word_ref[start:end, :]
        z0, z1 = z[:, :half], z[:, half:]
        p0 = jnp.exp(z0 - offset[:, :half])
        p1 = jnp.exp(z1 - offset[:, half:])
        gap = z0 - z1
        spot = lax.broadcasted_iota(jnp.int32, (end - start, half), 0)
        hit = spot == target_ref[0:1, :] - (base + start)
        picked = jnp.where(hit, target_weight, 0.0)
        g0 = p0 * (slant[:, :half] + gap) - p1 - picked
        g1 = p1 * (slant[:, half:] - gap) - p0 - picked
        dz = jnp.concatenate([g0.astype(BF16), g1.astype(BF16)], axis=1)
        grad = (dot(dz, hn_ref[...]) + flat_ref[0:1, :]).astype(BF16)
        (nears if n % 2 else fars)[n // 2][start:end, :] = grad
        part = lax.dot_general(rows, dz, (((0,), (0,)), ((), ())), preferred_element_type=F32)
        acc_refs[0][...] = sources[0][...] + part[:, :half]
        acc_refs[1][...] = sources[1][...] + part[:, half:]
        sources = acc_refs
        z = later
    if last:
        give_parts(flags_ref, [ref[...] for ref in acc_refs], *outs)


def second_sweep(flags, bases, words, ht, hn, stats, weight, target, flat, accs, last):
    count = len(bases)
    far_shape = words[0].shape
    first = accs[0].shape[0] == 8
    shape = (ht.shape[0], ht.shape[1] // 2)
    full = (shape, F32)
    outs = call(
        functools.partial(second_sweep_kernel, bases, first, last),
        [(far_shape, BF16)] * (2 * count) + [full, (shape, BF16) if last else full],
        *(*words, ht, hn, *stats, weight, target, flat, *accs),
        scalars=flags,
        scratch=[full, full] if last else [],
    )
    return outs[:count], outs[count : 2 * count], outs[2 * count :]


def gelu_parts(u):
    scale, cubic = 0.7978845608028654, 0.044715
    t = jnp.tanh(scale * (u + cubic * (u * u * u)))
    value = 0.5 * u * (1.0 + t)
    slope = 0.5 * (1.0 + t) + (0.5 * scale) * u * (1.0 - t * t) * (1.0 + (3.0 * cubic) * (u * u))
    return value, slope


def expert_rows(block_ref, which):
    return jnp.concatenate([block_ref[which, e] for e in range(block_ref.shape[1])], axis=0)


def expert_masks(route_ref, experts, hidden, tokens):
    names = lax.broadcasted_iota(jnp.int32, (experts * hidden, tokens), 0) // hidden
    return [names == route_ref[p : p + 1, :] for p in range(2)]


def give_parts(flags_ref, parts, mine_ref, theirs_ref):
    @pl.when(flags_ref[0] == 0)
    def _():
        mine_ref[...], theirs_ref[...] = parts[0], parts[1].astype(BF16)

    @pl.when(flags_ref[0] != 0)
    def _():
        mine_ref[...], theirs_ref[...] = parts[1], parts[0].astype(BF16)


def expert_forward_kernel(count, first, last, *refs):
    flags_ref, blocks, (a3_ref, route_ref) = refs[0], refs[1 : count + 1], refs[count + 1 : count + 3]
    ins, outs = refs[count + 3 : -2], refs[-2:]
    tokens = a3_ref.shape[1]
    accs = [0.0, 0.0] if first else [ref[...] for ref in ins]
    for block_ref in blocks:
        masks = expert_masks(route_ref, block_ref.shape[1], block_ref.shape[2], tokens)
        u = dot(expert_rows(block_ref, 0), a3_ref[...])
        g = gelu_parts(u)[0]
        w_out = expert_rows(block_ref, 1).T
        accs = [acc + dot(w_out, jnp.where(mask, g, 0.0).astype(BF16)) for acc, mask in zip(accs, masks)]
    if last:
        give_parts(flags_ref, accs, *outs)
    else:
        outs[0][...], outs[1][...] = accs


def expert_forward(flags, blocks, a3, route, accs, last):
    full = (a3.shape, F32)
    return call(
        functools.partial(expert_forward_kernel, len(blocks), not accs, last),
        [full, (a3.shape, BF16) if last else full],
        *(*blocks, a3, route, *accs),
        scalars=flags,
    )


def expert_backward_kernel(groups, flags_ref, *refs):
    blocks, rest = refs[: 2 * groups], refs[2 * groups :]
    a3_ref, an_ref, dy_ref, dn_ref, route_ref = rest[:5]
    fars, nears, (mine_ref, theirs_ref, acc_ref) = rest[5 : 5 + groups], rest[5 + groups : 7 + groups], rest[7 + groups :]
    tokens = a3_ref.shape[1]
    for n, block_ref in enumerate(blocks):
        experts, hidden = block_ref.shape[1:3]
        masks = expert_masks(route_ref, experts, hidden, tokens)
        w_in = expert_rows(block_ref, 0)
        u = dot(w_in, a3_ref[...])
        g, slope = gelu_parts(u)
        d_act = dot(expert_rows(block_ref, 1), dy_ref[...])
        active = jnp.concatenate([jnp.where(mask, g, 0.0) for mask in masks], axis=1).astype(BF16)
        routed = jnp.where(masks[0], d_act[:, :tokens], 0.0) + jnp.where(masks[1], d_act[:, tokens:], 0.0)
        du = (routed * slope).astype(BF16)
        for matrix, grad in enumerate((dot(du, an_ref[...]), dot(active, dn_ref[...]))):
            grad = grad.astype(BF16)
            for e in range(experts):
                piece = grad[e * hidden : (e + 1) * hidden]
                if n % 2:
                    nears[n // 2 % 2][n // 4, matrix, e] = piece
                else:
                    fars[n // 2][matrix, e] = piece
        part = dot(w_in.T, du)
        acc_ref[...] = part if n == 0 else acc_ref[...] + part
    half = tokens // 2
    give_parts(flags_ref, (acc_ref[:, :half], acc_ref[:, half:]), mine_ref, theirs_ref)


def expert_backward(flags, blocks, a3, a3_n, dy, dy_n, route):
    groups = len(blocks) // 2
    shape = blocks[0].shape
    half = (a3.shape[0], a3.shape[1] // 2)
    outs = call(
        functools.partial(expert_backward_kernel, groups),
        [(shape, BF16)] * groups + [((groups // 2,) + shape, BF16)] * 2 + [(half, F32), (half, BF16)],
        *(*blocks, a3, a3_n, dy, dy_n, route),
        scalars=flags,
        scratch=[(a3.shape, F32)],
    )
    return outs[:groups], outs[groups : groups + 2], outs[groups + 2 :]


def unpack_kernel(sizes, order_ref, mine_ref, twin_ref, *outs):
    count, half = mine_ref.shape[0], mine_ref.shape[1]

    def write(low_ref, high_ref):
        for j in range(count):
            source = order_ref[j]
            full = jnp.concatenate([low_ref[source], high_ref[source]], axis=0)
            start = 0
            for size, out in zip(sizes, outs):
                out[j * size : (j + 1) * size, :] = full[start : start + size]
                start += size

    pl.when(order_ref[count] == 0)(lambda: write(mine_ref, twin_ref))
    pl.when(order_ref[count] != 0)(lambda: write(twin_ref, mine_ref))


def unpack(mine, twin, order, core, sizes):
    count, half, width = mine.shape
    if any(size % 16 for size in sizes):
        low, high = jnp.where(core == 0, mine, twin), jnp.where(core == 0, twin, mine)
        full = jnp.concatenate([low, high], axis=1)[order]
        ends = [sum(sizes[: n + 1]) for n in range(len(sizes))]
        return [full[:, end - size : end].reshape(-1, width) for size, end in zip(sizes, ends)]
    return pl.pallas_call(
        functools.partial(unpack_kernel, sizes),
        in_specs=[pl.BlockSpec(memory_space=pltpu.SMEM)] + 2 * [pl.BlockSpec(memory_space=pltpu.VMEM)],
        out_specs=[pl.BlockSpec(memory_space=pltpu.VMEM)] * len(sizes),
        out_shape=[jax.ShapeDtypeStruct((count * size, width), mine.dtype) for size in sizes],
        compiler_params=PARAMS,
        cost_estimate=COST,
    )(jnp.concatenate([order, core[None]]).astype(jnp.int32), mine, twin)


def pack_kernel(sizes, order_ref, *refs):
    out_ref = refs[-1]
    count, half, width = out_ref.shape

    def write(core):
        for k in range(count):
            source = order_ref[k]
            start = -core * half
            for size, ref in zip(sizes, refs[:-1]):
                low, high = max(start, 0), min(start + size, half)
                if low < high:
                    rows = pl.ds(pl.multiple_of(source * size, 16) + (low - start), high - low)
                    out_ref[k, low:high, :] = ref[rows, :].astype(BF16)
                start += size
            low = max(start, 0)
            if low < half:
                out_ref[k, low:, :] = jnp.zeros((half - low, width), BF16)

    pl.when(order_ref[count] == 0)(lambda: write(0))
    pl.when(order_ref[count] != 0)(lambda: write(1))


def pack(grads, order, core, sizes, half):
    width = grads[0].shape[1]
    shards = grads[0].shape[0] // sizes[0]
    if any(size % 16 for size in sizes):
        full = jnp.concatenate([grad.reshape(shards, -1, width) for grad in grads], axis=1)
        full = jnp.pad(full, ((0, 0), (0, 2 * half - full.shape[1]), (0, 0)))[order].astype(BF16)
        return jnp.where(core == 0, full[:, :half], full[:, half:])
    return pl.pallas_call(
        functools.partial(pack_kernel, sizes),
        in_specs=[pl.BlockSpec(memory_space=pltpu.SMEM)]
        + len(grads) * [pl.BlockSpec(memory_space=pltpu.VMEM)],
        out_specs=pl.BlockSpec(memory_space=pltpu.VMEM),
        out_shape=jax.ShapeDtypeStruct((order.shape[0], half, width), BF16),
        compiler_params=PARAMS,
        cost_estimate=COST,
    )(jnp.concatenate([order, core[None]]).astype(jnp.int32), *grads)


def group_sum(mine, theirs):
    chip = (mine + swap(theirs, "vocab", 1).astype(F32)).astype(BF16)
    part = chip.astype(F32) + swap(chip, "pass", 1).astype(F32)
    half = part.shape[0] // 2
    return part, (swap(part[:half], "vocab", 1), swap(part[half:], "vocab", 1)), chip


def local(
    inputs,
    memory,
    expert_ids,
    targets,
    lengths,
    memory_mask,
    norm_gain,
    norm_bias,
    self_project,
    self_output,
    cross_query,
    memory_project,
    cross_output,
    expert_in,
    expert_out,
    embedding,
):
    seq_len, width = inputs.shape
    rows_axis = lax.axis_size("dp")
    here = lax.axis_index("dp")
    which = lax.axis_index("pass")
    core = lax.axis_index("vocab")
    shards = 2 * rows_axis

    sizes = [matrix.shape[1] for matrix in (self_project, self_output, cross_query, memory_project, cross_output)]
    norm_width = norm_gain.shape[1]
    norms = jnp.pad(jnp.concatenate([norm_gain, norm_bias], axis=0).T, ((0, 0), (0, width - 8)))
    sizes = (*sizes, norm_width)

    def core_rows(matrices):
        rows = jnp.concatenate(matrices, axis=0)
        half = -(-rows.shape[0] // 32) * 16
        rows = jnp.pad(rows, ((0, 2 * half - rows.shape[0]), (0, 0)))
        return jnp.where(core == 0, rows[:half], rows[half:])

    mine = core_rows(
        [jnp.concatenate([self_project, self_output, cross_query, memory_project, cross_output], axis=1).T, norms]
    )
    pack_half = mine.shape[0]
    experts = expert_in.shape[0] // 2
    hidden = expert_in.shape[2]

    def core_half(weights):
        halves = weights.reshape(2, experts, width, hidden)
        return jnp.where(core == 0, halves[0], halves[1]).transpose(0, 2, 1)

    expert_block = jnp.stack([core_half(expert_in), core_half(expert_out)])
    expert_gather = Gather(expert_block, "dp")
    layer_gather = Gather(mine, "dp")
    layer_gather.send((2, 3, 1))
    layer_gather.forward((0,))
    layer_gather.forward_together((1, 2, 3))
    expert_gather.forward((0,), layer_gather.arrived(far=(1, 2, 3)))
    parts = layer_gather.result()
    if rows_axis == 8:
        parts = parts[0::2] + parts[1::2]
        mine = [jnp.stack(parts[:4]), jnp.stack(parts[4:])]
        block_order = (0, 2, 4, 6, 1, 3, 5, 7)
    else:
        mine, block_order = [jnp.stack(parts)], range(rows_axis)
    mine = [array for part in mine for array in (part, swap(part, "pass", 1))]
    twin = jnp.concatenate([swap(part, "vocab", 1) for part in mine])
    mine = after(jnp.concatenate(mine), expert_gather.arrived(near=(0,)))
    position = {}
    for n, k in enumerate(block_order):
        part, place = divmod(n, 4) if rows_axis == 8 else (0, n)
        size = 4 if rows_axis == 8 else rows_axis
        position[k] = part * 2 * size + place, part * 2 * size + size + place
    where = jnp.array([position[k] for k in range(rows_axis)], jnp.int32)
    order = where[jnp.arange(shards) // 2 ^ here, jnp.arange(shards) % 2 ^ which]
    project_t, self_output_t, cross_query_t, memory_project_t, cross_output_t, norms = unpack(
        mine, twin, order, core, sizes
    )
    norms = norms[:, : min(width, 128)]
    flags = jnp.stack([core, which]).astype(jnp.int32)

    expert_gather.send((2, 1), layer_gather.mark(3))
    word_gather = Gather(embedding, "dp")
    word_gather.forward((0,), expert_gather.arrived(near=(0,)))

    a1, qkv_t, attended_t, self_lse, h1, a2, cross_t = self_forward(
        inputs, norms, project_t, self_output_t, cross_query_t
    )
    mark = h1, expert_gather.arrived(far=(1, 2)), word_gather.arrived(near=(0,))
    expert_gather.relay(mark)
    expert_gather.forward_together((2, 1), mark)
    word_gather.send((2, 1), mark)
    (memory_kv,) = call(
        memory_keys_kernel, [((memory.shape[0], 2 * width), BF16)], memory, memory_project_t
    )
    mem_bias = jnp.where(memory_mask[0][:, None] == 1, 0.0, -1e30).astype(F32)
    cross_att_t, cross_lse, h2, a3, a3_n = cross_forward(cross_t, memory_kv, mem_bias, h1, norms, cross_output_t)
    expert_gather.forward((3,), (a3, expert_gather.arrived(near=(1, 2))))

    my_route = expert_ids[0, :, 0].astype(F32)[None, :]
    other_route = swap(my_route, "pass", 1)
    routes = jnp.concatenate([my_route, other_route] + [my_route] * 6, axis=0)
    routes = jnp.where(which == 0, routes, jnp.roll(routes, -1, axis=0).at[1].set(my_route[0]))
    route = (routes - (core * experts).astype(F32)).astype(jnp.int32)
    per_half = rows_axis // (2 * GROUPS)

    def halves(parts, axis):
        parts = [parts[n * per_half : (n + 1) * per_half] for n in range(2 * GROUPS)]
        return [part[0] if per_half == 1 else jnp.concatenate(part, axis=axis) for part in parts]

    expert_parts = halves(expert_gather.result(), 2)
    parts = ()
    for place in (0, 1):
        parts = expert_forward(flags, expert_parts[place::2], a3, route, parts, place == 1)
    parts = after(parts, word_gather.arrived(far=(1, 2)))
    word_gather.relay()
    word_gather.forward((1, 2))
    y_part, y_other, mark = group_sum(*parts)
    y_part = after(y_part, word_gather.arrived(near=(1,)))
    half_words = embedding.shape[0] * per_half

    valid = (jnp.arange(seq_len) < lengths[here]).astype(F32)
    half_weight = 0.5 * valid
    weight2 = jnp.concatenate([half_weight, half_weight])[None, :]
    block0, block1, final_t, final_n, block_out, flat_grad = final_norm(
        flags, h2, y_part, y_other, norms, jnp.broadcast_to(weight2, (8, 2 * seq_len)).astype(BF16)
    )
    shard_rows = embedding.shape[0]
    owner = targets // shard_rows
    in_quarter = (owner % 2 == core) & (owner // 2 % 2 == which)
    place = ((owner // 4) ^ here) * shard_rows + targets % shard_rows
    target = jnp.broadcast_to(jnp.where(in_quarter, place, -1)[None, :], (8, seq_len)).astype(jnp.int32)
    word_gather.forward((3,), final_t)
    stats = jnp.concatenate(
        [jnp.full((1, 2 * seq_len), -1e30, F32), jnp.zeros((7, 2 * seq_len), F32)], axis=0
    )
    sums = jnp.zeros((8, width), F32)
    for g in (0, 1, 2, 3):
        words = halves(word_gather.result(), 0)
        stats, sums = first_sweep(
            2 * g * half_words, words[2 * g : 2 * g + 2], final_t, target, stats, sums
        )
    hits = stats[3, :seq_len]

    stats = merge_stats(stats, swap(stats, "vocab", 1))
    stats = stats, swap(stats, "pass", 1)
    lse, drift = stats_result(merge_stats(*stats))
    weight8 = jnp.broadcast_to(weight2, (8, 2 * seq_len))
    accs = [sums, sums]
    word_sum = ScatterSum("dp")
    loss = (
        0.25 * jnp.sum(weight2 * (lse + drift))
        - (1.0 - SMOOTH) * jnp.sum(half_weight * hits)
        + jnp.sum(flat_grad[0] * sums[0])
    )
    loss = jnp.broadcast_to(loss, (8, 128))
    loss_mark = loss
    if rows_axis == 8:
        stack = jnp.stack([loss] + [swap(loss, "dp", 2 * g) for g in (1, 2, 3)])
        loss = sum(lax.dynamic_index_in_dim(stack, here // 2 ^ z, 0, False) for z in range(4))
        loss_mark = loss
        loss = loss + swap(loss, "dp", 1)
    step = 1
    while rows_axis != 8 and step < rows_axis:
        loss = loss + swap(loss, "dp", step)
        step *= 2
    loss_end = loss
    for axis in ("vocab", "pass"):
        loss = loss + swap(loss, axis, 1)
    mean_loss = loss[0, 0] / jnp.sum(lengths).astype(F32)
    for groups in ((3,), (1, 2, 0)):
        fars, nears, accs = second_sweep(
            flags,
            [2 * g * half_words for g in groups],
            [words[2 * g + n] for g in groups for n in range(2)],
            *(final_t, final_n, stats, weight8, target, flat_grad, accs, groups[-1] == 0),
        )
        if groups[-1]:
            word_sum.give(groups, fars, nears, mark=loss_mark)
    word_sum.give((2, 1), fars[1::-1], nears[1::-1])
    accs = after(accs, (word_sum.arrived(near=(3,)), loss_end))
    word_sum.second((3,))

    dh_part, dh_other, mark = group_sum(*accs)
    db, dy, dy_n, cols = final_back(flags, block0, block1, dh_part, dh_other, norms)
    expert_sum = ScatterSum("dp")
    last_words = fars, nears
    *expert_grads, parts = expert_backward(flags, expert_parts, a3, a3_n, dy, dy_n, route)
    mark = (word_sum.arrived(near=(2,)), word_sum.step)
    word_sum.second((1,), parts)
    for start in (1, 0):
        expert_sum.give((start, start + 2), expert_grads[0][start::2], expert_grads[1][start], 2, mark)
    da_part, da_other, mark = group_sum(*parts)
    word_sum.third(parts)

    dh1, cross_output_grad, cross_query_grad, pair_grad, cols = cross_back(
        flags,
        *(db, da_part, *da_other, h2, norms, cols, cross_output_t, cross_att_t, cross_t, memory_kv),
        *(cross_lse, mem_bias, a2, cross_query_t, h1),
    )
    (memory_project_grad,) = call(memory_weight_kernel, [((2 * width, width), BF16)], pair_grad, memory)
    self_output_grad, self_project_grad, inputs_grad, norm_grads = self_back(
        dh1, self_output_t, attended_t, qkv_t, self_lse, a1, inputs, project_t, norms, cols
    )
    expert_sum.second(None, (inputs_grad, word_sum.step, word_sum.last))
    expert_sum.third()
    evens = jnp.concatenate([jnp.arange(0, rows_axis, 2), jnp.arange(1, rows_axis, 2)])
    pack_order = 2 * ((evens if rows_axis == 8 else jnp.arange(rows_axis)) ^ here) + which
    blocks = pack(
        [self_project_grad, self_output_grad, cross_query_grad, memory_project_grad, cross_output_grad, norm_grads],
        pack_order,
        core,
        sizes,
        pack_half,
    )
    (memory_grad,) = call(
        memory_back_kernel, [(memory.shape, F32)], after(pair_grad, blocks), memory_project_t
    )
    layer_sum = ScatterSum("dp")
    if rows_axis == 8:
        layer_sum.give((0, 1, 2, 3), [blocks[g] for g in range(4)], blocks[4:])
        layer_sum.second(None, memory_grad)
        word_sum.give((0,), last_words[0][2:], last_words[1][2:], mark=layer_sum.arrived(near=(0,)))
        layer_sum.third()
    else:
        layer_sum.blocks = {k: blocks[k] for k in range(rows_axis)}
    if rows_axis != 8:
        word_sum.give((0,), last_words[0][2:], last_words[1][2:])
    embedding_grad = word_sum.result()
    expert_grad = expert_sum.result()
    expert_twin = swap(expert_grad, "vocab", 1)
    expert_grad = jnp.concatenate(
        [
            jnp.where(core == 0, expert_grad, expert_twin),
            jnp.where(core == 0, expert_twin, expert_grad),
        ],
        axis=1,
    ).transpose(0, 1, 3, 2)
    layer_grad = layer_sum.result((expert_sum.last, word_sum.arrived(near=(0,))))
    twin = swap(layer_grad, "vocab", 1)
    layer_grad = jnp.concatenate(
        [jnp.where(core == 0, layer_grad, twin), jnp.where(core == 0, twin, layer_grad)], axis=0
    ).T
    ends = [sum(sizes[: n + 1]) for n in range(len(sizes))]
    layer_grads = [layer_grad[:, end - size : end] for size, end in zip(sizes, ends)]
    norm_out = layer_grads[5][:8]
    return (
        block_out[None],
        mean_loss,
        inputs_grad,
        memory_grad,
        norm_out[:4],
        norm_out[4:],
        *layer_grads[:5],
        expert_grad[0],
        expert_grad[1],
        embedding_grad,
    )


def solution(mesh):
    shared = P(None, ("dp", "pass"))
    placed = (
        P("dp", None),
        P("dp", None),
        P("pass", "dp", None),
        P("dp"),
        P(),
        P("dp", None),
        shared,
        shared,
        shared,
        shared,
        shared,
        shared,
        shared,
        P(None, None, ("dp", "pass")),
        P(None, None, ("dp", "pass")),
        P(("dp", "pass", "vocab"), None),
    )
    return jax.shard_map(
        local,
        mesh=mesh,
        in_specs=placed,
        out_specs=(
            P("pass", "dp", None),
            P(),
            P("dp", None),
            P("dp", None),
            shared,
            shared,
            shared,
            shared,
            shared,
            shared,
            shared,
            P(None, None, ("dp", "pass")),
            P(None, None, ("dp", "pass")),
            P(("dp", "pass", "vocab"), None),
        ),
        check_vma=False,
    )
```
